128 devices in a mesh: section: 2 (over core), expert: 16 (over z, x), shard: 4 (over y).
Axes of the slice: x: 4, y: 4, z: 4, core: 2. Of those that a mesh axis runs over, the one named last changes fastest.
Arguments:
- ends_in: bfloat16 [2, 2, 4096, 1024], P('section', None, ('expert', 'shard')), may hold values from -6 to 6
- segments: int32 [2, 4096], P(None, 'expert'), may hold values from 0 to 4, as said below
- routes: int32 [2, 2, 4096, 8], P('section', None, ('expert', 'shard')), may hold values from 0 to 31, all different within a row; in each aligned block of 64 rows (0 to 63, 64 to 127, ..., all dimensions but the last counted through in order) at most 24 rows name the same one
- gates: float32 [2, 2, 4096, 8], P('section', None, ('expert', 'shard')), may hold values from 0.2 to 0.6
- attn_gain: float32 [2, 1024], P('section'), may hold values from 0.1 to 1.9
- query_gain: float32 [2, 64], P('section'), may hold values from 0.1 to 1.9
- key_gain: float32 [2, 64], P('section'), may hold values from 0.1 to 1.9
- feed_gain: float32 [2, 1024], P('section'), may hold values from 0.1 to 1.9
- w_query: bfloat16 [2, 1024, 1024], P('section', 'expert', 'shard'), may hold values from -0.1875 to 0.1875
- key_weight: bfloat16 [2, 1024, 512], P('section', 'expert', 'shard'), may hold values from -0.1875 to 0.1875
- value_weight: bfloat16 [2, 1024, 512], P('section', 'expert', 'shard'), may hold values from -0.1875 to 0.1875
- w_out: bfloat16 [2, 1024, 1024], P('section', 'shard', 'expert'), may hold values from -1 to 1
- w_gate: bfloat16 [2, 32, 1024, 512], P('section', 'expert'), may hold values from -0.1875 to 0.1875
- w_up: bfloat16 [2, 32, 1024, 512], P('section', 'expert'), may hold values from -0.1875 to 0.1875
- w_down: bfloat16 [2, 32, 512, 1024], P('section', 'expert'), may hold values from -0.5 to 0.5
Outputs:
- ends: bfloat16 [2, 2, 4096, 1024], P('section', None, ('expert', 'shard'))
- grad_attn_gain: float32 [2, 1024], P('section')
- grad_query_gain: float32 [2, 64], P('section')
- grad_key_gain: float32 [2, 64], P('section')
- grad_feed_gain: float32 [2, 1024], P('section')
- grad_w_query: float32 [2, 1024, 1024], P('section', 'expert', 'shard')
- grad_w_key: float32 [2, 1024, 512], P('section', 'expert', 'shard')
- grad_w_value: float32 [2, 1024, 512], P('section', 'expert', 'shard')
- grad_w_out: float32 [2, 1024, 1024], P('section', 'shard', 'expert')
- grad_w_gate: float32 [2, 32, 1024, 512], P('section', 'expert', None, 'shard')
- grad_w_up: float32 [2, 32, 1024, 512], P('section', 'expert', None, 'shard')
- grad_w_down: float32 [2, 32, 512, 1024], P('section', 'expert', 'shard')
The draws below stay inside these ranges and needn't reach their ends.
Inputs may be any that keep to these rules, and one draw needn't show every extreme that they name: `segments`: within each sequence of 256 consecutive tokens the numbers start at 0 and never fall; a new document begins only within the first or the last 64 tokens of a sequence. `routes`: each row names 8 different experts; in the rows of one device in one micro-batch (aligned blocks of 64 rows) no expert is named more than 24 times.
All inputs are finite; a program needn't handle non-finite values.
Results may differ from the reference program's by a relative error of at most 0.04.
Values may be sent and summed in bfloat16 or wider, within the bound.
A program may use at most 192 MiB of HBM per device.

```python
import math
import jax
import jax.numpy as jnp
import numpy as np
from jax import lax

MODEL_WIDTH = 1024
FF = 512
QUERY_HEADS = 16
KEY_VALUE_HEADS = 8
HEAD_SIZE = 64
TOP = 8
MICRO = 2
ROWS_DEV = 64
EXPERTS = 32
SEQUENCE_TOKENS = 256
TOKENS = 4096
CAP = 24
N_SECTION = 2


def draw_segments(key, part):
    key = jax.random.fold_in(key, 7)
    blocks = TOKENS // SEQUENCE_TOKENS
    spots = (jnp.arange(MICRO * TOKENS, dtype=jnp.int32) % SEQUENCE_TOKENS).reshape(MICRO, blocks, SEQUENCE_TOKENS)
    half = ROWS_DEV // 2
    keys = jax.random.split(key, 4)
    shape = (MICRO, blocks, 1)
    first_cut = jax.random.randint(keys[0], shape, 1, half + 1)
    second_cut = jax.random.randint(keys[1], shape, half + 1, ROWS_DEV)
    third_cut = jax.random.randint(keys[2], shape, SEQUENCE_TOKENS - ROWS_DEV + 1, SEQUENCE_TOKENS - half + 1)
    fourth_cut = jax.random.randint(keys[3], shape, SEQUENCE_TOKENS - half + 1, SEQUENCE_TOKENS)
    cuts = ((spots == first_cut) | (spots == second_cut) | (spots == third_cut) | (spots == fourth_cut)).astype(jnp.int32)
    return jnp.cumsum(cuts, axis=-1).reshape(MICRO, TOKENS).astype(jnp.int32)


def steps_of(rng, extent, pieces, smallest, high):
    level = 1.0
    for axis_at, parts in pieces:
        heights = jax.random.uniform(jax.random.fold_in(jax.random.fold_in(rng, 6), axis_at), (parts,), jnp.float32, smallest / len(pieces), high / len(pieces))
        level = level * jnp.repeat(jnp.exp(heights), extent[axis_at] // parts).reshape((-1,) + (1,) * (len(extent) - 1 - axis_at))
    return level


def assign_block(key, own, number, rows, amount, top, bound, skew):
    ranking = jax.random.permutation(key, amount)
    crowded, common = shares(amount, rows * top, bound, skew, True), shares(amount, rows * top, bound, skew, False)
    places = jnp.arange(amount)

    def named(sizes, turn):
        used = int((sizes > 0).sum())
        fixed = max(1, used // 4)
        passed = fixed + (places - fixed + turn * (used - fixed)) % max(1, amount - fixed)
        return jnp.zeros((amount,), jnp.int32).at[ranking[jnp.where(places < fixed, places, passed)]].set(jnp.asarray(sizes, jnp.int32))

    sizes = jnp.where(number % 4 == 0, named(crowded, number // 4), named(common, number - number // 4 - 1))
    mixed = jax.random.permutation(jax.random.fold_in(own, 3), amount)
    source_of, taker = mixed[0:amount // 2 * 2:2], mixed[1:amount // 2 * 2:2]
    slack = jnp.minimum(sizes[source_of] - 1, bound - sizes[taker]) // 2
    slack = jnp.where((source_of == ranking[0]) | (taker == ranking[0]) | (sizes[taker] == 0), 0, jnp.maximum(slack, 0))
    passed = jax.random.randint(jax.random.fold_in(own, 4), (amount // 2,), 0, 1 << 20) % (slack + 1)
    sizes = sizes.at[source_of].add(-passed).at[taker].add(passed)
    items = jnp.searchsorted(jnp.cumsum(sizes), jnp.arange(rows * top), side="right").astype(jnp.int32)
    table = items.reshape(top, rows).T
    table = table[jax.random.permutation(jax.random.fold_in(own, 1), rows)]
    turn = jax.random.randint(jax.random.fold_in(own, 2), (rows, 1), 0, top)
    return jnp.take_along_axis(table, (jnp.arange(top)[None, :] + turn) % top, axis=1)


def shares(amount, total, limit, skew, full):
    portions = [(1 << 20) // math.isqrt(grade ** skew) + 1 for grade in range(1, amount + 1)]
    largest = limit if full else min(limit, max(-(-total // amount), total * portions[0] // sum(portions)))
    least = 1 if total - largest >= amount - 1 else 0
    holding, spare = [largest] + [least] * (amount - 1), total - largest - least * (amount - 1)
    while spare > 0:
        candidates = [i for i in range(1, amount) if holding[i] < largest] or [i for i in range(1, amount) if holding[i] < limit]
        pool, left = sum([portions[i] for i in candidates]), spare
        for i in candidates:
            addition = min(limit - holding[i], max(1, left * portions[i] // pool), spare)
            holding[i] = holding[i] + addition
            spare = spare - addition
    return np.array(holding)


def scatter_about(own_key, shape, scale, reach, cuts=(), kind=jnp.bfloat16):
    array = jax.random.normal(own_key, shape, jnp.float32) * scale
    if len(cuts) > 0:
        array = steps_of(own_key, shape, cuts, -0.22, 0.18) * array
    return jnp.clip(array, min=-reach, max=reach).astype(kind)


def setup_inputs(seed: int = 0) -> dict:
    seeds = jax.random.split(jax.random.key(seed), 16)
    ends_in = scatter_about(seeds[0], (2, MICRO, TOKENS, MODEL_WIDTH), 1.0, 6.0, ((0, 2), (2, 64)))
    segments = draw_segments(jax.random.fold_in(seeds[15], 71), 0)
    routes_keys = jax.random.split(jax.random.fold_in(seeds[2], 1), 2 * MICRO * TOKENS // ROWS_DEV)
    routes_turns = jax.random.permutation(jax.random.fold_in(seeds[2], 3), 2 * MICRO * TOKENS // ROWS_DEV)
    routes = jax.vmap(lambda own, number: assign_block(jax.random.fold_in(seeds[2], 2), own, number, ROWS_DEV, EXPERTS, TOP, CAP, 1))(routes_keys, routes_turns).reshape((2, MICRO, TOKENS, TOP))
    gates = jnp.clip(0.2 + 0.400000021 * jax.random.uniform(seeds[3], (2, MICRO, TOKENS, TOP), jnp.float32) ** steps_of(seeds[3], (2, MICRO, TOKENS, TOP), ((0, 2), (2, 64)), -0.2, 0.2), 0.2, 0.6)
    attn_gain = jnp.clip(1.0 + 0.18 * jax.random.normal(seeds[4], (2, MODEL_WIDTH), jnp.float32), 0.1, 1.9)
    query_gain = jnp.clip(1.0 + 0.18 * jax.random.normal(seeds[5], (2, HEAD_SIZE), jnp.float32), 0.1, 1.9)
    key_gain = jnp.clip(1.0 + 0.18 * jax.random.normal(seeds[6], (2, HEAD_SIZE), jnp.float32), 0.1, 1.9)
    feed_gain = jnp.clip(1.0 + 0.18 * jax.random.normal(seeds[7], (2, MODEL_WIDTH), jnp.float32), 0.1, 1.9)
    w_query = scatter_about(seeds[8], (2, MODEL_WIDTH, QUERY_HEADS * HEAD_SIZE), MODEL_WIDTH ** -0.5, 0.1875, ((0, 2), (1, 16), (2, 4)))
    key_weight = scatter_about(seeds[9], (2, MODEL_WIDTH, KEY_VALUE_HEADS * HEAD_SIZE), MODEL_WIDTH ** -0.5, 0.1875, ((0, 2), (1, 16), (2, 4)))
    value_weight = scatter_about(seeds[10], (2, MODEL_WIDTH, KEY_VALUE_HEADS * HEAD_SIZE), MODEL_WIDTH ** -0.5, 0.1875, ((0, 2), (1, 16), (2, 4)))
    w_out = scatter_about(seeds[11], (2, QUERY_HEADS * HEAD_SIZE, MODEL_WIDTH), (QUERY_HEADS * HEAD_SIZE // 32) ** -0.5, 1.0, ((0, 2), (1, 4), (2, 16)))
    w_gate = scatter_about(seeds[12], (2, EXPERTS, MODEL_WIDTH, FF), MODEL_WIDTH ** -0.5, 0.1875, ((0, 2), (1, 16)))
    w_up = scatter_about(seeds[13], (2, EXPERTS, MODEL_WIDTH, FF), MODEL_WIDTH ** -0.5, 0.1875, ((0, 2), (1, 16)))
    w_down = scatter_about(seeds[14], (2, EXPERTS, FF, MODEL_WIDTH), (FF // 4) ** -0.5, 0.5, ((0, 2), (1, 16)))
    return {"ends_in": ends_in, "segments": segments, "routes": routes, "gates": gates, "attn_gain": attn_gain, "query_gain": query_gain, "key_gain": key_gain, "feed_gain": feed_gain, "w_query": w_query, "key_weight": key_weight, "value_weight": value_weight, "w_out": w_out, "w_gate": w_gate, "w_up": w_up, "w_down": w_down}


EPS = 1e-06
NEG = -1e+30
HIGH_PRECISION = lax.Precision.HIGHEST

@jax.custom_vjp
def lower_input(v):
    return lax.optimization_barrier(v.astype(jnp.bfloat16)).astype(jnp.float32)

@jax.custom_vjp
def lower_gradient(v):
    return v

def low_keep(v):
    return (lower_input(v), None)

def low_pass(kept, grad):
    return (grad,)

def back_keep(v):
    return (v, None)

def back_low(kept, grad):
    return (lower_input(grad),)
lower_input.defvjp(low_keep, low_pass)
lower_gradient.defvjp(back_keep, back_low)

def rms_norm(values, gain):
    return values * lax.rsqrt(lax.optimization_barrier(jnp.mean(values * values, axis=-1, keepdims=True)) + EPS) * gain

def attend_sequence(block):
    query_rows, key, value_rows, document_segments = block
    head_group = QUERY_HEADS // KEY_VALUE_HEADS
    query_rows = query_rows.reshape(SEQUENCE_TOKENS, KEY_VALUE_HEADS, head_group, HEAD_SIZE)
    scores = jnp.einsum('qhgd,khd->hgqk', query_rows, key, precision=HIGH_PRECISION) * HEAD_SIZE ** (-0.5)
    spots = jnp.arange(SEQUENCE_TOKENS, dtype=jnp.int32)
    allowed = (spots[:, None] >= spots[None, :]) & (document_segments[:, None] == document_segments[None, :])
    scores = lower_gradient(jnp.where(allowed, scores, NEG))
    probs = lower_input(jax.nn.softmax(scores, axis=-1))
    mixed_output = jnp.einsum('hgqk,khd->qhgd', probs, value_rows, precision=HIGH_PRECISION)
    return lower_input(lower_gradient(mixed_output.reshape(SEQUENCE_TOKENS, QUERY_HEADS * HEAD_SIZE)))

def experts_apply(feed, route_rows, gate_rows, w_gate, w_up, w_down):
    token_count = feed.shape[0]
    most = CAP * (token_count // ROWS_DEV)
    flat = route_rows.reshape(-1).astype(jnp.int32)
    copies = lower_gradient(jnp.repeat(feed, TOP, axis=0))

    def locate(expert):
        picked = flat == expert
        places = jnp.nonzero(picked, size=most, fill_value=0)[0].astype(jnp.int32)
        valid = jnp.arange(most, dtype=jnp.int32) < jnp.sum(picked.astype(jnp.int32))
        return (places, valid)
    places, valids = lax.map(locate, jnp.arange(EXPERTS, dtype=jnp.int32))

    def apply_one(block):
        expert, where_rows, valid = block
        rows_in = copies[where_rows] * valid.astype(copies.dtype)[:, None]
        gate_part = lower_gradient(jnp.dot(rows_in, w_gate[expert], precision=HIGH_PRECISION))
        up_part = lower_gradient(jnp.dot(rows_in, w_up[expert], precision=HIGH_PRECISION))
        hidden = lower_input(jax.nn.silu(gate_part) * up_part)
        return lower_input(lower_gradient(jnp.dot(hidden, w_down[expert], precision=HIGH_PRECISION)))
    results = lax.map(jax.checkpoint(apply_one), (jnp.arange(EXPERTS, dtype=jnp.int32), places, valids))
    summed = jnp.zeros_like(copies).at[places.reshape(-1)].add(results.reshape(-1, MODEL_WIDTH))
    return lax.optimization_barrier(jnp.sum(summed.reshape(token_count, TOP, MODEL_WIDTH) * gate_rows[:, :, None], axis=1))

def layer(stream, document_segments, route_rows, gate_rows, params):
    attn_gain, query_gain, key_gain, feed_gain, w_query, key_weight, value_weight, w_out, w_gate, w_up, w_down = params
    token_count = stream.shape[0]
    normed_input = lower_input(rms_norm(stream, attn_gain))
    query_rows = lower_gradient(jnp.dot(normed_input, w_query, precision=HIGH_PRECISION)).reshape(token_count, QUERY_HEADS, HEAD_SIZE)
    key = lower_gradient(jnp.dot(normed_input, key_weight, precision=HIGH_PRECISION)).reshape(token_count, KEY_VALUE_HEADS, HEAD_SIZE)
    value_rows = lower_input(lower_gradient(jnp.dot(normed_input, value_weight, precision=HIGH_PRECISION))).reshape(token_count, KEY_VALUE_HEADS, HEAD_SIZE)
    query_rows = lower_input(rms_norm(query_rows, query_gain))
    key = lower_input(rms_norm(key, key_gain))
    layer_blocks = token_count // SEQUENCE_TOKENS
    mixed_output = lax.map(jax.checkpoint(attend_sequence), (query_rows.reshape(layer_blocks, SEQUENCE_TOKENS, QUERY_HEADS, HEAD_SIZE), key.reshape(layer_blocks, SEQUENCE_TOKENS, KEY_VALUE_HEADS, HEAD_SIZE), value_rows.reshape(layer_blocks, SEQUENCE_TOKENS, KEY_VALUE_HEADS, HEAD_SIZE), document_segments.reshape(layer_blocks, SEQUENCE_TOKENS)))
    middle = stream + lower_gradient(jnp.dot(mixed_output.reshape(token_count, QUERY_HEADS * HEAD_SIZE), w_out, precision=HIGH_PRECISION))
    feed = lower_input(rms_norm(middle, feed_gain))
    return middle + experts_apply(feed, route_rows, gate_rows, w_gate, w_up, w_down)

def forward(inputs, params, segments, routes, gates):
    outputs = []
    for micro in range(MICRO):
        stream = inputs[micro]
        for section in range(N_SECTION):
            section_params = tuple((item[section] for item in params))
            stream = layer(stream, segments[micro], routes[section, micro], gates[section, micro], section_params)
            if section + 1 < N_SECTION:
                stream = lower_input(lower_gradient(stream))
        outputs.append(stream)
    return jnp.stack(outputs)

def reference(ends_in, segments, routes, gates, attn_gain, query_gain, key_gain, feed_gain, w_query, key_weight, value_weight, w_out, w_gate, w_up, w_down):
    params = tuple((item.astype(jnp.float32) for item in (attn_gain, query_gain, key_gain, feed_gain, w_query, key_weight, value_weight, w_out, w_gate, w_up, w_down)))
    inputs = ends_in[0].astype(jnp.float32)
    cotangent = ends_in[1].astype(jnp.float32)
    gate_values = gates.astype(jnp.float32)

    def run(inputs, params):
        return forward(inputs, params, segments, routes, gate_values)
    result, pull = jax.vjp(run, inputs, params)
    back_input, back_params = pull(cotangent)
    ends = jnp.stack([back_input, result]).astype(jnp.bfloat16)
    return (ends, back_params[0], back_params[1], back_params[2], back_params[3], back_params[4], back_params[5], back_params[6], back_params[7], back_params[8], back_params[9], back_params[10])
```

```python
import functools

import jax
import jax.numpy as jnp
from jax import lax
from jax.experimental import pallas as pl
from jax.experimental.pallas import tpu as pltpu
from jax.sharding import PartitionSpec as P

EPS = 1e-06
NEG = -1e30
HEAD = 64
RING = 4
MESH = pl.DeviceIdType.MESH
F32 = jnp.float32
BF16 = jnp.bfloat16

NN = (((1,), (0,)), ((), ()))
NT = (((1,), (1,)), ((), ()))
TN = (((0,), (0,)), ((), ()))

(
    Y_GATHER,
    Y_SUM,
    TOKENS,
    PACKED,
    RESULT,
    PARTIAL,
    Y_GATHER_BACK,
    Y_SUM_BACK,
    TOKENS_BACK,
    PACKED_BACK,
    RESULT_BACK,
    PARTIAL_BACK,
    GRAD_Y,
    GRAD_Q,
    GRAD_Q_LATER,
    GAIN_P,
    GAIN_Q,
    GAIN_Y,
    WEIGHT_P,
    TABLE_P,
) = range(20)
RING_ROWS = 22

(
    C_ENDS,
    C_GAINS,
    C_ROUTES,
    C_PIECE,
    C_HALF,
    C_GATE,
    C_UP,
    C_DOWN,
    C_GRAD,
    C_PROJ,
    C_TERM,
    C_OUT_EXPERT,
    C_OUT_PROJ,
    C_OUT_ENDS,
) = (0, 1, 2, 3, 4, 6, 7, 8, 9, 10, 11, 12, 14, 16)
CORE_ROWS = 17


def dot(a, b, form=NN):
    return lax.dot_general(a, b, form, preferred_element_type=F32)


def exact_dot(a, b):
    return lax.dot_general(
        a, b, NN, preferred_element_type=F32, precision=lax.Precision.HIGHEST
    )


def scale_of(rows):
    return lax.rsqrt(jnp.mean(rows * rows, axis=-1, keepdims=True) + EPS)


def kernel(
    rows,
    width,
    hidden,
    capacity,
    ends_ref,
    seg_row_ref,
    seg_col_ref,
    routes_ref,
    gains_ref,
    piece_ref,
    gate_ref,
    up_ref,
    down_ref,
    ends_out,
    gains_out,
    proj_out,
    expert_out,
    w_gate,
    w_up,
    w_down,
    w_attn,
    ends_in,
    gains,
    routes,
    table_send,
    table_recv,
    slots,
    weights,
    stream,
    middle,
    cotangent,
    attn_all,
    raw_qk,
    values,
    mixed,
    y_send,
    y_recv,
    tokens,
    packed_send,
    packed,
    packed_back,
    result_send,
    result,
    partial_send,
    partial,
    parts,
    attn_back,
    back_qk,
    back_v,
    acts,
    grads,
    grads_core,
    grads_y,
    out_stage,
    proj,
    proj_core,
    proj_recv,
    proj_sum,
    proj_last,
    proj_stage,
    terms,
    terms_core,
    terms_recv,
    ends_stage,
    send_sem,
    recv_sem,
    w_send,
    w_recv,
    j_send,
    j_recv,
    c_send,
    c_recv,
    local_sem,
    credit,
):
    core = lax.axis_index("section")
    place = lax.axis_index("expert")
    shard = lax.axis_index("shard")
    x = lax.rem(place, RING)
    z = lax.div(place, RING)
    p = x + core * (z - x)
    q = z + core * (x - z)
    span = RING * rows
    group = RING * capacity
    other = 1 - core

    def mod(value):
        return lax.rem(value + 2 * RING, RING)

    def place_of(second, first):
        return (1 - core) * (second * RING + first) + core * (first * RING + second)

    def y_device(d):
        return (core, place, mod(shard + d))

    def p_device(d):
        return (core, place_of(q, mod(p + d)), shard)

    def q_device(d):
        return (core, place_of(mod(q + d), p), shard)

    core_device = (other, place, shard)

    def ring_copy(row, d, src, dst, device):
        return pltpu.make_async_remote_copy(
            src_ref=src,
            dst_ref=dst,
            send_sem=send_sem.at[row, d - 1],
            recv_sem=recv_sem.at[row, d - 1],
            device_id=device,
            device_id_type=MESH,
        )

    def core_copy(row, src, dst):
        return pltpu.make_async_remote_copy(
            src_ref=src,
            dst_ref=dst,
            send_sem=c_send.at[row],
            recv_sem=c_recv.at[row],
            device_id=core_device,
            device_id_type=MESH,
        )

    barrier = pltpu.get_barrier_semaphore()
    for d in (1, 2, 3):
        for device in (y_device(d), p_device(d), q_device(d)):
            pl.semaphore_signal(barrier, inc=1, device_id=device, device_id_type=MESH)
    pl.semaphore_signal(barrier, inc=1, device_id=core_device, device_id_type=MESH)
    pl.semaphore_wait(barrier, 10)

    piece_copy = core_copy(C_PIECE, piece_ref.at[other], w_attn.at[core, other, place])
    ends_copy = core_copy(C_ENDS, ends_ref.at[other], ends_in)
    gains_copy = core_copy(C_GAINS, gains_ref, gains.at[core])
    routes_copy = core_copy(C_ROUTES, routes_ref.at[other], routes.at[core])
    for copy in (piece_copy, ends_copy, gains_copy, routes_copy):
        copy.start()
    w_attn[core, core, place] = piece_ref[core]
    gains[core] = gains_ref[...]
    routes[core] = routes_ref[core]

    def local_weights():
        return (
            pltpu.make_async_copy(gate_ref, w_gate.at[core], local_sem.at[0]),
            pltpu.make_async_copy(up_ref, w_up.at[core], local_sem.at[1]),
            pltpu.make_async_copy(down_ref, w_down.at[core], local_sem.at[2]),
        )

    def sent_weights():
        return (
            core_copy(C_GATE, gate_ref, w_gate.at[core]),
            core_copy(C_UP, up_ref, w_up.at[core]),
            core_copy(C_DOWN, down_ref, w_down.at[core]),
        )

    for copy in local_weights():
        copy.start()

    def weight_first(layer, d):
        return pltpu.make_async_remote_copy(
            src_ref=w_attn.at[layer, core, place],
            dst_ref=w_attn.at[layer, core, place],
            send_sem=send_sem.at[WEIGHT_P + 2 * layer, d - 1],
            recv_sem=recv_sem.at[WEIGHT_P + 2 * layer, d - 1],
            device_id=p_device(d),
            device_id_type=MESH,
        )

    def weight_second(layer, d, i):
        held = place_of(q, mod(p - i))
        return pltpu.make_async_remote_copy(
            src_ref=w_attn.at[layer, core, held],
            dst_ref=w_attn.at[layer, core, held],
            send_sem=w_send.at[layer, d - 1, i],
            recv_sem=w_recv.at[layer, d - 1, i],
            device_id=q_device(d),
            device_id_type=MESH,
        )

    def weight_half(layer):
        return core_copy(C_HALF + layer, w_attn.at[layer, core], w_attn.at[layer, core])

    def start_first(layer):
        for d in (1, 3, 2):
            weight_first(layer, d).start()

    def start_second(layer):
        for i in (0, 1, 3, 2):
            if i:
                weight_first(layer, i).wait_recv()
            for d in (1, 3, 2):
                weight_second(layer, d, i).start()

    def start_half(layer):
        for i in (0, 1, 3, 2):
            for d in (1, 3, 2):
                weight_second(layer, d, i).wait_recv()
        weight_half(layer).start()

    piece_copy.wait_recv()
    start_first(0)
    start_first(1)
    ends_copy.wait_recv()
    gains_copy.wait_recv()
    first = core == 0
    stream[0] = jnp.where(first, ends_ref[0], ends_in[...]).astype(F32)
    cotangent[...] = jnp.where(first, ends_in[...], ends_ref[1]).astype(F32)

    def make_tables():
        routes_copy.wait_recv()
        tiles = 32
        names = lax.broadcasted_iota(jnp.int32, (tiles, rows), 0).astype(F32)
        ahead = (
            lax.broadcasted_iota(jnp.int32, (rows, rows), 0)
            < lax.broadcasted_iota(jnp.int32, (rows, rows), 1)
        ).astype(BF16)
        spread = (
            lax.broadcasted_iota(jnp.int32, (rows, span), 1)
            == lax.broadcasted_iota(jnp.int32, (rows, span), 0) + rows * p
        ).astype(F32)
        row_at = lax.broadcasted_iota(jnp.int32, (2 * RING, tiles), 0)
        col_at = lax.broadcasted_iota(jnp.int32, (2 * RING, tiles), 1)
        for layer in range(2):
            block = routes[layer]
            named = jnp.zeros((tiles, rows), F32)
            gate = jnp.zeros((tiles, rows), F32)
            for j in range(8):
                hit = (block[j : j + 1, :] == names).astype(F32)
                named = named + hit
                gate = gate + hit * block[8 + j : 9 + j, :]
            rank = dot(named.astype(BF16), ahead)
            slot = named * (rank + (1 + capacity * p).astype(F32))
            wide_slot = exact_dot(slot, spread)
            wide_gate = exact_dot(gate, spread)
            for d in range(RING):
                first_axis = mod(p + d)
                owner = place_of(lax.div(row_at, 2), first_axis)
                choose = (col_at == 2 * owner + lax.rem(row_at, 2)).astype(F32)
                table_send[d, layer, 0] = exact_dot(choose, wide_slot)
                table_send[d, layer, 1] = exact_dot(choose, wide_gate)
        for d in (1, 3, 2):
            ring_copy(
                TABLE_P, d, table_send.at[d], table_recv.at[d - 1], p_device(d)
            ).start()

    def take_tables():
        for d in (1, 3, 2):
            ring_copy(
                TABLE_P, d, table_send.at[d], table_recv.at[d - 1], p_device(d)
            ).wait_recv()
        for layer in range(2):
            for kind, target in ((0, slots), (1, weights)):
                whole = table_send[0, layer, kind]
                for d in (1, 2, 3):
                    whole = whole + table_recv[d - 1, layer, kind]
                for r in range(2 * RING):
                    target[layer, r] = whole[r : r + 1, :]

    def choose_rows(layer, second, f):
        at = lax.broadcasted_iota(jnp.int32, (group, span), 0).astype(F32) + 1.0
        return at == slots[layer, 2 * second + f]

    lanes = lax.broadcasted_iota(jnp.int32, (1, 2 * HEAD), 1)
    low_half = lanes < HEAD
    halves = (low_half, lanes >= HEAD)

    def head_mean(block):
        at_row = lax.broadcasted_iota(jnp.int32, (2 * HEAD, 2 * HEAD), 0) >= HEAD
        at_col = lax.broadcasted_iota(jnp.int32, (2 * HEAD, 2 * HEAD), 1) >= HEAD
        share = jnp.where(at_row == at_col, 1.0 / HEAD, 0.0).astype(F32)
        tiles = [
            exact_dot(block[:, i : i + 2 * HEAD], share)
            for i in range(0, block.shape[1], 2 * HEAD)
        ]
        return jnp.concatenate(tiles, axis=1)

    def qk_gain(layer):
        return jnp.concatenate(
            [gains[layer, 2:3, : 4 * HEAD], gains[layer, 3:4, : 2 * HEAD]], axis=1
        )

    def allowed():
        causal = lax.broadcasted_iota(jnp.int32, (span, span), 0) >= lax.broadcasted_iota(
            jnp.int32, (span, span), 1
        )
        return causal & (seg_col_ref[...] == seg_row_ref[...])

    def normed_qk(layer):
        raw = raw_qk[layer]
        scale = lax.rsqrt(head_mean(raw * raw) + EPS)
        normed = raw * scale
        low = (normed * qk_gain(layer)).astype(BF16)
        return low, normed, scale

    def probs_of(low, tile, half, mask):
        query = low[:, tile * 2 * HEAD : (tile + 1) * 2 * HEAD]
        key = low[:, 4 * HEAD :]
        query = jnp.where(halves[half], query, jnp.zeros_like(query))
        scores = dot(query, key, NT) * HEAD ** (-0.5)
        scores = jnp.where(mask, scores, NEG)
        expo = jnp.exp(scores - jnp.max(scores, axis=-1, keepdims=True))
        return expo / jnp.sum(expo, axis=-1, keepdims=True), query, key

    def weight_of(layer, half):
        return w_attn[layer, half].reshape(width, 6 * HEAD)

    def y_gather(row, buffer, layer):
        copies = [
            ring_copy(row, d, buffer.at[layer, shard], buffer.at[layer, shard], y_device(d))
            for d in (1, 3, 2)
        ]
        for copy in copies:
            copy.start()
        return copies

    def y_scatter(row):
        copies = [
            ring_copy(row, d, y_send.at[mod(shard + d)], y_recv.at[d - 1], y_device(d))
            for d in (1, 3, 2)
        ]
        for copy in copies:
            copy.start()
        return copies

    def y_total(copies):
        for copy in copies:
            copy.wait()
        total = y_send[shard].astype(F32)
        for d in (1, 2, 3):
            total = total + y_recv[d - 1].astype(F32)
        return total

    def spread_tokens(row, block):
        tokens[p] = block
        copies = [
            ring_copy(row, d, tokens.at[p], tokens.at[p], p_device(d)) for d in (1, 3, 2)
        ]
        for copy in copies:
            copy.start()
        return copies

    def order(k):
        return k + lax.div(k, 2) * (5 - 2 * k)

    def packed_copy(row, layer, d, target):
        return ring_copy(
            row, d, packed_send.at[d - 1], target.at[layer, q], q_device(d)
        )

    def pack(row, layer, target, gated):
        def step(k, _):
            d = order(lax.rem(k + 1, RING))
            second = mod(q + d)
            whole = tokens[...].reshape(span, width)
            for f in range(2):
                chosen = choose_rows(layer, second, f)
                block = dot(chosen.astype(BF16), whole)
                if gated:
                    share = jnp.sum(
                        jnp.where(chosen, weights[layer, 2 * second + f], 0.0),
                        axis=1,
                        keepdims=True,
                    )
                    block = block * share
                block = block.astype(BF16)

                @pl.when(d == 0)
                def _():
                    target[layer, q, f] = block

                @pl.when(d != 0)
                def _():
                    packed_send[d - 1, f] = block

            @pl.when(d != 0)
            def _():
                packed_copy(row, layer, d, target).start()

            return 0

        lax.fori_loop(0, RING, step, 0)

    def result_copy(row, d):
        return ring_copy(row, d, result_send.at[d - 1], result.at[q], q_device(-d))

    def put_result(d, f, block):
        @pl.when(d == 0)
        def _():
            result[q, f] = block

        @pl.when(d != 0)
        def _():
            result_send[d - 1, f] = block

    def combine(row, layer, gated):
        def step(k, _):
            d = order(k)
            second = mod(q + d)

            @pl.when(d != 0)
            def _():
                result_copy(row, d).wait_recv()

            total = jnp.zeros((span, width), F32)
            for f in range(2):
                chosen = choose_rows(layer, second, f)
                if gated:
                    share = jnp.where(chosen, weights[layer, 2 * second + f], 0.0)
                else:
                    share = chosen.astype(F32)
                total = total + dot(share.astype(BF16), result[second, f], TN)

            @pl.when(k == 0)
            def _():
                parts[...] = total

            @pl.when(k != 0)
            def _():
                parts[...] += total

            return 0

        lax.fori_loop(0, RING, step, 0)
        for i in range(RING):
            partial_send[i] = parts[i * rows : (i + 1) * rows].astype(BF16)

    def partial_copies(row):
        return [
            ring_copy(
                row, d, partial_send.at[mod(p + d)], partial.at[d - 1], p_device(d)
            )
            for d in (1, 3, 2)
        ]

    def total_of_partials(row):
        copies = partial_copies(row)
        for copy in copies:
            copy.start()
        for copy in copies:
            copy.wait()
        total = partial_send[p].astype(F32)
        for d in (1, 2, 3):
            total = total + partial[d - 1].astype(F32)
        return total

    def wait_expert_weights(layer):
        @pl.when(layer == core)
        def _():
            for copy in local_weights():
                copy.wait()

        @pl.when(layer != core)
        def _():
            for copy in sent_weights():
                copy.wait_recv()

    def forward(layer, _):
        held = stream[layer]
        attn_all[layer, shard] = (held * scale_of(held) * gains[layer, 0:1, :]).astype(BF16)
        copies = y_gather(Y_GATHER, attn_all, layer)

        @pl.when(layer == 0)
        def _():
            start_second(0)
            make_tables()
            start_half(0)
            for copy in sent_weights():
                copy.start()

        weight_half(layer).wait_recv()
        for copy in copies:
            copy.wait()
        whole = attn_all[layer].reshape(span, width)
        raw_qk[layer] = dot(whole, weight_of(layer, 0))
        second_half = weight_of(layer, 1)
        values[layer] = dot(whole, second_half[:, : 2 * HEAD]).astype(BF16)
        low, _n, _s = normed_qk(layer)
        mask = allowed()
        value = values[layer]
        for tile in range(2):
            halves_out = []
            for half in range(2):
                probs, _q, _k = probs_of(low, tile, half, mask)
                halves_out.append(dot(probs.astype(BF16), value))
            mixed[layer, :, tile * 2 * HEAD : (tile + 1) * 2 * HEAD] = jnp.where(
                low_half, halves_out[0], halves_out[1]
            ).astype(BF16)
        out = dot(mixed[layer], second_half[:, 2 * HEAD :], NT)
        for i in range(RING):
            y_send[i] = out[i * rows : (i + 1) * rows].astype(BF16)
        copies = y_scatter(Y_SUM)

        @pl.when(layer == 0)
        def _():
            start_second(1)
            take_tables()

        center = held + y_total(copies)
        middle[layer] = center
        feed = (center * scale_of(center) * gains[layer, 1:2, :]).astype(BF16)
        copies = spread_tokens(TOKENS, feed)

        @pl.when(layer == 0)
        def _():
            start_half(1)

        wait_expert_weights(layer)
        for copy in copies:
            copy.wait()
        pack(PACKED, layer, packed, False)

        def experts(k, _):
            d = order(k)
            source = mod(q - d)

            @pl.when(d != 0)
            def _():
                packed_copy(PACKED, layer, d, packed).wait_recv()

            def one(f, _):
                block = packed[layer, source, f]
                gate_part = dot(block, w_gate[layer, f])
                up_part = dot(block, w_up[layer, f])
                inner = (gate_part * jax.nn.sigmoid(gate_part) * up_part).astype(BF16)
                put_result(d, f, dot(inner, w_down[layer, f]).astype(BF16))
                return 0

            lax.fori_loop(0, 2, one, 0)

            @pl.when(d != 0)
            def _():
                result_copy(RESULT, d).start()

            return 0

        lax.fori_loop(0, RING, experts, 0)
        combine(RESULT, layer, True)
        final = center + total_of_partials(PARTIAL)
        low_final = final.astype(BF16)

        @pl.when(layer == 0)
        def _():
            stream[1] = low_final.astype(F32)

        @pl.when(layer == 1)
        def _():
            ends_stage[0] = low_final

        for d in (1, 2, 3):
            packed_copy(PACKED, layer, d, packed).wait_send()
            result_copy(RESULT, d).wait_send()
        return 0

    lax.fori_loop(0, 2, forward, 0)

    def grad_core():
        return core_copy(C_GRAD, grads.at[other], grads_core)

    def grad_y(d):
        return ring_copy(
            GRAD_Y, d, grads.at[core, :, mod(shard + d)], grads_y.at[d - 1], y_device(d)
        )

    def sum_cores():
        grad_core().wait()

        def step(i, _):
            kind, part = lax.div(i, RING), lax.rem(i, RING)
            grads[core, kind, part] = (
                grads[core, kind, part].astype(F32) + grads_core[kind, part].astype(F32)
            ).astype(BF16)
            return 0

        lax.fori_loop(0, 3 * RING, step, 0)
        for d in (1, 3, 2):
            grad_y(d).start()

    def out_expert(layer):
        return core_copy(C_OUT_EXPERT + layer, out_stage, expert_out.at[:, core])

    def finish_expert(layer):
        for d in (1, 3, 2):
            grad_y(d).wait()
        for kind in range(3):
            total = grads[core, kind, shard].astype(F32)
            for d in (1, 2, 3):
                total = total + grads_y[d - 1, kind].astype(F32)

            @pl.when(layer == core)
            def _():
                expert_out[kind, core] = total

            @pl.when(layer != core)
            def _():
                out_stage[kind] = total

        @pl.when(layer != core)
        def _():
            out_expert(layer).start()

    def proj_core_copy(layer):
        return core_copy(C_PROJ, proj.at[other], proj_core)

    def proj_first(d, i):
        return pltpu.make_async_remote_copy(
            src_ref=proj.at[core, place_of(i, mod(p + d))],
            dst_ref=proj_recv.at[d - 1, i],
            send_sem=j_send.at[d - 1, i],
            recv_sem=j_recv.at[d - 1, i],
            device_id=p_device(d),
            device_id_type=MESH,
        )

    def proj_second(layer, d):
        return ring_copy(
            GRAD_Q + layer,
            d,
            proj_sum.at[mod(q + d)],
            proj_last.at[layer, d - 1],
            q_device(d),
        )

    def out_proj(layer):
        return core_copy(C_OUT_PROJ + layer, proj_stage, proj_out.at[core])

    def proj_one():
        proj_core_copy(0).wait()

        def step(i, _):
            proj[core, i] = (proj[core, i].astype(F32) + proj_core[i].astype(F32)).astype(BF16)
            return 0

        lax.fori_loop(0, RING * RING, step, 0)
        for i in range(RING):
            for d in (1, 3, 2):
                proj_first(d, i).start()

    def proj_two(layer):
        for i in range(RING):
            for d in (1, 3, 2):
                proj_first(d, i).wait()
            total = proj[core, place_of(i, p)].astype(F32)
            for d in (1, 2, 3):
                total = total + proj_recv[d - 1, i].astype(F32)
            proj_sum[i] = total.astype(BF16)
        for d in (1, 3, 2):
            proj_second(layer, d).start()

    def proj_three(layer):
        total = proj_sum[q].astype(F32)
        for d in (1, 3, 2):
            proj_second(layer, d).wait()
        for d in (1, 2, 3):
            total = total + proj_last[layer, d - 1].astype(F32)

        @pl.when(layer == core)
        def _():
            proj_out[core] = total

        @pl.when(layer != core)
        def _():
            proj_stage[...] = total
            out_proj(layer).start()

    def backward(turn, _):
        layer = 1 - turn
        incoming = cotangent[...]
        copies = spread_tokens(TOKENS_BACK, incoming.astype(BF16))

        for copy in copies:
            copy.wait()
        pack(PACKED_BACK, layer, packed_back, True)

        @pl.when(turn == 1)
        def _():
            proj_two(1)

        def experts(k, _):
            d = order(k)
            source = mod(q - d)

            @pl.when(d != 0)
            def _():
                packed_copy(PACKED_BACK, layer, d, packed_back).wait_recv()

            def one(f, _):
                block = packed[layer, source, f]
                gate_part = dot(block, w_gate[layer, f])
                up_part = dot(block, w_up[layer, f])
                back = packed_back[layer, source, f]
                back_hidden = dot(back, w_down[layer, f], NT)
                sigmoid = jax.nn.sigmoid(gate_part)
                silu = gate_part * sigmoid
                back_gate = (
                    back_hidden * up_part * sigmoid * (1.0 + gate_part * (1.0 - sigmoid))
                ).astype(BF16)
                back_up = (back_hidden * silu).astype(BF16)
                acts[0, f, source] = back_gate
                acts[1, f, source] = back_up
                acts[2, f, source] = (silu * up_part).astype(BF16)
                block = dot(back_gate, w_gate[layer, f], NT) + dot(back_up, w_up[layer, f], NT)
                put_result(d, f, block.astype(BF16))
                return 0

            lax.fori_loop(0, 2, one, 0)

            @pl.when(d != 0)
            def _():
                result_copy(RESULT_BACK, d).start()

            return 0

        lax.fori_loop(0, RING, experts, 0)

        @pl.when(turn == 1)
        def _():
            finish_expert(1)
            proj_three(1)
            pl.semaphore_wait(credit, 1)

        def expert_grads(i, _):
            f, j = lax.div(i, 2), lax.rem(i, 2)
            cut = pl.ds(pl.multiple_of(j * 256, 256), 256)
            feed = packed[layer, :, f].reshape(RING * group, width)
            back = packed_back[layer, :, f].reshape(RING * group, width)
            for kind in range(3):
                act = acts[kind, f, :, :, cut].reshape(RING * group, 256)
                change = dot(act, back if kind == 2 else feed, TN).astype(BF16)
                grads[f, kind, 2 * j] = change[:128]
                grads[f, kind, 2 * j + 1] = change[128:]
            return 0

        lax.fori_loop(0, 4, expert_grads, 0)
        grad_core().start()

        combine(RESULT_BACK, layer, False)
        change = total_of_partials(PARTIAL_BACK)
        center = middle[layer]
        scale = scale_of(center)
        normed = center * scale
        terms[layer, 1:2] = jnp.sum(change * normed, axis=0, keepdims=True)
        scaled = change * gains[layer, 1:2, :]
        inner = jnp.mean(scaled * normed, axis=-1, keepdims=True)
        back_mid = incoming + scale * (scaled - normed * inner)
        attn_back[layer, shard] = back_mid.astype(BF16)
        copies = y_gather(Y_GATHER_BACK, attn_back, layer)
        for d in (1, 2, 3):
            packed_copy(PACKED_BACK, layer, d, packed_back).wait_send()
            result_copy(RESULT_BACK, d).wait_send()
        low, normed, scale = normed_qk(layer)
        for copy in copies:
            copy.wait()

        whole_back = attn_back[layer].reshape(span, width)
        second_half = weight_of(layer, 1)
        back_mixed = dot(whole_back, second_half[:, 2 * HEAD :]).astype(BF16)
        value = values[layer]
        mask = allowed()
        back_key = jnp.zeros((span, 2 * HEAD), F32)
        back_value = jnp.zeros((span, 2 * HEAD), F32)
        tiles = []
        for tile in range(2):
            pieces = []
            for half in range(2):
                probs, query, key = probs_of(low, tile, half, mask)
                piece = back_mixed[:, tile * 2 * HEAD : (tile + 1) * 2 * HEAD]
                piece = jnp.where(halves[half], piece, jnp.zeros_like(piece))
                back_probs = dot(piece, value, NT)
                back_value = back_value + dot(probs.astype(BF16), piece, TN)
                total = jnp.sum(probs * back_probs, axis=-1, keepdims=True)
                back_scores = (probs * (back_probs - total)).astype(BF16)
                pieces.append(dot(back_scores, key))
                back_key = back_key + dot(back_scores, query, TN)
            tiles.append(jnp.where(low_half, pieces[0], pieces[1]))
        change = jnp.concatenate(tiles + [back_key], axis=1) * HEAD ** (-0.5)
        term = jnp.sum(change * normed, axis=0, keepdims=True)
        terms[layer, 2:3, : 6 * HEAD] = term
        scaled = change * qk_gain(layer)
        inner = head_mean(scaled * normed)
        back_qk[...] = (scale * (scaled - normed * inner)).astype(BF16)
        back_v[...] = back_value.astype(BF16)
        out = dot(back_qk[...], weight_of(layer, 0), NT) + dot(
            back_v[...], second_half[:, : 2 * HEAD], NT
        )
        for i in range(RING):
            y_send[i] = out[i * rows : (i + 1) * rows].astype(BF16)
        copies = y_scatter(Y_SUM_BACK)

        @pl.when(turn == 1)
        def _():
            for copy in (out_proj(1),):
                @pl.when(core != 1)
                def _():
                    copy.wait_send()

        whole = attn_all[layer].reshape(span, width)
        proj[0] = dot(whole, back_qk[...], TN).astype(BF16).reshape(16, rows, 6 * HEAD)
        low_half_proj = dot(whole, back_v[...], TN).astype(BF16)
        proj[1, :, :, : 2 * HEAD] = low_half_proj.reshape(16, rows, 2 * HEAD)
        high = dot(whole_back, mixed[layer], TN).astype(BF16)
        proj[1, :, :, 2 * HEAD :] = high.reshape(16, rows, 4 * HEAD)
        total = y_total(copies)
        held = stream[layer]
        scale = scale_of(held)
        normed = held * scale
        terms[layer, 0:1] = jnp.sum(total * normed, axis=0, keepdims=True)
        scaled = total * gains[layer, 0:1, :]
        inner = jnp.mean(scaled * normed, axis=-1, keepdims=True)
        back_in = (back_mid + scale * (scaled - normed * inner)).astype(BF16)

        @pl.when(turn == 0)
        def _():
            cotangent[...] = back_in.astype(F32)

        @pl.when(turn == 1)
        def _():
            ends_stage[1] = back_in

        sum_cores()

        @pl.when(turn == 0)
        def _():
            pl.semaphore_signal(credit, inc=1, device_id=core_device, device_id_type=MESH)

        proj_core_copy(layer).start()
        proj_one()
        return 0

    terms[...] = jnp.zeros_like(terms)
    lax.fori_loop(0, 2, backward, 0)

    ends_out[core] = jnp.where(first, ends_stage[1], ends_stage[0])
    ends_copy_out = core_copy(C_OUT_ENDS, ends_stage.at[core], ends_out.at[core])
    ends_copy_out.start()
    term_copy = core_copy(C_TERM, terms.at[other], terms_core)
    term_copy.start()
    term_copy.wait()
    terms_recv[0, 0] = terms[core] + terms_core[...]
    for axis, (row, device) in enumerate(
        ((GAIN_P, p_device), (GAIN_Q, q_device), (GAIN_Y, y_device))
    ):
        copies = [
            ring_copy(
                row, d, terms_recv.at[axis, 0], terms_recv.at[axis, d], device(d)
            )
            for d in (1, 3, 2)
        ]
        for copy in copies:
            copy.start()
        if axis == 0:
            proj_two(0)
        if axis == 1:
            proj_three(0)
        for copy in copies:
            copy.wait()
        total = terms_recv[axis, 0]
        for d in (1, 2, 3):
            total = total + terms_recv[axis, d]
        if axis < 2:
            terms_recv[axis + 1, 0] = total
        else:
            gains_out[...] = total

    finish_expert(0)
    for layer in range(2):
        @pl.when(layer == core)
        def _():
            out_expert(layer).wait_recv()
            out_proj(layer).wait_recv()

        @pl.when(layer != core)
        def _():
            out_expert(layer).wait_send()

            if layer == 0:
                out_proj(layer).wait_send()

    ends_copy_out.wait()
    for copy in (piece_copy, ends_copy, gains_copy, routes_copy):
        copy.wait_send()
    for copy in sent_weights():
        copy.wait_send()
    for layer in range(2):
        weight_half(layer).wait_send()
        for d in (1, 2, 3):
            weight_first(layer, d).wait_send()
            for i in range(RING):
                weight_second(layer, d, i).wait_send()
    for d in (1, 2, 3):
        ring_copy(
            TABLE_P, d, table_send.at[d], table_recv.at[d - 1], p_device(d)
        ).wait_send()


HEAD_ORDER = (0, 2, 1, 3)


def reorder_heads(block):
    parts = [block[:, HEAD * i : HEAD * (i + 1)] for i in HEAD_ORDER]
    return jnp.concatenate(parts, axis=1)


def shards(
    ends_in,
    segments,
    routes,
    gates,
    attn_gain,
    query_gain,
    key_gain,
    feed_gain,
    w_query,
    key_weight,
    value_weight,
    w_out,
    w_gate,
    w_up,
    w_down,
):
    core = lax.axis_index("section")
    rows = ends_in.shape[2]
    width = ends_in.shape[3]
    top = routes.shape[3]
    hidden = w_gate.shape[3]
    experts_all = w_gate.shape[1] * lax.axis_size("expert")
    capacity = 3 * rows * top // (2 * experts_all)
    group = RING * capacity
    span = RING * rows
    segment = jnp.where(core == 0, segments[0], segments[1])
    table = jnp.concatenate([routes[0].astype(F32), gates[0]], axis=-1).transpose(0, 2, 1)
    gains = jnp.concatenate(
        [
            attn_gain,
            feed_gain,
            jnp.tile(query_gain, (1, width // HEAD)),
            jnp.tile(key_gain, (1, width // HEAD)),
            jnp.zeros((4, width), F32),
        ],
        axis=0,
    )
    piece = jnp.stack(
        [
            jnp.concatenate([reorder_heads(w_query[0]), key_weight[0]], axis=1),
            jnp.concatenate([value_weight[0], reorder_heads(w_out[0].T)], axis=1),
        ]
    )
    vmem = pl.BlockSpec(memory_space=pltpu.VMEM)
    anywhere = pl.BlockSpec(memory_space=pl.ANY)
    half = 6 * HEAD
    everyone = RING * RING
    scratch = [
        pltpu.VMEM((2, 2, width, hidden), BF16),
        pltpu.VMEM((2, 2, width, hidden), BF16),
        pltpu.VMEM((2, 2, hidden, width), BF16),
        pltpu.VMEM((2, 2, everyone, rows, half), BF16),
        pltpu.VMEM((rows, width), BF16),
        pltpu.VMEM((2, 8, width), F32),
        pltpu.VMEM((2, 16, rows), F32),
        pltpu.VMEM((RING, 2, 2, 8, span), F32),
        pltpu.VMEM((RING - 1, 2, 2, 8, span), F32),
        pltpu.VMEM((2, 8, 1, span), F32),
        pltpu.VMEM((2, 8, 1, span), F32),
        pltpu.VMEM((2, rows, width), F32),
        pltpu.VMEM((2, rows, width), F32),
        pltpu.VMEM((rows, width), F32),
        pltpu.VMEM((2, RING, rows, width), BF16),
        pltpu.VMEM((2, span, half), F32),
        pltpu.VMEM((2, span, 2 * HEAD), BF16),
        pltpu.VMEM((2, span, 4 * HEAD), BF16),
        pltpu.VMEM((RING, rows, width), BF16),
        pltpu.VMEM((RING - 1, rows, width), BF16),
        pltpu.VMEM((RING, rows, width), BF16),
        pltpu.VMEM((RING - 1, 2, group, width), BF16),
        pltpu.VMEM((2, RING, 2, group, width), BF16),
        pltpu.VMEM((2, RING, 2, group, width), BF16),
        pltpu.VMEM((RING - 1, 2, group, width), BF16),
        pltpu.VMEM((RING, 2, group, width), BF16),
        pltpu.VMEM((RING, rows, width), BF16),
        pltpu.VMEM((RING - 1, rows, width), BF16),
        pltpu.VMEM((span, width), F32),
        pltpu.VMEM((2, RING, rows, width), BF16),
        pltpu.VMEM((span, half), BF16),
        pltpu.VMEM((span, 2 * HEAD), BF16),
        pltpu.VMEM((3, 2, RING, group, hidden), BF16),
        pltpu.VMEM((2, 3, RING, hidden // RING, width), BF16),
        pltpu.VMEM((3, RING, hidden // RING, width), BF16),
        pltpu.VMEM((RING - 1, 3, hidden // RING, width), BF16),
        pltpu.VMEM((3, hidden // RING, width), F32),
        pltpu.VMEM((2, everyone, rows, half), BF16),
        pltpu.VMEM((everyone, rows, half), BF16),
        pltpu.VMEM((RING - 1, RING, rows, half), BF16),
        pltpu.VMEM((RING, rows, half), BF16),
        pltpu.VMEM((2, RING - 1, rows, half), BF16),
        pltpu.VMEM((rows, half), F32),
        pltpu.VMEM((2, 8, width), F32),
        pltpu.VMEM((8, width), F32),
        pltpu.VMEM((3, RING, 8, width), F32),
        pltpu.VMEM((2, rows, width), BF16),
        pltpu.SemaphoreType.DMA((RING_ROWS, RING - 1)),
        pltpu.SemaphoreType.DMA((RING_ROWS, RING - 1)),
        pltpu.SemaphoreType.DMA((2, RING - 1, RING)),
        pltpu.SemaphoreType.DMA((2, RING - 1, RING)),
        pltpu.SemaphoreType.DMA((RING - 1, RING)),
        pltpu.SemaphoreType.DMA((RING - 1, RING)),
        pltpu.SemaphoreType.DMA((CORE_ROWS,)),
        pltpu.SemaphoreType.DMA((CORE_ROWS,)),
        pltpu.SemaphoreType.DMA((3,)),
        pltpu.SemaphoreType.REGULAR,
    ]
    ends, gain_sums, proj, experts = pl.pallas_call(
        functools.partial(kernel, rows, width, hidden, capacity),
        out_shape=(
            jax.ShapeDtypeStruct((2, rows, width), BF16),
            jax.ShapeDtypeStruct((8, width), F32),
            jax.ShapeDtypeStruct((2, rows, half), F32),
            jax.ShapeDtypeStruct((3, 2, hidden // RING, width), F32),
        ),
        in_specs=[vmem] * 6 + [anywhere] * 3,
        out_specs=(vmem,) * 4,
        scratch_shapes=scratch,
        compiler_params=pltpu.CompilerParams(
            collective_id=0, has_side_effects=True, vmem_limit_bytes=62 << 20
        ),
        cost_estimate=pl.CostEstimate(
            flops=60_000_000_000, bytes_accessed=20_000_000, transcendentals=4_000_000
        ),
        name="layers",
    )(
        ends_in[0],
        segment[None, :],
        segment[:, None],
        table,
        gains,
        piece,
        w_gate[0],
        w_up[0],
        w_down[0],
    )
    query_term = gain_sums[2, : 4 * HEAD].reshape(4, HEAD).sum(axis=0)
    key_term = gain_sums[2, 4 * HEAD : 6 * HEAD].reshape(2, HEAD).sum(axis=0)
    return (
        ends[None],
        gain_sums[0:1],
        query_term[None],
        key_term[None],
        gain_sums[1:2],
        reorder_heads(proj[0, :, : 4 * HEAD])[None],
        proj[0, :, 4 * HEAD :][None],
        proj[1, :, : 2 * HEAD][None],
        reorder_heads(proj[1, :, 2 * HEAD :]).T[None],
        experts[0].transpose(0, 2, 1)[None],
        experts[1].transpose(0, 2, 1)[None],
        experts[2][None],
    )


def solution(mesh):
    return jax.shard_map(
        shards,
        mesh=mesh,
        in_specs=(
            P("section", None, ("expert", "shard"), None),
            P(None, "expert"),
            P("section", None, ("expert", "shard"), None),
            P("section", None, ("expert", "shard"), None),
            P("section", None),
            P("section", None),
            P("section", None),
            P("section", None),
            P("section", "expert", "shard"),
            P("section", "expert", "shard"),
            P("section", "expert", "shard"),
            P("section", "shard", "expert"),
            P("section", "expert", None, None),
            P("section", "expert", None, None),
            P("section", "expert", None, None),
        ),
        out_specs=(
            P("section", None, ("expert", "shard"), None),
            P("section", None),
            P("section", None),
            P("section", None),
            P("section", None),
            P("section", "expert", "shard"),
            P("section", "expert", "shard"),
            P("section", "expert", "shard"),
            P("section", "shard", "expert"),
            P("section", "expert", None, "shard"),
            P("section", "expert", None, "shard"),
            P("section", "expert", "shard", None),
        ),
        check_vma=False,
    )
```

```python
import functools

import jax
import jax.numpy as jnp
from jax import lax
from jax.experimental import pallas as pl
from jax.experimental.pallas import tpu as pltpu
from jax.sharding import PartitionSpec as P

EPS = 1e-06
NEG = -1e30
HEAD = 64
RING = 4
MESH = pl.DeviceIdType.MESH
F32 = jnp.float32
BF16 = jnp.bfloat16

NN = (((1,), (0,)), ((), ()))
NT = (((1,), (1,)), ((), ()))
TN = (((0,), (0,)), ((), ()))

(
    Y_GATHER,
    Y_SUM,
    Y_GATHER_BACK,
    Y_SUM_BACK,
    TOKENS,
    TOKENS_BACK,
    PACKED,
    _packed_next,
    PACKED_BACK,
    _packed_back_next,
    RESULT,
    _result_next,
    RESULT_BACK,
    _result_back_next,
    PARTIAL,
    PARTIAL_BACK,
    GRAD_Q,
    _grad_q_next,
    GAIN_P,
    GAIN_Q,
    GAIN_Y,
    WEIGHT_P,
    _weight_p_next,
    TABLE_P,
    RING_ROWS,
) = range(25)

(
    C_ENDS,
    C_GAINS,
    C_ROUTES,
    C_GATES,
    C_PIECE,
    C_HALF,
    _half_next,
    C_GATE,
    C_UP,
    C_DOWN,
    C_GRAD,
    _grad_next,
    _grad_last,
    C_PROJ,
    C_TERM,
    C_OUT_EXPERT,
    _out_expert_next,
    C_OUT_PROJ,
    _out_proj_next,
    C_OUT_ENDS,
    CORE_ROWS,
) = range(21)


def dot(a, b, form=NN):
    return lax.dot_general(a, b, form, preferred_element_type=F32)


def exact_dot(a, b, form=NN):
    return lax.dot_general(
        a, b, form, preferred_element_type=F32, precision=lax.Precision.HIGHEST
    )


def iota(shape, dimension):
    return lax.broadcasted_iota(jnp.int32, shape, dimension)


def swap_heads():
    size = 4 * HEAD
    row, col = iota((size, size), 0), iota((size, size), 1)
    head = lax.div(row, HEAD)
    shift = jnp.where(head == 1, HEAD, jnp.where(head == 2, -HEAD, 0))
    return (col == row + shift).astype(F32)


def copies_of_head(count):
    shape = (HEAD, count * HEAD)
    return (lax.rem(iota(shape, 1), HEAD) == iota(shape, 0)).astype(F32)


def scale_of(rows):
    return lax.rsqrt(jnp.mean(rows * rows, axis=-1, keepdims=True) + EPS)


def kernel(
    rows,
    width,
    hidden,
    capacity,
    ends_ref,
    segments_ref,
    routes_ref,
    gates_ref,
    attn_gain_ref,
    query_gain_ref,
    key_gain_ref,
    feed_gain_ref,
    query_ref,
    key_ref,
    value_ref,
    out_ref,
    gate_ref,
    up_ref,
    down_ref,
    ends_out,
    gains_out,
    proj_out,
    expert_out,
    w_gate,
    w_up,
    w_down,
    w_attn,
    ends_in,
    gains,
    routes,
    gates,
    mask_ref,
    piece_ref,
    gains_ref,
    table_send,
    table_recv,
    slots,
    weights,
    stream,
    middle,
    cotangent,
    attn_all,
    raw_qk,
    values,
    mixed,
    y_send,
    y_recv,
    tokens,
    tokens_back,
    packed_send,
    packed,
    packed_back,
    result_send,
    result,
    result_back_send,
    result_back,
    partial_send,
    partial,
    partial_back,
    parts,
    slopes,
    attn_back,
    back_qk,
    back_v,
    acts,
    grads,
    grads_core,
    grads_y,
    out_stage,
    proj,
    proj_core,
    proj_recv,
    proj_sum,
    proj_last,
    proj_stage,
    terms,
    terms_core,
    terms_recv,
    ends_stage,
    send_sem,
    recv_sem,
    w_send,
    w_recv,
    j_send,
    j_recv,
    g_send,
    g_recv,
    c_send,
    c_recv,
    local_sem,
    out_sem,
    credit,
    y_credit,
):
    core = lax.axis_index("section")
    place = lax.axis_index("expert")
    shard = lax.axis_index("shard")
    x = lax.rem(place, RING)
    z = lax.div(place, RING)
    p = x + core * (z - x)
    q = z + core * (x - z)
    span = RING * rows
    group = RING * capacity
    other = 1 - core

    def mod(value):
        return lax.rem(value + 2 * RING, RING)

    def place_of(second, first):
        return (1 - core) * (second * RING + first) + core * (first * RING + second)

    def y_device(d):
        return (core, place, mod(shard + d))

    def p_device(d):
        return (core, place_of(q, mod(p + d)), shard)

    def q_device(d):
        return (core, place_of(mod(q + d), p), shard)

    core_device = (other, place, shard)

    def ring_copy(row, d, src, dst, device):
        return pltpu.make_async_remote_copy(
            src_ref=src,
            dst_ref=dst,
            send_sem=send_sem.at[row, d - 1],
            recv_sem=recv_sem.at[row, d - 1],
            device_id=device,
            device_id_type=MESH,
        )

    def core_copy(row, src, dst):
        return pltpu.make_async_remote_copy(
            src_ref=src,
            dst_ref=dst,
            send_sem=c_send.at[row],
            recv_sem=c_recv.at[row],
            device_id=core_device,
            device_id_type=MESH,
        )

    barrier = pltpu.get_barrier_semaphore()
    for d in (1, 2, 3):
        for device in (y_device(d), p_device(d), q_device(d)):
            pl.semaphore_signal(barrier, inc=1, device_id=device, device_id_type=MESH)
    pl.semaphore_signal(barrier, inc=1, device_id=core_device, device_id_type=MESH)
    pl.semaphore_wait(barrier, 10)

    swap = swap_heads().astype(BF16)
    piece_ref[0, :, : 4 * HEAD] = dot(query_ref[...], swap).astype(BF16)
    piece_ref[0, :, 4 * HEAD :] = key_ref[...]
    piece_ref[1, :, : 2 * HEAD] = value_ref[...]
    piece_ref[1, :, 2 * HEAD :] = dot(out_ref[...], swap).astype(BF16)
    gains_ref[0:1] = attn_gain_ref[...]
    gains_ref[1:2] = feed_gain_ref[...]
    gains_ref[2:3, : 4 * HEAD] = exact_dot(query_gain_ref[...], copies_of_head(4))
    gains_ref[2:3, 4 * HEAD : 6 * HEAD] = exact_dot(key_gain_ref[...], copies_of_head(2))
    piece_copy = core_copy(C_PIECE, piece_ref.at[other], w_attn.at[core, other, place])
    ends_copy = core_copy(C_ENDS, ends_ref.at[other], ends_in)
    gains_copy = core_copy(C_GAINS, gains_ref, gains.at[core])
    routes_copy = core_copy(C_ROUTES, routes_ref.at[other], routes.at[core])
    gates_copy = core_copy(C_GATES, gates_ref.at[other], gates.at[core])
    for copy in (piece_copy, ends_copy, gains_copy, routes_copy, gates_copy):
        copy.start()
    w_attn[core, core, place] = piece_ref[core]
    gains[core] = gains_ref[...]
    routes[core] = routes_ref[core]
    gates[core] = gates_ref[core]

    def local_weights():
        return (
            pltpu.make_async_copy(gate_ref, w_gate.at[core], local_sem.at[0]),
            pltpu.make_async_copy(up_ref, w_up.at[core], local_sem.at[1]),
            pltpu.make_async_copy(down_ref, w_down.at[core], local_sem.at[2]),
        )

    def sent_weights():
        return (
            core_copy(C_GATE, gate_ref, w_gate.at[core]),
            core_copy(C_UP, up_ref, w_up.at[core]),
            core_copy(C_DOWN, down_ref, w_down.at[core]),
        )

    for copy in local_weights():
        copy.start()

    def weight_first(layer, d):
        return pltpu.make_async_remote_copy(
            src_ref=w_attn.at[layer, core, place],
            dst_ref=w_attn.at[layer, core, place],
            send_sem=send_sem.at[WEIGHT_P + layer, d - 1],
            recv_sem=recv_sem.at[WEIGHT_P + layer, d - 1],
            device_id=p_device(d),
            device_id_type=MESH,
        )

    def weight_second(layer, d, i):
        held = place_of(q, mod(p - i))
        return pltpu.make_async_remote_copy(
            src_ref=w_attn.at[layer, core, held],
            dst_ref=w_attn.at[layer, core, held],
            send_sem=w_send.at[layer, d - 1, i],
            recv_sem=w_recv.at[layer, d - 1, i],
            device_id=q_device(d),
            device_id_type=MESH,
        )

    def weight_half(layer):
        return core_copy(C_HALF + layer, w_attn.at[layer, core], w_attn.at[layer, core])

    def start_first(layer):
        for d in (1, 3, 2):
            weight_first(layer, d).start()

    def start_second(layer):
        for i in (0, 1, 3, 2):
            if i:
                weight_first(layer, i).wait_recv()
            for d in (1, 3, 2):
                weight_second(layer, d, i).start()

    def start_half(layer):
        for i in (0, 1, 3, 2):
            for d in (1, 3, 2):
                weight_second(layer, d, i).wait_recv()
        weight_half(layer).start()

    piece_copy.wait_recv()
    start_first(0)
    start_first(1)
    ends_copy.wait_recv()
    gains_copy.wait_recv()
    first = core == 0
    stream[0] = jnp.where(first, ends_ref[0], ends_in[...]).astype(F32)
    cotangent[...] = jnp.where(first, ends_in[...], ends_ref[1]).astype(F32)

    def make_tables():
        routes_copy.wait_recv()
        gates_copy.wait_recv()
        tiles = 32
        names = iota((tiles, rows), 0)
        ahead = (iota((rows, rows), 0) < iota((rows, rows), 1)).astype(BF16)
        spread = (iota((rows, span), 1) == iota((rows, span), 0) + rows * p).astype(F32)
        row_at = lax.broadcasted_iota(jnp.int32, (2 * RING, tiles), 0)
        col_at = lax.broadcasted_iota(jnp.int32, (2 * RING, tiles), 1)
        for layer in range(2):
            named = jnp.zeros((tiles, rows), F32)
            gate = jnp.zeros((tiles, rows), F32)
            for j in range(routes.shape[1]):
                hit = (routes[layer, j : j + 1, :] == names).astype(F32)
                named = named + hit
                gate = gate + hit * gates[layer, j : j + 1, :]
            rank = dot(named.astype(BF16), ahead)
            slot = named * (rank + (1 + capacity * p).astype(F32))
            wide_slot = exact_dot(slot, spread)
            wide_gate = exact_dot(gate, spread)
            for d in range(RING):
                first_axis = mod(p + d)
                owner = place_of(lax.div(row_at, 2), first_axis)
                choose = (col_at == 2 * owner + lax.rem(row_at, 2)).astype(F32)
                table_send[d, layer, 0] = exact_dot(choose, wide_slot)
                table_send[d, layer, 1] = exact_dot(choose, wide_gate)
        for d in (1, 3, 2):
            ring_copy(
                TABLE_P, d, table_send.at[d], table_recv.at[d - 1], p_device(d)
            ).start()

    def take_tables():
        for d in (1, 3, 2):
            ring_copy(
                TABLE_P, d, table_send.at[d], table_recv.at[d - 1], p_device(d)
            ).wait_recv()
        for layer in range(2):
            for kind, target in ((0, slots), (1, weights)):
                whole = table_send[0, layer, kind]
                for d in (1, 2, 3):
                    whole = whole + table_recv[d - 1, layer, kind]
                for r in range(2 * RING):
                    target[layer, r] = whole[r : r + 1, :]

    def choose_rows(layer, second, f):
        at = lax.broadcasted_iota(jnp.int32, (group, span), 0).astype(F32) + 1.0
        return at == slots[layer, 2 * second + f]

    lanes = lax.broadcasted_iota(jnp.int32, (1, 2 * HEAD), 1)
    low_half = lanes < HEAD
    halves = (low_half, lanes >= HEAD)

    def head_mean(block):
        at_row = lax.broadcasted_iota(jnp.int32, (2 * HEAD, 2 * HEAD), 0) >= HEAD
        at_col = lax.broadcasted_iota(jnp.int32, (2 * HEAD, 2 * HEAD), 1) >= HEAD
        share = jnp.where(at_row == at_col, 1.0 / HEAD, 0.0).astype(F32)
        tiles = [
            exact_dot(block[:, i : i + 2 * HEAD], share)
            for i in range(0, block.shape[1], 2 * HEAD)
        ]
        return jnp.concatenate(tiles, axis=1)

    def qk_gain(layer):
        return gains[layer, 2:3, : 6 * HEAD]

    def make_mask():
        across = jnp.broadcast_to(
            jnp.where(core == 0, segments_ref[0:1], segments_ref[1:2]), (span, span)
        ).astype(F32)
        causal = iota((span, span), 0) >= iota((span, span), 1)
        mask_ref[...] = (causal & (across == across.T)).astype(F32)

    def allowed():
        return mask_ref[...] != 0.0

    def normed_qk(layer):
        raw = raw_qk[layer]
        scale = lax.rsqrt(head_mean(raw * raw) + EPS)
        normed = raw * scale
        low = (normed * qk_gain(layer)).astype(BF16)
        return low, normed, scale

    def probs_of(low, tile, half, mask):
        query = low[:, tile * 2 * HEAD : (tile + 1) * 2 * HEAD]
        key = low[:, 4 * HEAD :]
        query = jnp.where(halves[half], query, jnp.zeros_like(query))
        scores = dot(query, key, NT) * HEAD ** (-0.5)
        scores = jnp.where(mask, scores, NEG)
        expo = jnp.exp(scores - jnp.max(scores, axis=-1, keepdims=True))
        return expo / jnp.sum(expo, axis=-1, keepdims=True), query, key

    def weight_of(layer, half):
        return w_attn[layer, half].reshape(width, 6 * HEAD)

    def y_gather(row, buffer, layer):
        copies = [
            ring_copy(row, d, buffer.at[layer, shard], buffer.at[layer, shard], y_device(d))
            for d in (1, 3, 2)
        ]
        for copy in copies:
            copy.start()
        return copies

    def y_scatter(row):
        copies = [
            ring_copy(row, d, y_send.at[mod(shard + d)], y_recv.at[d - 1], y_device(d))
            for d in (1, 3, 2)
        ]
        for copy in copies:
            copy.start()
        return copies

    def y_total(copies):
        for copy in copies:
            copy.wait()
        total = y_send[shard].astype(F32)
        for d in (1, 2, 3):
            total = total + y_recv[d - 1].astype(F32)
        return total

    def spread_tokens(row, buffer, block):
        buffer[p] = block
        copies = [
            ring_copy(row, d, buffer.at[p], buffer.at[p], p_device(d)) for d in (1, 3, 2)
        ]
        for copy in copies:
            copy.start()
        return copies

    column_halves = (pl.ds(0, width // 2), pl.ds(width // 2, width // 2))

    def packed_copies(row, layer, f, target):
        return [
            ring_copy(
                row + f, d, packed_send.at[f, d - 1], target.at[layer, f, d], q_device(d)
            )
            for d in (1, 3, 2)
        ]

    def choose_all(layer, f):
        return jnp.concatenate(
            [choose_rows(layer, mod(q + d), f) for d in range(RING)], axis=0
        )

    def gates_all(layer, f):
        return jnp.concatenate(
            [
                jnp.broadcast_to(weights[layer, 2 * mod(q + d) + f], (group, span))
                for d in range(RING)
            ],
            axis=0,
        )

    def pack(row, layer, f, source, target, gated):
        chosen = choose_all(layer, f)
        low = chosen.astype(BF16)
        if gated:
            share = jnp.sum(
                jnp.where(chosen, gates_all(layer, f), 0.0), axis=1, keepdims=True
            )
        for cut in column_halves:
            block = dot(low, source[:, :, cut].reshape(span, width // 2))
            if gated:
                block = block * share
            block = block.astype(BF16)
            for d in (1, 3, 2):
                packed_send[f, d - 1, :, cut] = block[d * group : (d + 1) * group]
            target[layer, f, 0, :, cut] = block[:group]
        for copy in packed_copies(row, layer, f, target):
            copy.start()

    def result_copies(row, f, send, target):
        return [
            ring_copy(row + f, d, send.at[f, d - 1], target.at[f, d], q_device(-d))
            for d in (1, 3, 2)
        ]

    def put_result(row, f, send, target, columns):
        for cut in column_halves:
            block = columns(cut).astype(BF16)
            for d in (1, 3, 2):
                send[f, d - 1, :, cut] = block[d * group : (d + 1) * group]
            target[f, 0, :, cut] = block[:group]
        for copy in result_copies(row, f, send, target):
            copy.start()

    def combine(row, layer, send, target, gated):
        for f in range(2):
            chosen = choose_all(layer, f)
            if gated:
                share = jnp.where(chosen, gates_all(layer, f), 0.0)
            else:
                share = chosen.astype(F32)
            for copy in result_copies(row, f, send, target):
                copy.wait()
            share = share.astype(BF16)
            for cut in column_halves:
                total = dot(
                    share, target[f, :, :, cut].reshape(RING * group, width // 2), TN
                )
                if f == 0:
                    parts[:, cut] = total
                else:
                    total = total + parts[:, cut]
                    for i in range(RING):
                        partial_send[i, :, cut] = total[i * rows : (i + 1) * rows].astype(BF16)

    def partial_copies(row, target):
        return [
            ring_copy(
                row, d, partial_send.at[mod(p + d)], target.at[d - 1], p_device(d)
            )
            for d in (1, 3, 2)
        ]

    def start_partials(row, target):
        copies = partial_copies(row, target)
        for copy in copies:
            copy.start()
        return copies

    def total_of_partials(copies, target):
        for copy in copies:
            copy.wait()
        total = partial_send[p].astype(F32)
        for d in (1, 2, 3):
            total = total + target[d - 1].astype(F32)
        return total

    def wait_expert_weights(layer):
        @pl.when(core == layer)
        def _():
            for copy in local_weights():
                copy.wait()

        @pl.when(core != layer)
        def _():
            for copy in sent_weights():
                copy.wait_recv()

    def wait_all(copies):
        for copy in copies:
            copy.wait()

    def start_attention(layer):
        held = stream[layer]
        attn_all[layer, shard] = (held * scale_of(held) * gains[layer, 0:1, :]).astype(BF16)
        return y_gather(Y_GATHER, attn_all, layer)

    def attention(layer, copies):
        wait_all(copies)
        whole = attn_all[layer].reshape(span, width)
        raw_qk[layer] = dot(whole, weight_of(layer, 0))
        second_half = weight_of(layer, 1)
        values[layer] = dot(whole, second_half[:, : 2 * HEAD]).astype(BF16)
        low, _n, _s = normed_qk(layer)
        mask = allowed()
        value = values[layer]
        for tile in range(2):
            halves_out = []
            for half in range(2):
                probs, _q, _k = probs_of(low, tile, half, mask)
                halves_out.append(dot(probs.astype(BF16), value))
            mixed[layer, :, tile * 2 * HEAD : (tile + 1) * 2 * HEAD] = jnp.where(
                low_half, halves_out[0], halves_out[1]
            ).astype(BF16)
        out = dot(mixed[layer], second_half[:, 2 * HEAD :], NT)
        for i in range(RING):
            y_send[i] = out[i * rows : (i + 1) * rows].astype(BF16)
        return y_scatter(Y_SUM)

    def finish_attention(layer, copies):
        center = stream[layer] + y_total(copies)
        middle[layer] = center
        feed = (center * scale_of(center) * gains[layer, 1:2, :]).astype(BF16)
        return spread_tokens(TOKENS, tokens, feed)

    def feed_block(layer, f):
        return packed[layer, f].reshape(RING * group, width)

    def back_block(layer, f):
        return packed_back[layer, f].reshape(RING * group, width)

    def by_source(block):
        return block.astype(BF16).reshape(RING, group, hidden)

    def grad_core(kind):
        return core_copy(C_GRAD + kind, grads.at[other, kind], grads_core.at[kind])

    lower, upper = pl.ds(0, rows), pl.ds(rows, rows)

    def grad_ring(kind, step):
        ahead = step in (0, 2, 4)
        part, cut = (
            (2, lower),
            (2, upper),
            (1, upper),
            (-1, lower),
            (1, lower),
            (-1, upper),
        )[step]
        return pltpu.make_async_remote_copy(
            src_ref=grads.at[core, kind, mod(shard + part), cut],
            dst_ref=grads_y.at[kind, step],
            send_sem=g_send.at[kind, step],
            recv_sem=g_recv.at[kind, step],
            device_id=y_device(1 if ahead else -1),
            device_id_type=MESH,
        )

    def sum_cores():
        for kind in range(3):
            grad_core(kind).wait()

            def step(part, _):
                grads[core, kind, part] = (
                    grads[core, kind, part].astype(F32) + grads_core[kind, part].astype(F32)
                ).astype(BF16)
                return 0

            lax.fori_loop(0, RING, step, 0)
            for i in range(4):
                grad_ring(kind, i).start()

    def pass_grads():
        for kind in range(3):
            for i, part, cut in ((0, 1, lower), (1, -1, upper)):
                grad_ring(kind, i).wait()
                at = mod(shard + part)
                grads[core, kind, at, cut] = (
                    grads[core, kind, at, cut].astype(F32) + grads_y[kind, i].astype(F32)
                ).astype(BF16)
                grad_ring(kind, i + 4).start()

    def out_expert(layer):
        return core_copy(C_OUT_EXPERT + layer, out_stage, expert_out.at[:, core])

    def out_local():
        return pltpu.make_async_copy(out_stage, expert_out.at[:, core], out_sem)

    def finish_expert(layer):
        for kind in range(3):
            for i in (2, 3, 4, 5):
                grad_ring(kind, i).wait()
            for cut, merged, direct in ((lower, 4, 3), (upper, 5, 2)):
                out_stage[kind, cut] = (
                    grads[core, kind, shard, cut].astype(F32)
                    + grads_y[kind, merged].astype(F32)
                    + grads_y[kind, direct].astype(F32)
                )

        @pl.when(core == layer)
        def _():
            out_local().start()

        @pl.when(core != layer)
        def _():
            out_expert(layer).start()

    def wait_out(layer):
        @pl.when(core == layer)
        def _():
            out_local().wait()

        @pl.when(core != layer)
        def _():
            out_expert(layer).wait_send()

    def expert_grads(layer):
        for kind in range(3):
            def step(i, _):
                f, j = lax.div(i, 2), lax.rem(i, 2)
                cut = pl.ds(pl.multiple_of(j * 256, 256), 256)
                act = acts[kind, f, :, :, cut].reshape(RING * group, 256)
                rhs = back_block(layer, f) if kind == 2 else feed_block(layer, f)
                change = dot(act, rhs, TN).astype(BF16)
                grads[f, kind, 2 * j] = change[:128]
                grads[f, kind, 2 * j + 1] = change[128:]
                return 0

            lax.fori_loop(0, 4, step, 0)
            grad_core(kind).start()

    def proj_core_copy():
        return core_copy(C_PROJ, proj.at[other], proj_core)

    def proj_first(d, i):
        return pltpu.make_async_remote_copy(
            src_ref=proj.at[core, place_of(i, mod(p + d))],
            dst_ref=proj_recv.at[d - 1, i],
            send_sem=j_send.at[d - 1, i],
            recv_sem=j_recv.at[d - 1, i],
            device_id=p_device(d),
            device_id_type=MESH,
        )

    def proj_second(layer, d):
        return ring_copy(
            GRAD_Q + layer,
            d,
            proj_sum.at[mod(q + d)],
            proj_last.at[layer, d - 1],
            q_device(d),
        )

    def out_proj(layer):
        return core_copy(C_OUT_PROJ + layer, proj_stage, proj_out.at[core])

    def proj_one():
        proj_core_copy().wait()

        def step(i, _):
            proj[core, i] = (proj[core, i].astype(F32) + proj_core[i].astype(F32)).astype(BF16)
            return 0

        lax.fori_loop(0, RING * RING, step, 0)
        for i in range(RING):
            for d in (1, 3, 2):
                proj_first(d, i).start()

    def proj_two(layer):
        for i in range(RING):
            for d in (1, 3, 2):
                proj_first(d, i).wait()
            total = proj[core, place_of(i, p)].astype(F32)
            for d in (1, 2, 3):
                total = total + proj_recv[d - 1, i].astype(F32)
            proj_sum[i] = total.astype(BF16)
        for d in (1, 3, 2):
            proj_second(layer, d).start()

    def proj_three(layer):
        total = proj_sum[q].astype(F32)
        for d in (1, 3, 2):
            proj_second(layer, d).wait()
        for d in (1, 2, 3):
            total = total + proj_last[layer, d - 1].astype(F32)

        @pl.when(layer == core)
        def _():
            proj_out[core] = total

        @pl.when(layer != core)
        def _():
            proj_stage[...] = total
            out_proj(layer).start()

    def start_back(layer, incoming, change):
        center = middle[layer]
        scale = scale_of(center)
        normed = center * scale
        terms[layer, 1:2] = jnp.sum(change * normed, axis=0, keepdims=True)
        scaled = change * gains[layer, 1:2, :]
        inner = jnp.mean(scaled * normed, axis=-1, keepdims=True)
        back_mid = incoming + scale * (scaled - normed * inner)
        cotangent[...] = back_mid
        attn_back[layer, shard] = back_mid.astype(BF16)
        return y_gather(Y_GATHER_BACK, attn_back, layer)

    def attention_back(layer, copies):
        low, normed, scale = normed_qk(layer)
        wait_all(copies)
        whole_back = attn_back[layer].reshape(span, width)
        second_half = weight_of(layer, 1)
        back_mixed = dot(whole_back, second_half[:, 2 * HEAD :]).astype(BF16)
        value = values[layer]
        mask = allowed()
        back_key = jnp.zeros((span, 2 * HEAD), F32)
        back_value = jnp.zeros((span, 2 * HEAD), F32)
        tiles = []
        for tile in range(2):
            pieces = []
            for half in range(2):
                probs, query, key = probs_of(low, tile, half, mask)
                piece = back_mixed[:, tile * 2 * HEAD : (tile + 1) * 2 * HEAD]
                piece = jnp.where(halves[half], piece, jnp.zeros_like(piece))
                back_probs = dot(piece, value, NT)
                back_value = back_value + dot(probs.astype(BF16), piece, TN)
                total = jnp.sum(probs * back_probs, axis=-1, keepdims=True)
                back_scores = (probs * (back_probs - total)).astype(BF16)
                pieces.append(dot(back_scores, key))
                back_key = back_key + dot(back_scores, query, TN)
            tiles.append(jnp.where(low_half, pieces[0], pieces[1]))
        change = jnp.concatenate(tiles + [back_key], axis=1) * HEAD ** (-0.5)
        term = jnp.sum(change * normed, axis=0, keepdims=True)
        terms[layer, 2:3, : 6 * HEAD] = term
        scaled = change * qk_gain(layer)
        inner = head_mean(scaled * normed)
        back_qk[...] = (scale * (scaled - normed * inner)).astype(BF16)
        back_v[...] = back_value.astype(BF16)
        out = dot(back_qk[...], weight_of(layer, 0), NT) + dot(
            back_v[...], second_half[:, : 2 * HEAD], NT
        )
        for i in range(RING):
            y_send[i] = out[i * rows : (i + 1) * rows].astype(BF16)
        return y_scatter(Y_SUM_BACK)

    def proj_grads(layer):
        whole = attn_all[layer].reshape(span, width)
        whole_back = attn_back[layer].reshape(span, width)
        everyone = RING * RING
        first_part = dot(whole, back_qk[...], TN).astype(BF16)
        proj[0] = first_part.reshape(everyone, rows, 6 * HEAD)
        value_part = dot(whole, back_v[...], TN).astype(BF16)
        proj[1, :, :, : 2 * HEAD] = value_part.reshape(everyone, rows, 2 * HEAD)
        out_part = dot(whole_back, mixed[layer], TN).astype(BF16)
        proj[1, :, :, 2 * HEAD :] = out_part.reshape(everyone, rows, 4 * HEAD)
        proj_core_copy().start()

    def finish_back(layer, copies):
        total = y_total(copies)
        held = stream[layer]
        scale = scale_of(held)
        normed = held * scale
        terms[layer, 0:1] = jnp.sum(total * normed, axis=0, keepdims=True)
        scaled = total * gains[layer, 0:1, :]
        inner = jnp.mean(scaled * normed, axis=-1, keepdims=True)
        return (cotangent[...] + scale * (scaled - normed * inner)).astype(BF16)

    def slopes_of(gate_part, up_part):
        sigmoid = jax.nn.sigmoid(gate_part)
        silu = gate_part * sigmoid
        return up_part * sigmoid * (1.0 + gate_part * (1.0 - sigmoid)), silu

    def expert_back(layer, f, back_hidden, to_gate, to_up):
        back_gate = (back_hidden * to_gate).astype(BF16)
        back_up = (back_hidden * to_up).astype(BF16)
        acts[0, f] = by_source(back_gate)
        acts[1, f] = by_source(back_up)

        def columns(cut):
            return dot(back_gate, w_gate[layer, f, cut], NT) + dot(
                back_up, w_up[layer, f, cut], NT
            )

        put_result(RESULT_BACK, f, result_back_send, result_back, columns)

    def put_forward(layer, f, inner):
        def columns(cut):
            return dot(inner, w_down[layer, f, :, cut])

        put_result(RESULT, f, result_send, result, columns)

    terms[...] = jnp.zeros_like(terms)

    gather = start_attention(0)
    start_second(0)
    make_mask()
    make_tables()
    early = spread_tokens(TOKENS_BACK, tokens_back, cotangent[...].astype(BF16))
    start_half(0)
    for copy in sent_weights():
        copy.start()
    weight_half(0).wait_recv()
    scatter = attention(0, gather)
    start_second(1)
    take_tables()
    wait_all(early)
    for f in range(2):
        pack(PACKED_BACK, 1, f, tokens_back, packed_back, True)
    spread = finish_attention(0, scatter)
    start_half(1)
    for f in range(2):
        for copy in packed_copies(PACKED_BACK, 1, f, packed_back):
            copy.wait_send()
    wait_expert_weights(0)
    wait_all(spread)
    for f in range(2):
        pack(PACKED, 0, f, tokens, packed, False)
    for f in range(2):
        wait_all(packed_copies(PACKED, 0, f, packed))
        block = feed_block(0, f)
        gate_part = dot(block, w_gate[0, f])
        up_part = dot(block, w_up[0, f])
        inner = (gate_part * jax.nn.sigmoid(gate_part) * up_part).astype(BF16)
        put_forward(0, f, inner)
    combine(RESULT, 0, result_send, result, True)
    final = middle[0] + total_of_partials(start_partials(PARTIAL, partial), partial)
    stream[1] = final.astype(BF16).astype(F32)

    gather = start_attention(1)
    weight_half(1).wait_recv()
    scatter = attention(1, gather)
    for f in range(2):
        for copy in packed_copies(PACKED_BACK, 1, f, packed_back):
            copy.wait_recv()
    wait_expert_weights(1)
    spread = finish_attention(1, scatter)
    wait_all(spread)
    for f in range(2):
        pack(PACKED, 1, f, tokens, packed, False)
    for f in range(2):
        wait_all(packed_copies(PACKED, 1, f, packed))
        block = feed_block(1, f)
        gate_part = dot(block, w_gate[1, f])
        up_part = dot(block, w_up[1, f])
        back_hidden = dot(back_block(1, f), w_down[1, f], NT)
        to_gate, to_up = slopes_of(gate_part, up_part)
        acts[2, f] = by_source(to_up * up_part)
        expert_back(1, f, back_hidden, to_gate, to_up)
    for f in range(2):
        inner = acts[2, f].reshape(RING * group, hidden)
        put_forward(1, f, inner)
    expert_grads(1)
    combine(RESULT_BACK, 1, result_back_send, result_back, False)
    change = total_of_partials(start_partials(PARTIAL_BACK, partial_back), partial_back)

    gather = start_back(1, cotangent[...], change)
    combine(RESULT, 1, result_send, result, True)
    late = start_partials(PARTIAL, partial)
    sum_cores()
    pl.semaphore_signal(credit, inc=1, device_id=core_device, device_id_type=MESH)
    scatter = attention_back(1, gather)
    proj_grads(1)
    ends_stage[0] = (middle[1] + total_of_partials(late, partial)).astype(BF16)
    pass_grads()
    incoming = finish_back(1, scatter)
    cotangent[...] = incoming.astype(F32)

    spread = spread_tokens(TOKENS_BACK, tokens_back, incoming)
    proj_one()
    for f in range(2):
        block = feed_block(0, f)
        gate_part = dot(block, w_gate[0, f])
        up_part = dot(block, w_up[0, f])
        to_gate, to_up = slopes_of(gate_part, up_part)
        slopes[0, f] = to_gate
        slopes[1, f] = to_up
        acts[2, f] = by_source(to_up * up_part)
    wait_all(spread)
    for f in range(2):
        pack(PACKED_BACK, 0, f, tokens_back, packed_back, True)
    proj_two(1)
    for f in range(2):
        wait_all(packed_copies(PACKED_BACK, 0, f, packed_back))
        back_hidden = dot(back_block(0, f), w_down[0, f], NT)
        expert_back(0, f, back_hidden, slopes[0, f], slopes[1, f])
    finish_expert(1)
    for d in (1, -1):
        pl.semaphore_signal(y_credit, inc=1, device_id=y_device(d), device_id_type=MESH)
    pl.semaphore_wait(credit, 1)
    expert_grads(0)
    proj_three(1)
    combine(RESULT_BACK, 0, result_back_send, result_back, False)
    change = total_of_partials(start_partials(PARTIAL_BACK, partial_back), partial_back)
    gather = start_back(0, cotangent[...], change)
    pl.semaphore_wait(y_credit, 2)
    sum_cores()
    scatter = attention_back(0, gather)
    @pl.when(core != 1)
    def _():
        out_proj(1).wait_send()

    proj_grads(0)
    pass_grads()
    ends_stage[1] = finish_back(0, scatter)
    proj_one()

    ends_out[core] = jnp.where(first, ends_stage[1], ends_stage[0])
    ends_copy_out = core_copy(C_OUT_ENDS, ends_stage.at[core], ends_out.at[core])
    ends_copy_out.start()
    term_copy = core_copy(C_TERM, terms.at[other], terms_core)
    term_copy.start()
    term_copy.wait()
    terms_recv[0, 0] = terms[core] + terms_core[...]
    for axis, (row, device) in enumerate(
        ((GAIN_P, p_device), (GAIN_Q, q_device), (GAIN_Y, y_device))
    ):
        copies = [
            ring_copy(
                row, d, terms_recv.at[axis, 0], terms_recv.at[axis, d], device(d)
            )
            for d in (1, 3, 2)
        ]
        for copy in copies:
            copy.start()
        if axis == 0:
            proj_two(0)
        if axis == 1:
            proj_three(0)
        for copy in copies:
            copy.wait()
        total = terms_recv[axis, 0]
        for d in (1, 2, 3):
            total = total + terms_recv[axis, d]
        if axis < 2:
            terms_recv[axis + 1, 0] = total
        else:
            gains_out[...] = total

    wait_out(1)
    finish_expert(0)
    wait_out(0)
    for layer in range(2):
        @pl.when(core == layer)
        def _():
            out_expert(layer).wait_recv()
            out_proj(layer).wait_recv()

    @pl.when(core != 0)
    def _():
        out_proj(0).wait_send()

    ends_copy_out.wait()
    for copy in (piece_copy, ends_copy, gains_copy, routes_copy, gates_copy):
        copy.wait_send()
    for copy in sent_weights():
        copy.wait_send()
    for layer in range(2):
        weight_half(layer).wait_send()
        for d in (1, 2, 3):
            weight_first(layer, d).wait_send()
            for i in range(RING):
                weight_second(layer, d, i).wait_send()
    for d in (1, 2, 3):
        ring_copy(
            TABLE_P, d, table_send.at[d], table_recv.at[d - 1], p_device(d)
        ).wait_send()


def finish(
    ends_ref,
    gains_ref,
    proj_ref,
    experts_ref,
    ends_out,
    attn_gain_out,
    query_gain_out,
    key_gain_out,
    feed_gain_out,
    query_out,
    key_out,
    value_out,
    out_out,
    gate_out,
    up_out,
    down_out,
):
    ends_out[0] = ends_ref[...]
    attn_gain_out[...] = gains_ref[0:1]
    feed_gain_out[...] = gains_ref[1:2]
    query_gain_out[...] = exact_dot(gains_ref[2:3, : 4 * HEAD], copies_of_head(4), NT)
    key_gain_out[...] = exact_dot(gains_ref[2:3, 4 * HEAD : 6 * HEAD], copies_of_head(2), NT)
    swap = swap_heads()
    query_out[0] = exact_dot(proj_ref[0, :, : 4 * HEAD], swap)
    key_out[0] = proj_ref[0, :, 4 * HEAD :]
    value_out[0] = proj_ref[1, :, : 2 * HEAD]
    out_out[0] = exact_dot(proj_ref[1, :, 2 * HEAD :], swap)
    for f in range(2):
        gate_out[0, f] = experts_ref[0, f].T
        up_out[0, f] = experts_ref[1, f].T
        down_out[0, f] = experts_ref[2, f]


def shards(
    ends_in,
    segments,
    routes,
    gates,
    attn_gain,
    query_gain,
    key_gain,
    feed_gain,
    w_query,
    key_weight,
    value_weight,
    w_out,
    w_gate,
    w_up,
    w_down,
):
    rows = ends_in.shape[2]
    width = ends_in.shape[3]
    top = routes.shape[3]
    hidden = w_gate.shape[3]
    experts_all = w_gate.shape[1] * lax.axis_size("expert")
    capacity = 3 * rows * top // (2 * experts_all)
    group = RING * capacity
    span = RING * rows
    vmem = pl.BlockSpec(memory_space=pltpu.VMEM)
    anywhere = pl.BlockSpec(memory_space=pl.ANY)
    half = 6 * HEAD
    everyone = RING * RING
    scratch = [
        pltpu.VMEM((2, 2, width, hidden), BF16),
        pltpu.VMEM((2, 2, width, hidden), BF16),
        pltpu.VMEM((2, 2, hidden, width), BF16),
        pltpu.VMEM((2, 2, everyone, rows, half), BF16),
        pltpu.VMEM((rows, width), BF16),
        pltpu.VMEM((2, 8, width), F32),
        pltpu.VMEM((2, top, rows), jnp.int32),
        pltpu.VMEM((2, top, rows), F32),
        pltpu.VMEM((span, span), F32),
        pltpu.VMEM((2, rows, half), BF16),
        pltpu.VMEM((8, width), F32),
        pltpu.VMEM((RING, 2, 2, 8, span), F32),
        pltpu.VMEM((RING - 1, 2, 2, 8, span), F32),
        pltpu.VMEM((2, 8, 1, span), F32),
        pltpu.VMEM((2, 8, 1, span), F32),
        pltpu.VMEM((2, rows, width), F32),
        pltpu.VMEM((2, rows, width), F32),
        pltpu.VMEM((rows, width), F32),
        pltpu.VMEM((2, RING, rows, width), BF16),
        pltpu.VMEM((2, span, half), F32),
        pltpu.VMEM((2, span, 2 * HEAD), BF16),
        pltpu.VMEM((2, span, 4 * HEAD), BF16),
        pltpu.VMEM((RING, rows, width), BF16),
        pltpu.VMEM((RING - 1, rows, width), BF16),
        pltpu.VMEM((RING, rows, width), BF16),
        pltpu.VMEM((RING, rows, width), BF16),
        pltpu.VMEM((2, RING - 1, group, width), BF16),
        pltpu.VMEM((2, 2, RING, group, width), BF16),
        pltpu.VMEM((2, 2, RING, group, width), BF16),
        pltpu.VMEM((2, RING - 1, group, width), BF16),
        pltpu.VMEM((2, RING, group, width), BF16),
        pltpu.VMEM((2, RING - 1, group, width), BF16),
        pltpu.VMEM((2, RING, group, width), BF16),
        pltpu.VMEM((RING, rows, width), BF16),
        pltpu.VMEM((RING - 1, rows, width), BF16),
        pltpu.VMEM((RING - 1, rows, width), BF16),
        pltpu.VMEM((span, width), F32),
        pltpu.VMEM((2, 2, RING * group, hidden), F32),
        pltpu.VMEM((2, RING, rows, width), BF16),
        pltpu.VMEM((span, half), BF16),
        pltpu.VMEM((span, 2 * HEAD), BF16),
        pltpu.VMEM((3, 2, RING, group, hidden), BF16),
        pltpu.VMEM((2, 3, RING, hidden // RING, width), BF16),
        pltpu.VMEM((3, RING, hidden // RING, width), BF16),
        pltpu.VMEM((3, 6, rows, width), BF16),
        pltpu.VMEM((3, hidden // RING, width), F32),
        pltpu.VMEM((2, everyone, rows, half), BF16),
        pltpu.VMEM((everyone, rows, half), BF16),
        pltpu.VMEM((RING - 1, RING, rows, half), BF16),
        pltpu.VMEM((RING, rows, half), BF16),
        pltpu.VMEM((2, RING - 1, rows, half), BF16),
        pltpu.VMEM((rows, half), F32),
        pltpu.VMEM((2, 8, width), F32),
        pltpu.VMEM((8, width), F32),
        pltpu.VMEM((3, RING, 8, width), F32),
        pltpu.VMEM((2, rows, width), BF16),
        pltpu.SemaphoreType.DMA((RING_ROWS, RING - 1)),
        pltpu.SemaphoreType.DMA((RING_ROWS, RING - 1)),
        pltpu.SemaphoreType.DMA((2, RING - 1, RING)),
        pltpu.SemaphoreType.DMA((2, RING - 1, RING)),
        pltpu.SemaphoreType.DMA((RING - 1, RING)),
        pltpu.SemaphoreType.DMA((RING - 1, RING)),
        pltpu.SemaphoreType.DMA((3, 6)),
        pltpu.SemaphoreType.DMA((3, 6)),
        pltpu.SemaphoreType.DMA((CORE_ROWS,)),
        pltpu.SemaphoreType.DMA((CORE_ROWS,)),
        pltpu.SemaphoreType.DMA((3,)),
        pltpu.SemaphoreType.DMA,
        pltpu.SemaphoreType.REGULAR,
        pltpu.SemaphoreType.REGULAR,
    ]
    ends, gain_sums, proj, experts = pl.pallas_call(
        functools.partial(kernel, rows, width, hidden, capacity),
        out_shape=(
            jax.ShapeDtypeStruct((2, rows, width), BF16),
            jax.ShapeDtypeStruct((8, width), F32),
            jax.ShapeDtypeStruct((2, rows, half), F32),
            jax.ShapeDtypeStruct((3, 2, hidden // RING, width), F32),
        ),
        in_specs=[vmem] * 12 + [anywhere] * 3,
        out_specs=(vmem, vmem, vmem, anywhere),
        scratch_shapes=scratch,
        compiler_params=pltpu.CompilerParams(
            collective_id=0, has_side_effects=True, vmem_limit_bytes=62 << 20
        ),
        cost_estimate=pl.CostEstimate(
            flops=60_000_000_000, bytes_accessed=20_000_000, transcendentals=4_000_000
        ),
        name="layers",
    )(
        ends_in[0],
        segments,
        routes[0].transpose(0, 2, 1),
        gates[0].transpose(0, 2, 1),
        attn_gain,
        query_gain,
        key_gain,
        feed_gain,
        w_query[0],
        key_weight[0],
        value_weight[0],
        w_out[0].T,
        w_gate[0],
        w_up[0],
        w_down[0],
    )
    shapes = (
        ((1, 2, rows, width), BF16),
        ((1, width), F32),
        ((1, HEAD), F32),
        ((1, HEAD), F32),
        ((1, width), F32),
        ((1,) + w_query.shape[1:], F32),
        ((1,) + key_weight.shape[1:], F32),
        ((1,) + value_weight.shape[1:], F32),
        ((1, w_out.shape[2], w_out.shape[1]), F32),
        ((1, 2, width, hidden // RING), F32),
        ((1, 2, width, hidden // RING), F32),
        ((1, 2, hidden // RING, width), F32),
    )
    outputs = pl.pallas_call(
        finish,
        out_shape=tuple(jax.ShapeDtypeStruct(shape, dtype) for shape, dtype in shapes),
        in_specs=[vmem] * 4,
        out_specs=(vmem,) * len(shapes),
        compiler_params=pltpu.CompilerParams(vmem_limit_bytes=32 << 20),
        name="finish",
    )(ends, gain_sums, proj, experts)
    return (*outputs[:8], outputs[8].transpose(0, 2, 1), *outputs[9:])


def solution(mesh):
    return jax.shard_map(
        shards,
        mesh=mesh,
        in_specs=(
            P("section", None, ("expert", "shard"), None),
            P(None, "expert"),
            P("section", None, ("expert", "shard"), None),
            P("section", None, ("expert", "shard"), None),
            P("section", None),
            P("section", None),
            P("section", None),
            P("section", None),
            P("section", "expert", "shard"),
            P("section", "expert", "shard"),
            P("section", "expert", "shard"),
            P("section", "shard", "expert"),
            P("section", "expert", None, None),
            P("section", "expert", None, None),
            P("section", "expert", None, None),
        ),
        out_specs=(
            P("section", None, ("expert", "shard"), None),
            P("section", None),
            P("section", None),
            P("section", None),
            P("section", None),
            P("section", "expert", "shard"),
            P("section", "expert", "shard"),
            P("section", "expert", "shard"),
            P("section", "shard", "expert"),
            P("section", "expert", None, "shard"),
            P("section", "expert", None, "shard"),
            P("section", "expert", "shard", None),
        ),
        check_vma=False,
    )
```

```python
import functools

import jax
import jax.numpy as jnp
from jax import lax
from jax.experimental import pallas as pl
from jax.experimental.pallas import tpu as pltpu
from jax.sharding import PartitionSpec as P

EPS = 1e-06
NEG = -1e30
HEAD = 64
RING = 4
MESH = pl.DeviceIdType.MESH
F32 = jnp.float32
BF16 = jnp.bfloat16

NN = (((1,), (0,)), ((), ()))
NT = (((1,), (1,)), ((), ()))
TN = (((0,), (0,)), ((), ()))

Y_GATHER, Y_SUM, Y_GATHER_BACK, Y_SUM_BACK, TOKENS, TOKENS_BACK = range(6)
PARTIAL, PARTIAL_BACK, GRAD_Q, GAIN_P, GAIN_Q, GAIN_Y = 6, 7, 8, 10, 11, 12
WEIGHT_P, TABLE_P = 13, 15
PACKED, PACKED_BACK, RESULT, RESULT_BACK, RING_ROWS = 16, 20, 24, 28, 32

C_ENDS, C_GAINS, C_ROUTES, C_GATES, C_PIECE = range(5)
C_GATE, C_UP, C_DOWN, C_GRAD, C_PROJ, C_TERM, C_OUT_ENDS = 5, 6, 7, 8, 11, 12, 13
C_OUT_EXPERT, C_OUT_PROJ, CORE_ROWS = 14, 20, 22


def dot(a, b, form=NN):
    return lax.dot_general(a, b, form, preferred_element_type=F32)


def exact_dot(a, b, form=NN):
    return lax.dot_general(
        a, b, form, preferred_element_type=F32, precision=lax.Precision.HIGHEST
    )


def iota(shape, dimension):
    return lax.broadcasted_iota(jnp.int32, shape, dimension)


def swap_heads():
    size = 4 * HEAD
    row, col = iota((size, size), 0), iota((size, size), 1)
    head = lax.div(row, HEAD)
    shift = jnp.where(head == 1, HEAD, jnp.where(head == 2, -HEAD, 0))
    return (col == row + shift).astype(F32)


def copies_of_head(count):
    shape = (HEAD, count * HEAD)
    return (lax.rem(iota(shape, 1), HEAD) == iota(shape, 0)).astype(F32)


def scale_of(rows):
    return lax.rsqrt(jnp.mean(rows * rows, axis=-1, keepdims=True) + EPS)


def kernel(
    rows,
    width,
    hidden,
    capacity,
    ends_ref,
    segments_ref,
    routes_ref,
    gates_ref,
    attn_gain_ref,
    query_gain_ref,
    key_gain_ref,
    feed_gain_ref,
    query_ref,
    key_ref,
    value_ref,
    out_ref,
    gate_ref,
    up_ref,
    down_ref,
    ends_out,
    gains_out,
    proj_out,
    expert_out,
    w_gate,
    w_up,
    w_down,
    w_attn,
    ends_in,
    gains,
    routes,
    gates,
    mask_ref,
    piece_ref,
    gains_ref,
    table_send,
    table_recv,
    slots,
    weights,
    stream,
    middle,
    cotangent,
    attn_all,
    raw_qk,
    values,
    mixed,
    y_send,
    y_recv,
    tokens,
    tokens_back,
    packed_send,
    packed,
    packed_back,
    result_send,
    result,
    result_back,
    partial_send,
    partial,
    partial_back,
    parts,
    slopes,
    attn_back,
    back_qk,
    back_v,
    acts,
    grads,
    grads_core,
    grads_y,
    out_stage,
    proj,
    proj_core,
    proj_recv,
    proj_sum,
    proj_last,
    proj_stage,
    terms,
    terms_core,
    terms_recv,
    ends_stage,
    send_sem,
    recv_sem,
    w_send,
    w_recv,
    h_send,
    h_recv,
    j_send,
    j_recv,
    g_send,
    g_recv,
    c_send,
    c_recv,
    local_sem,
    out_sem,
    credit,
    y_credit,
):
    core = lax.axis_index("section")
    place = lax.axis_index("expert")
    shard = lax.axis_index("shard")
    x = lax.rem(place, RING)
    z = lax.div(place, RING)
    p = x + core * (z - x)
    q = z + core * (x - z)
    span = RING * rows
    group = RING * capacity
    part_rows = group // 2
    chunk = RING * part_rows
    other = 1 - core

    def mod(value):
        return lax.rem(value + 2 * RING, RING)

    def place_of(second, first):
        return (1 - core) * (second * RING + first) + core * (first * RING + second)

    def y_device(d):
        return (core, place, mod(shard + d))

    def p_device(d):
        return (core, place_of(q, mod(p + d)), shard)

    def q_device(d):
        return (core, place_of(mod(q + d), p), shard)

    core_device = (other, place, shard)

    def ring_copy(row, d, src, dst, device):
        return pltpu.make_async_remote_copy(
            src_ref=src,
            dst_ref=dst,
            send_sem=send_sem.at[row, d - 1],
            recv_sem=recv_sem.at[row, d - 1],
            device_id=device,
            device_id_type=MESH,
        )

    def core_copy(row, src, dst):
        return pltpu.make_async_remote_copy(
            src_ref=src,
            dst_ref=dst,
            send_sem=c_send.at[row],
            recv_sem=c_recv.at[row],
            device_id=core_device,
            device_id_type=MESH,
        )

    barrier = pltpu.get_barrier_semaphore()
    for d in (1, 2, 3):
        for device in (y_device(d), p_device(d), q_device(d)):
            pl.semaphore_signal(barrier, inc=1, device_id=device, device_id_type=MESH)
    pl.semaphore_signal(barrier, inc=1, device_id=core_device, device_id_type=MESH)

    def local_weights():
        return (
            pltpu.make_async_copy(gate_ref, w_gate.at[core], local_sem.at[0]),
            pltpu.make_async_copy(up_ref, w_up.at[core], local_sem.at[1]),
            pltpu.make_async_copy(down_ref, w_down.at[core], local_sem.at[2]),
        )

    swap = swap_heads().astype(BF16)
    piece_ref[0, :, : 4 * HEAD] = dot(query_ref[...], swap).astype(BF16)
    piece_ref[0, :, 4 * HEAD :] = key_ref[...]
    piece_ref[1, :, : 2 * HEAD] = value_ref[...]
    piece_ref[1, :, 2 * HEAD :] = dot(out_ref[...], swap).astype(BF16)
    gains_ref[0:1] = attn_gain_ref[...]
    gains_ref[1:2] = feed_gain_ref[...]
    gains_ref[2:3, : 4 * HEAD] = exact_dot(query_gain_ref[...], copies_of_head(4))
    gains_ref[2:3, 4 * HEAD : 6 * HEAD] = exact_dot(key_gain_ref[...], copies_of_head(2))
    w_attn[core, core, place] = piece_ref[core]
    gains[core] = gains_ref[...]
    routes[core] = routes_ref[core]
    gates[core] = gates_ref[core]
    across = jnp.broadcast_to(
        jnp.where(core == 0, segments_ref[0:1], segments_ref[1:2]), (span, span)
    ).astype(F32)
    causal = iota((span, span), 0) >= iota((span, span), 1)
    mask_ref[...] = (causal & (across == across.T)).astype(F32)
    terms[...] = jnp.zeros_like(terms)
    for copy in local_weights():
        copy.start()

    pl.semaphore_wait(barrier, 10)
    piece_copy = core_copy(C_PIECE, piece_ref.at[other], w_attn.at[core, other, place])
    ends_copy = core_copy(C_ENDS, ends_ref.at[other], ends_in)
    gains_copy = core_copy(C_GAINS, gains_ref, gains.at[core])
    routes_copy = core_copy(C_ROUTES, routes_ref.at[other], routes.at[core])
    gates_copy = core_copy(C_GATES, gates_ref.at[other], gates.at[core])
    for copy in (piece_copy, ends_copy, gains_copy, routes_copy, gates_copy):
        copy.start()

    def sent_weights():
        return (
            core_copy(C_GATE, gate_ref, w_gate.at[core]),
            core_copy(C_UP, up_ref, w_up.at[core]),
            core_copy(C_DOWN, down_ref, w_down.at[core]),
        )

    def weight_first(layer, d):
        return pltpu.make_async_remote_copy(
            src_ref=w_attn.at[layer, core, place],
            dst_ref=w_attn.at[layer, core, place],
            send_sem=send_sem.at[WEIGHT_P + layer, d - 1],
            recv_sem=recv_sem.at[WEIGHT_P + layer, d - 1],
            device_id=p_device(d),
            device_id_type=MESH,
        )

    def weight_second(layer, d, i):
        held = place_of(q, mod(p - i))
        return pltpu.make_async_remote_copy(
            src_ref=w_attn.at[layer, core, held],
            dst_ref=w_attn.at[layer, core, held],
            send_sem=w_send.at[layer, d - 1, i],
            recv_sem=w_recv.at[layer, d - 1, i],
            device_id=q_device(d),
            device_id_type=MESH,
        )

    def weight_pass(layer, d, i):
        held = place_of(mod(q - d), mod(p - i))
        return pltpu.make_async_remote_copy(
            src_ref=w_attn.at[layer, core, held],
            dst_ref=w_attn.at[layer, core, held],
            send_sem=h_send.at[layer, d, i],
            recv_sem=h_recv.at[layer, d, i],
            device_id=core_device,
            device_id_type=MESH,
        )

    def start_first(layer):
        for d in (1, 3, 2):
            weight_first(layer, d).start()

    def start_second(layer):
        for i in (0, 1, 3, 2):
            if i:
                weight_first(layer, i).wait_recv()
            for d in (1, 3, 2):
                weight_second(layer, d, i).start()
            weight_pass(layer, 0, i).start()

    def start_pass(layer):
        for i in (0, 1, 3, 2):
            for d in (1, 3, 2):
                weight_second(layer, d, i).wait_recv()
                weight_pass(layer, d, i).start()

    def wait_pass(layer):
        for d in range(RING):
            for i in range(RING):
                weight_pass(layer, d, i).wait_recv()

    piece_copy.wait_recv()
    start_first(0)
    start_first(1)
    ends_copy.wait_recv()
    gains_copy.wait_recv()
    first = core == 0
    stream[0] = jnp.where(first, ends_ref[0], ends_in[...]).astype(F32)
    cotangent[...] = jnp.where(first, ends_in[...], ends_ref[1]).astype(F32)

    def make_tables():
        routes_copy.wait_recv()
        gates_copy.wait_recv()
        tiles = 32
        names = iota((tiles, rows), 0)
        ahead = (iota((rows, rows), 0) < iota((rows, rows), 1)).astype(BF16)
        spread = (iota((rows, span), 1) == iota((rows, span), 0) + rows * p).astype(F32)
        row_at = lax.broadcasted_iota(jnp.int32, (2 * RING, tiles), 0)
        col_at = lax.broadcasted_iota(jnp.int32, (2 * RING, tiles), 1)
        for layer in range(2):
            named = jnp.zeros((tiles, rows), F32)
            gate = jnp.zeros((tiles, rows), F32)
            for j in range(routes.shape[1]):
                hit = (routes[layer, j : j + 1, :] == names).astype(F32)
                named = named + hit
                gate = gate + hit * gates[layer, j : j + 1, :]
            rank = dot(named.astype(BF16), ahead)
            slot = named * (rank + (1 + capacity * p).astype(F32))
            wide_slot = exact_dot(slot, spread)
            wide_gate = exact_dot(gate, spread)
            for d in range(RING):
                first_axis = mod(p + d)
                owner = place_of(lax.div(row_at, 2), first_axis)
                choose = (col_at == 2 * owner + lax.rem(row_at, 2)).astype(F32)
                table_send[d, layer, 0] = exact_dot(choose, wide_slot)
                table_send[d, layer, 1] = exact_dot(choose, wide_gate)
        for d in (1, 3, 2):
            ring_copy(
                TABLE_P, d, table_send.at[d], table_recv.at[d - 1], p_device(d)
            ).start()

    def take_tables():
        for d in (1, 3, 2):
            ring_copy(
                TABLE_P, d, table_send.at[d], table_recv.at[d - 1], p_device(d)
            ).wait_recv()
        for layer in range(2):
            for kind, target in ((0, slots), (1, weights)):
                whole = table_send[0, layer, kind]
                for d in (1, 2, 3):
                    whole = whole + table_recv[d - 1, layer, kind]
                for r in range(2 * RING):
                    target[layer, r] = whole[r : r + 1, :]

    def choose_rows(layer, second, f, h):
        at = iota((part_rows, span), 0) + (1 + part_rows * h)
        return at.astype(F32) == slots[layer, 2 * second + f]

    lanes = lax.broadcasted_iota(jnp.int32, (1, 2 * HEAD), 1)
    low_half = lanes < HEAD
    halves = (low_half, lanes >= HEAD)

    def head_mean(block):
        at_row = lax.broadcasted_iota(jnp.int32, (2 * HEAD, 2 * HEAD), 0) >= HEAD
        at_col = lax.broadcasted_iota(jnp.int32, (2 * HEAD, 2 * HEAD), 1) >= HEAD
        share = jnp.where(at_row == at_col, 1.0 / HEAD, 0.0).astype(F32)
        tiles = [
            exact_dot(block[:, i : i + 2 * HEAD], share)
            for i in range(0, block.shape[1], 2 * HEAD)
        ]
        return jnp.concatenate(tiles, axis=1)

    def qk_gain(layer):
        return gains[layer, 2:3, : 6 * HEAD]

    def allowed():
        return mask_ref[...] != 0.0

    def normed_qk(layer):
        raw = raw_qk[layer]
        scale = lax.rsqrt(head_mean(raw * raw) + EPS)
        normed = raw * scale
        low = (normed * qk_gain(layer)).astype(BF16)
        return low, normed, scale

    def probs_of(low, tile, half, mask):
        query = low[:, tile * 2 * HEAD : (tile + 1) * 2 * HEAD]
        key = low[:, 4 * HEAD :]
        query = jnp.where(halves[half], query, jnp.zeros_like(query))
        scores = dot(query, key, NT) * HEAD ** (-0.5)
        scores = jnp.where(mask, scores, NEG)
        expo = jnp.exp(scores - jnp.max(scores, axis=-1, keepdims=True))
        return expo / jnp.sum(expo, axis=-1, keepdims=True), query, key

    half_rows = (slice(0, 8), slice(8, 16))

    def weight_of(layer, half, start, stop, places=slice(0, 16)):
        block = w_attn[layer, half, places, :, start * HEAD : stop * HEAD]
        return block.reshape(block.shape[0] * rows, (stop - start) * HEAD)

    def y_gather(row, buffer, layer):
        copies = [
            ring_copy(row, d, buffer.at[layer, shard], buffer.at[layer, shard], y_device(d))
            for d in (1, 3, 2)
        ]
        for copy in copies:
            copy.start()
        return copies

    def y_scatter(row):
        copies = [
            ring_copy(row, d, y_send.at[mod(shard + d)], y_recv.at[d - 1], y_device(d))
            for d in (1, 3, 2)
        ]
        for copy in copies:
            copy.start()
        return copies

    def y_total(copies):
        for copy in copies:
            copy.wait()
        total = y_send[shard].astype(F32)
        for d in (1, 2, 3):
            total = total + y_recv[d - 1].astype(F32)
        return total

    def spread_tokens(row, buffer, block):
        buffer[p] = block
        copies = [
            ring_copy(row, d, buffer.at[p], buffer.at[p], p_device(d)) for d in (1, 3, 2)
        ]
        for copy in copies:
            copy.start()
        return copies

    column_halves = (pl.ds(0, width // 2), pl.ds(width // 2, width // 2))

    def packed_copies(row, layer, f, h, target):
        return [
            ring_copy(
                row + 2 * f + h,
                d,
                packed_send.at[f, h, d - 1],
                target.at[layer, f, h, d],
                q_device(d),
            )
            for d in (1, 3, 2)
        ]

    def choose_all(layer, f, h):
        return jnp.concatenate(
            [choose_rows(layer, mod(q + d), f, h) for d in range(RING)], axis=0
        )

    def gates_all(layer, f):
        return jnp.concatenate(
            [
                jnp.broadcast_to(weights[layer, 2 * mod(q + d) + f], (part_rows, span))
                for d in range(RING)
            ],
            axis=0,
        )

    def each_chunk(step):
        def body(i, _):
            step(lax.div(i, 2), lax.rem(i, 2))
            return 0

        lax.fori_loop(0, 4, body, 0)

    def pack(row, layer, source, target, gated):
        def step(f, h):
            chosen = choose_all(layer, f, h)
            low = chosen.astype(BF16)
            if gated:
                share = jnp.sum(
                    jnp.where(chosen, gates_all(layer, f), 0.0), axis=1, keepdims=True
                )
            for cut in column_halves:
                block = dot(low, source[:, :, cut].reshape(span, width // 2))
                if gated:
                    block = block * share
                block = block.astype(BF16)
                for d in (1, 3, 2):
                    packed_send[f, h, d - 1, :, cut] = block[
                        d * part_rows : (d + 1) * part_rows
                    ]
                target[layer, f, h, 0, :, cut] = block[:part_rows]
            for copy in packed_copies(row, layer, f, h, target):
                copy.start()

        each_chunk(step)

    def result_copies(row, f, h, send, target):
        return [
            ring_copy(
                row + 2 * f + h,
                d,
                send.at[f, h, d - 1],
                target.at[f, h, d],
                q_device(-d),
            )
            for d in (1, 3, 2)
        ]

    def put_result(row, f, h, send, target, columns):
        for cut in column_halves:
            block = columns(cut).astype(BF16)
            for d in (1, 3, 2):
                send[f, h, d - 1, :, cut] = block[d * part_rows : (d + 1) * part_rows]
            target[f, h, 0, :, cut] = block[:part_rows]
        for copy in result_copies(row, f, h, send, target):
            copy.start()

    def combine(row, layer, send, target, gated):
        parts[...] = jnp.zeros_like(parts)

        def step(f, h):
            chosen = choose_all(layer, f, h)
            if gated:
                share = jnp.where(chosen, gates_all(layer, f), 0.0)
            else:
                share = chosen.astype(F32)
            share = share.astype(BF16)
            wait_all(result_copies(row, f, h, send, target))
            for cut in column_halves:
                parts[:, cut] += dot(
                    share, target[f, h, :, :, cut].reshape(chunk, width // 2), TN
                )

        each_chunk(step)
        for i in range(RING):
            partial_send[i] = parts[i * rows : (i + 1) * rows].astype(BF16)

    def partial_copies(row, target):
        return [
            ring_copy(
                row, d, partial_send.at[mod(p + d)], target.at[d - 1], p_device(d)
            )
            for d in (1, 3, 2)
        ]

    def start_partials(row, target):
        copies = partial_copies(row, target)
        for copy in copies:
            copy.start()
        return copies

    def total_of_partials(copies, target):
        for copy in copies:
            copy.wait()
        total = partial_send[p].astype(F32)
        for d in (1, 2, 3):
            total = total + target[d - 1].astype(F32)
        return total

    def wait_expert_weights(layer):
        @pl.when(core == layer)
        def _():
            for copy in local_weights():
                copy.wait()

        @pl.when(core != layer)
        def _():
            for copy in sent_weights():
                copy.wait_recv()

    def wait_all(copies):
        for copy in copies:
            copy.wait()

    def start_attention(layer):
        held = stream[layer]
        attn_all[layer, shard] = (held * scale_of(held) * gains[layer, 0:1, :]).astype(BF16)
        return y_gather(Y_GATHER, attn_all, layer)

    def attention(layer, copies):
        wait_all(copies)
        whole = attn_all[layer].reshape(span, width)
        raw_qk[layer] = dot(whole, weight_of(layer, 0, 0, 6))
        values[layer] = dot(whole, weight_of(layer, 1, 0, 2)).astype(BF16)
        low, _n, _s = normed_qk(layer)
        mask = allowed()
        value = values[layer]
        for tile in range(2):
            halves_out = []
            for half in range(2):
                probs, _q, _k = probs_of(low, tile, half, mask)
                halves_out.append(dot(probs.astype(BF16), value))
            mixed[layer, :, tile * 2 * HEAD : (tile + 1) * 2 * HEAD] = jnp.where(
                low_half, halves_out[0], halves_out[1]
            ).astype(BF16)
        for places, cut in zip(half_rows, column_halves):
            out = dot(mixed[layer], weight_of(layer, 1, 2, 6, places), NT)
            for i in range(RING):
                y_send[i, :, cut] = out[i * rows : (i + 1) * rows].astype(BF16)
        return y_scatter(Y_SUM)

    def finish_attention(layer, copies):
        center = stream[layer] + y_total(copies)
        middle[layer] = center
        feed = (center * scale_of(center) * gains[layer, 1:2, :]).astype(BF16)
        return spread_tokens(TOKENS, tokens, feed)

    def feed_block(layer, f):
        return packed[layer, f].reshape(RING * group, width)

    def back_block(layer, f):
        return packed_back[layer, f].reshape(RING * group, width)

    def feed_chunk(layer, f, h):
        return packed[layer, f, h].reshape(chunk, width)

    def back_chunk(layer, f, h):
        return packed_back[layer, f, h].reshape(chunk, width)

    def grad_core(kind):
        return core_copy(C_GRAD + kind, grads.at[other, kind], grads_core.at[kind])

    lower, upper = pl.ds(0, rows), pl.ds(rows, rows)

    def grad_ring(kind, step):
        ahead = step in (0, 2, 4)
        part, cut = (
            (2, lower),
            (2, upper),
            (1, upper),
            (-1, lower),
            (1, lower),
            (-1, upper),
        )[step]
        return pltpu.make_async_remote_copy(
            src_ref=grads.at[core, kind, mod(shard + part), cut],
            dst_ref=grads_y.at[kind, step],
            send_sem=g_send.at[kind, step],
            recv_sem=g_recv.at[kind, step],
            device_id=y_device(1 if ahead else -1),
            device_id_type=MESH,
        )

    def sum_cores(kind):
        grad_core(kind).wait()

        def step(part, _):
            grads[core, kind, part] = (
                grads[core, kind, part].astype(F32) + grads_core[kind, part].astype(F32)
            ).astype(BF16)
            return 0

        lax.fori_loop(0, RING, step, 0)

    def start_ring(kind):
        for i in range(4):
            grad_ring(kind, i).start()

    def pass_grads(kind):
        for i, part, cut in ((0, 1, lower), (1, -1, upper)):
            grad_ring(kind, i).wait()
            at = mod(shard + part)
            grads[core, kind, at, cut] = (
                grads[core, kind, at, cut].astype(F32) + grads_y[kind, i].astype(F32)
            ).astype(BF16)
            grad_ring(kind, i + 4).start()

    def out_expert(layer, kind):
        return core_copy(
            C_OUT_EXPERT + 3 * layer + kind, out_stage.at[kind], expert_out.at[kind, core]
        )

    def out_local(kind):
        return pltpu.make_async_copy(
            out_stage.at[kind], expert_out.at[kind, core], out_sem.at[kind]
        )

    def finish_expert(layer, kind):
        for i in (2, 3, 4, 5):
            grad_ring(kind, i).wait()
        for cut, merged, direct in ((lower, 4, 3), (upper, 5, 2)):
            out_stage[kind, cut] = (
                grads[core, kind, shard, cut].astype(F32)
                + grads_y[kind, merged].astype(F32)
                + grads_y[kind, direct].astype(F32)
            )

        @pl.when(core == layer)
        def _():
            out_local(kind).start()

        @pl.when(core != layer)
        def _():
            out_expert(layer, kind).start()

    def wait_out(layer):
        for kind in range(3):
            @pl.when(core == layer)
            def _():
                out_local(kind).wait()

            @pl.when(core != layer)
            def _():
                out_expert(layer, kind).wait_send()

    def expert_grads(layer):
        for kind in range(3):
            def step(i, _):
                f, j = lax.div(i, 2), lax.rem(i, 2)
                cut = pl.ds(pl.multiple_of(j * 256, 256), 256)
                act = acts[kind, f, :, :, cut].reshape(2 * chunk, 256)
                rhs = back_block(layer, f) if kind == 2 else feed_block(layer, f)
                change = dot(act, rhs, TN).astype(BF16)
                grads[f, kind, 2 * j] = change[:128]
                grads[f, kind, 2 * j + 1] = change[128:]
                return 0

            lax.fori_loop(0, 4, step, 0)
            grad_core(kind).start()

    def proj_core_copy():
        return core_copy(C_PROJ, proj.at[other], proj_core)

    def proj_first(d, i):
        return pltpu.make_async_remote_copy(
            src_ref=proj.at[core, place_of(i, mod(p + d))],
            dst_ref=proj_recv.at[d - 1, i],
            send_sem=j_send.at[d - 1, i],
            recv_sem=j_recv.at[d - 1, i],
            device_id=p_device(d),
            device_id_type=MESH,
        )

    def proj_second(layer, d):
        return ring_copy(
            GRAD_Q + layer,
            d,
            proj_sum.at[mod(q + d)],
            proj_last.at[layer, d - 1],
            q_device(d),
        )

    def out_proj(layer):
        return core_copy(C_OUT_PROJ + layer, proj_stage, proj_out.at[core])

    def proj_one():
        proj_core_copy().wait()

        def step(i, _):
            proj[core, i] = (proj[core, i].astype(F32) + proj_core[i].astype(F32)).astype(BF16)
            return 0

        lax.fori_loop(0, RING * RING, step, 0)
        for i in range(RING):
            for d in (1, 3, 2):
                proj_first(d, i).start()

    def proj_two(layer):
        for i in range(RING):
            for d in (1, 3, 2):
                proj_first(d, i).wait()
            total = proj[core, place_of(i, p)].astype(F32)
            for d in (1, 2, 3):
                total = total + proj_recv[d - 1, i].astype(F32)
            proj_sum[i] = total.astype(BF16)
        for d in (1, 3, 2):
            proj_second(layer, d).start()

    def proj_three(layer):
        total = proj_sum[q].astype(F32)
        for d in (1, 3, 2):
            proj_second(layer, d).wait()
        for d in (1, 2, 3):
            total = total + proj_last[layer, d - 1].astype(F32)

        @pl.when(layer == core)
        def _():
            proj_out[core] = total

        @pl.when(layer != core)
        def _():
            proj_stage[...] = total
            out_proj(layer).start()

    def start_back(layer, incoming, change):
        center = middle[layer]
        scale = scale_of(center)
        normed = center * scale
        terms[layer, 1:2] = jnp.sum(change * normed, axis=0, keepdims=True)
        scaled = change * gains[layer, 1:2, :]
        inner = jnp.mean(scaled * normed, axis=-1, keepdims=True)
        back_mid = incoming + scale * (scaled - normed * inner)
        cotangent[...] = back_mid
        attn_back[layer, shard] = back_mid.astype(BF16)
        return y_gather(Y_GATHER_BACK, attn_back, layer)

    def attention_back(layer):
        low, normed, scale = normed_qk(layer)
        whole_back = attn_back[layer].reshape(span, width)
        back_mixed = dot(whole_back, weight_of(layer, 1, 2, 6)).astype(BF16)
        value = values[layer]
        mask = allowed()
        back_key = jnp.zeros((span, 2 * HEAD), F32)
        back_value = jnp.zeros((span, 2 * HEAD), F32)
        tiles = []
        for tile in range(2):
            pieces = []
            for half in range(2):
                probs, query, key = probs_of(low, tile, half, mask)
                piece = back_mixed[:, tile * 2 * HEAD : (tile + 1) * 2 * HEAD]
                piece = jnp.where(halves[half], piece, jnp.zeros_like(piece))
                back_probs = dot(piece, value, NT)
                back_value = back_value + dot(probs.astype(BF16), piece, TN)
                total = jnp.sum(probs * back_probs, axis=-1, keepdims=True)
                back_scores = (probs * (back_probs - total)).astype(BF16)
                pieces.append(dot(back_scores, key))
                back_key = back_key + dot(back_scores, query, TN)
            tiles.append(jnp.where(low_half, pieces[0], pieces[1]))
        change = jnp.concatenate(tiles + [back_key], axis=1) * HEAD ** (-0.5)
        term = jnp.sum(change * normed, axis=0, keepdims=True)
        terms[layer, 2:3, : 6 * HEAD] = term
        scaled = change * qk_gain(layer)
        inner = head_mean(scaled * normed)
        back_qk[...] = (scale * (scaled - normed * inner)).astype(BF16)
        back_v[...] = back_value.astype(BF16)
        for places, cut in zip(half_rows, column_halves):
            out = dot(back_qk[...], weight_of(layer, 0, 0, 6, places), NT)
            out = out + dot(back_v[...], weight_of(layer, 1, 0, 2, places), NT)
            for i in range(RING):
                y_send[i, :, cut] = out[i * rows : (i + 1) * rows].astype(BF16)
        return y_scatter(Y_SUM_BACK)

    def proj_grads(layer):
        def step(i, _):
            cut = pl.ds(pl.multiple_of(i * 4 * rows, 4 * rows), 4 * rows)
            at = pl.ds(i * 4, 4)
            feed = attn_all[layer, :, :, cut].reshape(span, 4 * rows)
            back = attn_back[layer, :, :, cut].reshape(span, 4 * rows)
            for half, start, stop, lhs, rhs in (
                (0, 0, 6, feed, back_qk[...]),
                (1, 0, 2, feed, back_v[...]),
                (1, 2, 6, back, mixed[layer]),
            ):
                change = dot(lhs, rhs, TN).astype(BF16)
                proj[half, at, :, start * HEAD : stop * HEAD] = change.reshape(
                    4, rows, (stop - start) * HEAD
                )
            return 0

        lax.fori_loop(0, 4, step, 0)
        proj_core_copy().start()

    def finish_back(layer, copies):
        total = y_total(copies)
        held = stream[layer]
        scale = scale_of(held)
        normed = held * scale
        terms[layer, 0:1] = jnp.sum(total * normed, axis=0, keepdims=True)
        scaled = total * gains[layer, 0:1, :]
        inner = jnp.mean(scaled * normed, axis=-1, keepdims=True)
        return (cotangent[...] + scale * (scaled - normed * inner)).astype(BF16)

    def slopes_of(gate_part, up_part):
        sigmoid = jax.nn.sigmoid(gate_part)
        silu = gate_part * sigmoid
        return up_part * sigmoid * (1.0 + gate_part * (1.0 - sigmoid)), silu

    def expert_back(layer, f, h, back_hidden, to_gate, to_up):
        back_gate = (back_hidden * to_gate).astype(BF16)
        back_up = (back_hidden * to_up).astype(BF16)
        acts[0, f, h] = back_gate
        acts[1, f, h] = back_up

        def columns(cut):
            return dot(back_gate, w_gate[layer, f, cut], NT) + dot(
                back_up, w_up[layer, f, cut], NT
            )

        put_result(RESULT_BACK, f, h, packed_send, result_back, columns)

    def put_forward(layer, f, h, inner):
        def columns(cut):
            return dot(inner, w_down[layer, f, :, cut])

        put_result(RESULT, f, h, result_send, result, columns)

    def gate_and_up(layer, f, h):
        block = feed_chunk(layer, f, h)
        return dot(block, w_gate[layer, f]), dot(block, w_up[layer, f])

    gather = start_attention(0)
    start_second(0)
    make_tables()
    early = spread_tokens(TOKENS_BACK, tokens_back, cotangent[...].astype(BF16))
    start_pass(0)
    for copy in sent_weights():
        copy.start()
    wait_pass(0)
    scatter = attention(0, gather)
    start_second(1)
    take_tables()
    wait_all(early)
    pack(PACKED_BACK, 1, tokens_back, packed_back, True)
    spread = finish_attention(0, scatter)
    start_pass(1)

    def packed_back_sent(f, h):
        for copy in packed_copies(PACKED_BACK, 1, f, h, packed_back):
            copy.wait_send()

    each_chunk(packed_back_sent)
    wait_expert_weights(0)
    wait_all(spread)
    pack(PACKED, 0, tokens, packed, False)

    def experts_forward(f, h):
        wait_all(packed_copies(PACKED, 0, f, h, packed))
        gate_part, up_part = gate_and_up(0, f, h)
        inner = (gate_part * jax.nn.sigmoid(gate_part) * up_part).astype(BF16)
        put_forward(0, f, h, inner)

    each_chunk(experts_forward)
    combine(RESULT, 0, result_send, result, True)
    final = middle[0] + total_of_partials(start_partials(PARTIAL, partial), partial)
    stream[1] = final.astype(BF16).astype(F32)

    gather = start_attention(1)
    wait_pass(1)
    wait_expert_weights(1)

    def hidden_back(f, h):
        for copy in packed_copies(PACKED_BACK, 1, f, h, packed_back):
            copy.wait_recv()
        slopes[0, f, h] = dot(back_chunk(1, f, h), w_down[1, f], NT)

    each_chunk(hidden_back)
    scatter = attention(1, gather)
    spread = finish_attention(1, scatter)
    wait_all(spread)
    pack(PACKED, 1, tokens, packed, False)

    def experts_both(f, h):
        wait_all(packed_copies(PACKED, 1, f, h, packed))
        gate_part, up_part = gate_and_up(1, f, h)
        to_gate, to_up = slopes_of(gate_part, up_part)
        acts[2, f, h] = (to_up * up_part).astype(BF16)
        expert_back(1, f, h, slopes[0, f, h], to_gate, to_up)

    each_chunk(experts_both)
    each_chunk(lambda f, h: put_forward(1, f, h, acts[2, f, h]))
    expert_grads(1)
    combine(RESULT_BACK, 1, packed_send, result_back, False)
    copies = start_partials(PARTIAL_BACK, partial_back)
    sum_cores(0)
    start_ring(0)
    change = total_of_partials(copies, partial_back)

    gather = start_back(1, cotangent[...], change)
    combine(RESULT, 1, result_send, result, True)
    late = start_partials(PARTIAL, partial)
    sum_cores(1)
    wait_all(gather)
    start_ring(1)
    pass_grads(0)
    scatter = attention_back(1)
    proj_grads(1)
    ends_stage[0] = (middle[1] + total_of_partials(late, partial)).astype(BF16)
    sum_cores(2)
    pl.semaphore_signal(credit, inc=1, device_id=core_device, device_id_type=MESH)
    incoming = finish_back(1, scatter)
    cotangent[...] = incoming.astype(F32)

    spread = spread_tokens(TOKENS_BACK, tokens_back, incoming)
    start_ring(2)
    pass_grads(1)
    proj_one()

    def find_slopes(f, h):
        gate_part, up_part = gate_and_up(0, f, h)
        to_gate, to_up = slopes_of(gate_part, up_part)
        slopes[0, f, h] = to_gate
        slopes[1, f, h] = to_up
        acts[2, f, h] = (to_up * up_part).astype(BF16)

    each_chunk(find_slopes)
    wait_all(spread)
    pack(PACKED_BACK, 0, tokens_back, packed_back, True)
    pass_grads(2)
    proj_two(1)

    def experts_back(f, h):
        wait_all(packed_copies(PACKED_BACK, 0, f, h, packed_back))
        back_hidden = dot(back_chunk(0, f, h), w_down[0, f], NT)
        expert_back(0, f, h, back_hidden, slopes[0, f, h], slopes[1, f, h])

    each_chunk(experts_back)
    for kind in range(3):
        finish_expert(1, kind)
    for d in (1, -1):
        pl.semaphore_signal(y_credit, inc=1, device_id=y_device(d), device_id_type=MESH)
    pl.semaphore_wait(credit, 1)
    expert_grads(0)
    proj_three(1)
    combine(RESULT_BACK, 0, packed_send, result_back, False)
    copies = start_partials(PARTIAL_BACK, partial_back)
    pl.semaphore_wait(y_credit, 2)
    sum_cores(0)
    start_ring(0)
    change = total_of_partials(copies, partial_back)
    gather = start_back(0, cotangent[...], change)
    sum_cores(1)
    wait_all(gather)
    start_ring(1)
    pass_grads(0)
    scatter = attention_back(0)

    @pl.when(core != 1)
    def _():
        out_proj(1).wait_send()

    proj_grads(0)
    sum_cores(2)
    start_ring(2)
    ends_stage[1] = finish_back(0, scatter)

    ends_out[core] = jnp.where(first, ends_stage[1], ends_stage[0])
    ends_copy_out = core_copy(C_OUT_ENDS, ends_stage.at[core], ends_out.at[core])
    ends_copy_out.start()
    term_copy = core_copy(C_TERM, terms.at[other], terms_core)
    term_copy.start()
    wait_out(1)
    proj_one()
    term_copy.wait()
    terms_recv[0, 0] = terms[core] + terms_core[...]
    for axis, (row, device) in enumerate(
        ((GAIN_P, p_device), (GAIN_Q, q_device), (GAIN_Y, y_device))
    ):
        copies = [
            ring_copy(
                row, d, terms_recv.at[axis, 0], terms_recv.at[axis, d], device(d)
            )
            for d in (1, 3, 2)
        ]
        for copy in copies:
            copy.start()
        if axis == 0:
            pass_grads(1)
            proj_two(0)
        if axis == 1:
            pass_grads(2)
            proj_three(0)
            finish_expert(0, 0)
        if axis == 2:
            finish_expert(0, 1)
        wait_all(copies)
        total = terms_recv[axis, 0]
        for d in (1, 2, 3):
            total = total + terms_recv[axis, d]
        if axis < 2:
            terms_recv[axis + 1, 0] = total
        else:
            gains_out[...] = total

    finish_expert(0, 2)
    wait_out(0)
    for layer in range(2):
        @pl.when(core == layer)
        def _():
            for kind in range(3):
                out_expert(layer, kind).wait_recv()
            out_proj(layer).wait_recv()

    @pl.when(core != 0)
    def _():
        out_proj(0).wait_send()

    ends_copy_out.wait()
    for copy in (piece_copy, ends_copy, gains_copy, routes_copy, gates_copy):
        copy.wait_send()
    for copy in sent_weights():
        copy.wait_send()
    for layer in range(2):
        for d in range(RING):
            for i in range(RING):
                weight_pass(layer, d, i).wait_send()
        for d in (1, 2, 3):
            weight_first(layer, d).wait_send()
            for i in range(RING):
                weight_second(layer, d, i).wait_send()
    for d in (1, 2, 3):
        ring_copy(
            TABLE_P, d, table_send.at[d], table_recv.at[d - 1], p_device(d)
        ).wait_send()


def finish(
    ends_ref,
    gains_ref,
    proj_ref,
    experts_ref,
    ends_out,
    attn_gain_out,
    query_gain_out,
    key_gain_out,
    feed_gain_out,
    query_out,
    key_out,
    value_out,
    out_out,
    gate_out,
    up_out,
    down_out,
    ends,
    gains,
    proj,
    experts,
    turned,
    sems,
):
    pieces = [(kind, f) for kind in range(3) for f in range(2)]
    moves = [
        pltpu.make_async_copy(
            experts_ref.at[kind, f], experts.at[kind, f], sems.at[2 * kind + f]
        )
        for kind, f in pieces
    ]
    moves += [
        pltpu.make_async_copy(ends_ref, ends, sems.at[6]),
        pltpu.make_async_copy(gains_ref, gains, sems.at[7]),
        pltpu.make_async_copy(proj_ref, proj, sems.at[8]),
    ]
    for move in moves:
        move.start()
    results = []
    for i, (kind, f) in enumerate(pieces):
        moves[i].wait()
        if kind < 2:
            turned[kind, f] = experts[kind, f].T
        source = experts.at[kind, f] if kind == 2 else turned.at[kind, f]
        target = (gate_out, up_out, down_out)[kind]
        results.append(pltpu.make_async_copy(source, target.at[0, f], sems.at[9 + i]))
        results[-1].start()
    moves[6].wait()
    results.append(pltpu.make_async_copy(ends, ends_out.at[0], sems.at[15]))
    results[-1].start()
    moves[7].wait()
    attn_gain_out[...] = gains[0:1]
    feed_gain_out[...] = gains[1:2]
    query_gain_out[...] = exact_dot(gains[2:3, : 4 * HEAD], copies_of_head(4), NT)
    key_gain_out[...] = exact_dot(gains[2:3, 4 * HEAD : 6 * HEAD], copies_of_head(2), NT)
    moves[8].wait()
    swap = swap_heads()
    query_out[0] = exact_dot(proj[0, :, : 4 * HEAD], swap)
    key_out[0] = proj[0, :, 4 * HEAD :]
    value_out[0] = proj[1, :, : 2 * HEAD]
    out_out[0] = exact_dot(proj[1, :, 2 * HEAD :], swap)
    for result in results:
        result.wait()


def shards(
    ends_in,
    segments,
    routes,
    gates,
    attn_gain,
    query_gain,
    key_gain,
    feed_gain,
    w_query,
    key_weight,
    value_weight,
    w_out,
    w_gate,
    w_up,
    w_down,
):
    rows = ends_in.shape[2]
    width = ends_in.shape[3]
    top = routes.shape[3]
    hidden = w_gate.shape[3]
    experts_all = w_gate.shape[1] * lax.axis_size("expert")
    capacity = 3 * rows * top // (2 * experts_all)
    group = RING * capacity
    part_rows = group // 2
    chunk = RING * part_rows
    span = RING * rows
    vmem = pl.BlockSpec(memory_space=pltpu.VMEM)
    anywhere = pl.BlockSpec(memory_space=pl.ANY)
    half = 6 * HEAD
    everyone = RING * RING
    scratch = [
        pltpu.VMEM((2, 2, width, hidden), BF16),
        pltpu.VMEM((2, 2, width, hidden), BF16),
        pltpu.VMEM((2, 2, hidden, width), BF16),
        pltpu.VMEM((2, 2, everyone, rows, half), BF16),
        pltpu.VMEM((rows, width), BF16),
        pltpu.VMEM((2, 8, width), F32),
        pltpu.VMEM((2, top, rows), jnp.int32),
        pltpu.VMEM((2, top, rows), F32),
        pltpu.VMEM((span, span), F32),
        pltpu.VMEM((2, rows, half), BF16),
        pltpu.VMEM((8, width), F32),
        pltpu.VMEM((RING, 2, 2, 8, span), F32),
        pltpu.VMEM((RING - 1, 2, 2, 8, span), F32),
        pltpu.VMEM((2, 8, 1, span), F32),
        pltpu.VMEM((2, 8, 1, span), F32),
        pltpu.VMEM((2, rows, width), F32),
        pltpu.VMEM((2, rows, width), F32),
        pltpu.VMEM((rows, width), F32),
        pltpu.VMEM((2, RING, rows, width), BF16),
        pltpu.VMEM((2, span, half), F32),
        pltpu.VMEM((2, span, 2 * HEAD), BF16),
        pltpu.VMEM((2, span, 4 * HEAD), BF16),
        pltpu.VMEM((RING, rows, width), BF16),
        pltpu.VMEM((RING - 1, rows, width), BF16),
        pltpu.VMEM((RING, rows, width), BF16),
        pltpu.VMEM((RING, rows, width), BF16),
        pltpu.VMEM((2, 2, RING - 1, group // 2, width), BF16),
        pltpu.VMEM((2, 2, 2, RING, group // 2, width), BF16),
        pltpu.VMEM((2, 2, 2, RING, group // 2, width), BF16),
        pltpu.VMEM((2, 2, RING - 1, group // 2, width), BF16),
        pltpu.VMEM((2, 2, RING, group // 2, width), BF16),
        pltpu.VMEM((2, 2, RING, group // 2, width), BF16),
        pltpu.VMEM((RING, rows, width), BF16),
        pltpu.VMEM((RING - 1, rows, width), BF16),
        pltpu.VMEM((RING - 1, rows, width), BF16),
        pltpu.VMEM((span, width), F32),
        pltpu.VMEM((2, 2, 2, 2 * group, hidden), F32),
        pltpu.VMEM((2, RING, rows, width), BF16),
        pltpu.VMEM((span, half), BF16),
        pltpu.VMEM((span, 2 * HEAD), BF16),
        pltpu.VMEM((3, 2, 2, 2 * group, hidden), BF16),
        pltpu.VMEM((2, 3, RING, hidden // RING, width), BF16),
        pltpu.VMEM((3, RING, hidden // RING, width), BF16),
        pltpu.VMEM((3, 6, rows, width), BF16),
        pltpu.VMEM((3, hidden // RING, width), F32),
        pltpu.VMEM((2, everyone, rows, half), BF16),
        pltpu.VMEM((everyone, rows, half), BF16),
        pltpu.VMEM((RING - 1, RING, rows, half), BF16),
        pltpu.VMEM((RING, rows, half), BF16),
        pltpu.VMEM((2, RING - 1, rows, half), BF16),
        pltpu.VMEM((rows, half), F32),
        pltpu.VMEM((2, 8, width), F32),
        pltpu.VMEM((8, width), F32),
        pltpu.VMEM((3, RING, 8, width), F32),
        pltpu.VMEM((2, rows, width), BF16),
        pltpu.SemaphoreType.DMA((RING_ROWS, RING - 1)),
        pltpu.SemaphoreType.DMA((RING_ROWS, RING - 1)),
        pltpu.SemaphoreType.DMA((2, RING - 1, RING)),
        pltpu.SemaphoreType.DMA((2, RING - 1, RING)),
        pltpu.SemaphoreType.DMA((2, RING, RING)),
        pltpu.SemaphoreType.DMA((2, RING, RING)),
        pltpu.SemaphoreType.DMA((RING - 1, RING)),
        pltpu.SemaphoreType.DMA((RING - 1, RING)),
        pltpu.SemaphoreType.DMA((3, 6)),
        pltpu.SemaphoreType.DMA((3, 6)),
        pltpu.SemaphoreType.DMA((CORE_ROWS,)),
        pltpu.SemaphoreType.DMA((CORE_ROWS,)),
        pltpu.SemaphoreType.DMA((3,)),
        pltpu.SemaphoreType.DMA((3,)),
        pltpu.SemaphoreType.REGULAR,
        pltpu.SemaphoreType.REGULAR,
    ]
    ends, gain_sums, proj, experts = pl.pallas_call(
        functools.partial(kernel, rows, width, hidden, capacity),
        out_shape=(
            jax.ShapeDtypeStruct((2, rows, width), BF16),
            jax.ShapeDtypeStruct((8, width), F32),
            jax.ShapeDtypeStruct((2, rows, half), F32),
            jax.ShapeDtypeStruct((3, 2, hidden // RING, width), F32),
        ),
        in_specs=[vmem] * 12 + [anywhere] * 3,
        out_specs=(vmem, vmem, vmem, anywhere),
        scratch_shapes=scratch,
        compiler_params=pltpu.CompilerParams(
            collective_id=0, has_side_effects=True, vmem_limit_bytes=63 << 20
        ),
        cost_estimate=pl.CostEstimate(
            flops=60_000_000_000, bytes_accessed=20_000_000, transcendentals=4_000_000
        ),
        name="layers",
    )(
        ends_in[0],
        segments,
        routes[0].transpose(0, 2, 1),
        gates[0].transpose(0, 2, 1),
        attn_gain,
        query_gain,
        key_gain,
        feed_gain,
        w_query[0],
        key_weight[0],
        value_weight[0],
        w_out[0].T,
        w_gate[0],
        w_up[0],
        w_down[0],
    )
    shapes = (
        ((1, 2, rows, width), BF16),
        ((1, width), F32),
        ((1, HEAD), F32),
        ((1, HEAD), F32),
        ((1, width), F32),
        ((1,) + w_query.shape[1:], F32),
        ((1,) + key_weight.shape[1:], F32),
        ((1,) + value_weight.shape[1:], F32),
        ((1, w_out.shape[2], w_out.shape[1]), F32),
        ((1, 2, width, hidden // RING), F32),
        ((1, 2, width, hidden // RING), F32),
        ((1, 2, hidden // RING, width), F32),
    )
    outputs = pl.pallas_call(
        finish,
        out_shape=tuple(jax.ShapeDtypeStruct(shape, dtype) for shape, dtype in shapes),
        in_specs=[anywhere] * 4,
        out_specs=(anywhere,) + (vmem,) * 8 + (anywhere,) * 3,
        scratch_shapes=[
            pltpu.VMEM((2, rows, width), BF16),
            pltpu.VMEM((8, width), F32),
            pltpu.VMEM((2, rows, half), F32),
            pltpu.VMEM((3, 2, hidden // RING, width), F32),
            pltpu.VMEM((2, 2, width, hidden // RING), F32),
            pltpu.SemaphoreType.DMA((16,)),
        ],
        compiler_params=pltpu.CompilerParams(vmem_limit_bytes=60 << 20),
        name="finish",
    )(ends, gain_sums, proj, experts)
    return (*outputs[:8], outputs[8].transpose(0, 2, 1), *outputs[9:])


def solution(mesh):
    return jax.shard_map(
        shards,
        mesh=mesh,
        in_specs=(
            P("section", None, ("expert", "shard"), None),
            P(None, "expert"),
            P("section", None, ("expert", "shard"), None),
            P("section", None, ("expert", "shard"), None),
            P("section", None),
            P("section", None),
            P("section", None),
            P("section", None),
            P("section", "expert", "shard"),
            P("section", "expert", "shard"),
            P("section", "expert", "shard"),
            P("section", "shard", "expert"),
            P("section", "expert", None, None),
            P("section", "expert", None, None),
            P("section", "expert", None, None),
        ),
        out_specs=(
            P("section", None, ("expert", "shard"), None),
            P("section", None),
            P("section", None),
            P("section", None),
            P("section", None),
            P("section", "expert", "shard"),
            P("section", "expert", "shard"),
            P("section", "expert", "shard"),
            P("section", "shard", "expert"),
            P("section", "expert", None, "shard"),
            P("section", "expert", None, "shard"),
            P("section", "expert", "shard", None),
        ),
        check_vma=False,
    )
```

```python
import functools

import jax
import jax.numpy as jnp
from jax import lax
from jax.experimental import pallas as pl
from jax.experimental.pallas import tpu as pltpu
from jax.sharding import PartitionSpec as P

EPS = 1e-06
NEG = -1e30
HEAD = 64
RING = 4
MESH = pl.DeviceIdType.MESH
F32 = jnp.float32
BF16 = jnp.bfloat16

NN = (((1,), (0,)), ((), ()))
NT = (((1,), (1,)), ((), ()))
TN = (((0,), (0,)), ((), ()))

PIECES = 4
Y_GATHER, Y_SUM, Y_GATHER_BACK, Y_SUM_BACK = 0, 4, 8, 12
TOKENS, TOKENS_BACK, PARTIAL, PARTIAL_BACK = 16, 20, 24, 28
GRAD_Q, GAIN_P, GAIN_Q, GAIN_Y, WEIGHT_P, TABLE_P = 32, 34, 35, 36, 37, 39
PACKED, PACKED_BACK, RESULT, RESULT_BACK, RING_ROWS = 40, 44, 48, 52, 56

C_ENDS, C_GAINS, C_ROUTES, C_GATES, C_PIECE = range(5)
C_GATE, C_UP, C_DOWN, C_GRAD, C_PROJ, C_TERM, C_OUT_ENDS = 5, 6, 7, 8, 11, 12, 13
C_OUT_EXPERT, C_OUT_PROJ, CORE_ROWS = 14, 20, 22


def dot(a, b, form=NN):
    return lax.dot_general(a, b, form, preferred_element_type=F32)


def exact_dot(a, b, form=NN):
    return lax.dot_general(
        a, b, form, preferred_element_type=F32, precision=lax.Precision.HIGHEST
    )


def iota(shape, dimension):
    return lax.broadcasted_iota(jnp.int32, shape, dimension)


def swap_heads():
    size = 4 * HEAD
    row, col = iota((size, size), 0), iota((size, size), 1)
    head = lax.div(row, HEAD)
    shift = jnp.where(head == 1, HEAD, jnp.where(head == 2, -HEAD, 0))
    return (col == row + shift).astype(F32)


def copies_of_head(count):
    shape = (HEAD, count * HEAD)
    return (lax.rem(iota(shape, 1), HEAD) == iota(shape, 0)).astype(F32)


def scale_of(rows):
    return lax.rsqrt(jnp.mean(rows * rows, axis=-1, keepdims=True) + EPS)


def kernel(
    rows,
    width,
    hidden,
    capacity,
    ends_ref,
    segments_ref,
    routes_ref,
    gates_ref,
    attn_gain_ref,
    query_gain_ref,
    key_gain_ref,
    feed_gain_ref,
    query_ref,
    key_ref,
    value_ref,
    out_ref,
    gate_ref,
    up_ref,
    down_ref,
    ends_out,
    gains_out,
    proj_out,
    expert_out,
    w_gate,
    w_up,
    w_down,
    w_attn,
    ends_in,
    gains,
    routes,
    gates,
    mask_ref,
    piece_ref,
    gains_ref,
    table_send,
    table_recv,
    slots,
    weights,
    stream,
    middle,
    cotangent,
    attn_all,
    raw_qk,
    values,
    mixed,
    y_send,
    y_recv,
    tokens,
    tokens_back,
    packed_send,
    packed,
    packed_back,
    result_send,
    result,
    result_back,
    partial_send,
    partial,
    partial_back,
    parts,
    slopes,
    attn_back,
    low_qk,
    back_v,
    acts,
    grads,
    grads_core,
    grads_y,
    out_stage,
    proj,
    proj_core,
    proj_recv,
    proj_sum,
    proj_last,
    proj_stage,
    terms,
    terms_core,
    terms_recv,
    ends_stage,
    send_sem,
    recv_sem,
    w_send,
    w_recv,
    h_send,
    h_recv,
    j_send,
    j_recv,
    g_send,
    g_recv,
    c_send,
    c_recv,
    local_sem,
    out_sem,
    credit,
    y_credit,
):
    core = lax.axis_index("section")
    place = lax.axis_index("expert")
    shard = lax.axis_index("shard")
    x = lax.rem(place, RING)
    z = lax.div(place, RING)
    p = x + core * (z - x)
    q = z + core * (x - z)
    span = RING * rows
    group = RING * capacity
    part_rows = group // 2
    chunk = RING * part_rows
    other = 1 - core

    def mod(value):
        return lax.rem(value + 2 * RING, RING)

    def place_of(second, first):
        return (1 - core) * (second * RING + first) + core * (first * RING + second)

    def y_device(d):
        return (core, place, mod(shard + d))

    def p_device(d):
        return (core, place_of(q, mod(p + d)), shard)

    def q_device(d):
        return (core, place_of(mod(q + d), p), shard)

    core_device = (other, place, shard)

    def order(k):
        return k + lax.div(k, 2) * (5 - 2 * k)

    def ring_copy(row, d, src, dst, device):
        return pltpu.make_async_remote_copy(
            src_ref=src,
            dst_ref=dst,
            send_sem=send_sem.at[row, d - 1],
            recv_sem=recv_sem.at[row, d - 1],
            device_id=device,
            device_id_type=MESH,
        )

    def core_copy(row, src, dst):
        return pltpu.make_async_remote_copy(
            src_ref=src,
            dst_ref=dst,
            send_sem=c_send.at[row],
            recv_sem=c_recv.at[row],
            device_id=core_device,
            device_id_type=MESH,
        )

    barrier = pltpu.get_barrier_semaphore()
    for d in (1, 2, 3):
        for device in (y_device(d), p_device(d), q_device(d)):
            pl.semaphore_signal(barrier, inc=1, device_id=device, device_id_type=MESH)
    pl.semaphore_signal(barrier, inc=1, device_id=core_device, device_id_type=MESH)

    def local_weights():
        return (
            pltpu.make_async_copy(gate_ref, w_gate.at[core], local_sem.at[0]),
            pltpu.make_async_copy(up_ref, w_up.at[core], local_sem.at[1]),
            pltpu.make_async_copy(down_ref, w_down.at[core], local_sem.at[2]),
        )

    swap = swap_heads().astype(BF16)
    piece_ref[0, :, : 4 * HEAD] = dot(query_ref[...], swap).astype(BF16)
    piece_ref[0, :, 4 * HEAD :] = key_ref[...]
    piece_ref[1, :, : 2 * HEAD] = value_ref[...]
    piece_ref[1, :, 2 * HEAD :] = dot(out_ref[...], swap).astype(BF16)
    gains_ref[0:1] = attn_gain_ref[...]
    gains_ref[1:2] = feed_gain_ref[...]
    gains_ref[2:3, : 4 * HEAD] = exact_dot(query_gain_ref[...], copies_of_head(4))
    gains_ref[2:3, 4 * HEAD : 6 * HEAD] = exact_dot(key_gain_ref[...], copies_of_head(2))
    w_attn[core, core, place] = piece_ref[core]
    gains[core] = gains_ref[...]
    routes[core] = routes_ref[core]
    gates[core] = gates_ref[core]
    across = jnp.broadcast_to(
        jnp.where(core == 0, segments_ref[0:1], segments_ref[1:2]), (span, span)
    ).astype(F32)
    causal = iota((span, span), 0) >= iota((span, span), 1)
    mask_ref[...] = (causal & (across == across.T)).astype(F32)
    terms[...] = jnp.zeros_like(terms)
    for copy in local_weights():
        copy.start()

    pl.semaphore_wait(barrier, 10)
    piece_copy = core_copy(C_PIECE, piece_ref.at[other], w_attn.at[core, other, place])
    ends_copy = core_copy(C_ENDS, ends_ref.at[other], ends_in)
    gains_copy = core_copy(C_GAINS, gains_ref, gains.at[core])
    routes_copy = core_copy(C_ROUTES, routes_ref.at[other], routes.at[core])
    gates_copy = core_copy(C_GATES, gates_ref.at[other], gates.at[core])
    for copy in (piece_copy, ends_copy, gains_copy, routes_copy, gates_copy):
        copy.start()

    def sent_weights():
        return (
            core_copy(C_GATE, gate_ref, w_gate.at[core]),
            core_copy(C_UP, up_ref, w_up.at[core]),
            core_copy(C_DOWN, down_ref, w_down.at[core]),
        )

    def weight_first(layer, d):
        return pltpu.make_async_remote_copy(
            src_ref=w_attn.at[layer, core, place],
            dst_ref=w_attn.at[layer, core, place],
            send_sem=send_sem.at[WEIGHT_P + layer, d - 1],
            recv_sem=recv_sem.at[WEIGHT_P + layer, d - 1],
            device_id=p_device(d),
            device_id_type=MESH,
        )

    def weight_second(layer, d, i):
        held = place_of(q, mod(p - i))
        return pltpu.make_async_remote_copy(
            src_ref=w_attn.at[layer, core, held],
            dst_ref=w_attn.at[layer, core, held],
            send_sem=w_send.at[layer, d - 1, i],
            recv_sem=w_recv.at[layer, d - 1, i],
            device_id=q_device(d),
            device_id_type=MESH,
        )

    def weight_pass(layer, d, i):
        held = place_of(mod(q - d), mod(p - i))
        return pltpu.make_async_remote_copy(
            src_ref=w_attn.at[layer, core, held],
            dst_ref=w_attn.at[layer, core, held],
            send_sem=h_send.at[layer, d, i],
            recv_sem=h_recv.at[layer, d, i],
            device_id=core_device,
            device_id_type=MESH,
        )

    def start_first(layer):
        for d in (1, 3, 2):
            weight_first(layer, d).start()

    def start_second(layer):
        for i in (0, 1, 3, 2):
            if i:
                weight_first(layer, i).wait_recv()
            for d in (1, 3, 2):
                weight_second(layer, d, i).start()
            weight_pass(layer, 0, i).start()

    def start_pass(layer):
        for i in (0, 1, 3, 2):
            for d in (1, 3, 2):
                weight_second(layer, d, i).wait_recv()
                weight_pass(layer, d, i).start()

    def wait_pass(layer):
        for d in range(RING):
            for i in range(RING):
                weight_pass(layer, d, i).wait_recv()

    piece_copy.wait_recv()
    start_first(0)
    start_first(1)
    ends_copy.wait_recv()
    gains_copy.wait_recv()
    first = core == 0
    stream[0] = jnp.where(first, ends_ref[0], ends_in[...]).astype(F32)
    cotangent[...] = jnp.where(first, ends_in[...], ends_ref[1]).astype(F32)

    def make_tables():
        routes_copy.wait_recv()
        gates_copy.wait_recv()
        tiles = 32
        names = iota((tiles, rows), 0)
        ahead = (iota((rows, rows), 0) < iota((rows, rows), 1)).astype(BF16)
        spread = (iota((rows, span), 1) == iota((rows, span), 0) + rows * p).astype(F32)
        row_at = lax.broadcasted_iota(jnp.int32, (2 * RING, tiles), 0)
        col_at = lax.broadcasted_iota(jnp.int32, (2 * RING, tiles), 1)
        for layer in range(2):
            named = jnp.zeros((tiles, rows), F32)
            gate = jnp.zeros((tiles, rows), F32)
            for j in range(routes.shape[1]):
                hit = (routes[layer, j : j + 1, :] == names).astype(F32)
                named = named + hit
                gate = gate + hit * gates[layer, j : j + 1, :]
            rank = dot(named.astype(BF16), ahead)
            slot = named * (rank + (1 + capacity * p).astype(F32))
            wide_slot = exact_dot(slot, spread)
            wide_gate = exact_dot(gate, spread)
            for d in range(RING):
                first_axis = mod(p + d)
                owner = place_of(lax.div(row_at, 2), first_axis)
                choose = (col_at == 2 * owner + lax.rem(row_at, 2)).astype(F32)
                table_send[d, layer, 0] = exact_dot(choose, wide_slot)
                table_send[d, layer, 1] = exact_dot(choose, wide_gate)
        for d in (1, 3, 2):
            ring_copy(
                TABLE_P, d, table_send.at[d], table_recv.at[d - 1], p_device(d)
            ).start()

    def take_tables():
        for d in (1, 3, 2):
            ring_copy(
                TABLE_P, d, table_send.at[d], table_recv.at[d - 1], p_device(d)
            ).wait_recv()
        for layer in range(2):
            for kind, target in ((0, slots), (1, weights)):
                whole = table_send[0, layer, kind]
                for d in (1, 2, 3):
                    whole = whole + table_recv[d - 1, layer, kind]
                for r in range(2 * RING):
                    target[layer, r] = whole[r : r + 1, :]

    def choose_rows(layer, second, f, h):
        at = iota((part_rows, span), 0) + (1 + part_rows * h)
        return at.astype(F32) == slots[layer, 2 * second + f]

    lanes = lax.broadcasted_iota(jnp.int32, (1, 2 * HEAD), 1)
    low_half = lanes < HEAD
    halves = (low_half, lanes >= HEAD)

    def head_mean(block):
        at_row = lax.broadcasted_iota(jnp.int32, (2 * HEAD, 2 * HEAD), 0) >= HEAD
        at_col = lax.broadcasted_iota(jnp.int32, (2 * HEAD, 2 * HEAD), 1) >= HEAD
        share = jnp.where(at_row == at_col, 1.0 / HEAD, 0.0).astype(F32)
        tiles = [
            exact_dot(block[:, i : i + 2 * HEAD], share)
            for i in range(0, block.shape[1], 2 * HEAD)
        ]
        return jnp.concatenate(tiles, axis=1)

    def qk_gain(layer):
        return gains[layer, 2:3, : 6 * HEAD]

    def normed_qk(layer):
        raw = raw_qk[layer]
        scale = lax.rsqrt(head_mean(raw * raw) + EPS)
        normed = raw * scale
        low = (normed * qk_gain(layer)).astype(BF16)
        return low, normed, scale

    def head_columns(tile):
        return slice(tile * 2 * HEAD, (tile + 1) * 2 * HEAD)

    def block_rows(block):
        return pl.ds(pl.multiple_of(block * rows, rows), rows)

    def one_half(block, half):
        return jnp.where(halves[half], block, jnp.zeros_like(block))

    def exp_scores(query, key, mask):
        scores = dot(query, key, NT) * HEAD ** (-0.5)
        expo = jnp.exp(jnp.where(mask != 0.0, scores, NEG))
        return expo, 1.0 / jnp.sum(expo, axis=-1, keepdims=True)

    half_rows = (slice(0, 8), slice(8, 16))

    def weight_of(layer, half, start, stop, places=slice(0, 16)):
        block = w_attn[layer, half, places, :, start * HEAD : stop * HEAD]
        return block.reshape(block.shape[0] * rows, (stop - start) * HEAD)

    row_halves = tuple(pl.ds(i * rows // PIECES, rows // PIECES) for i in range(PIECES))

    def y_gather_copy(row, d, h, buffer, layer):
        held = buffer.at[layer, shard, row_halves[h]]
        return ring_copy(row + h, d, held, held, y_device(d))

    def start_gather(row, h, buffer, layer):
        for d in (1, 3, 2):
            y_gather_copy(row, d, h, buffer, layer).start()

    def y_scatter_copy(row, d, h):
        cut = row_halves[h]
        return ring_copy(
            row + h, d, y_send.at[mod(shard + d), cut], y_recv.at[d - 1, cut], y_device(d)
        )

    def y_scatter(row):
        for h in range(len(row_halves)):
            for d in (1, 3, 2):
                y_scatter_copy(row, d, h).start()

    def y_total(row, h):
        cut = row_halves[h]
        for d in (1, 3, 2):
            y_scatter_copy(row, d, h).wait()
        total = y_send[shard, cut].astype(F32)
        for d in (1, 2, 3):
            total = total + y_recv[d - 1, cut].astype(F32)
        return total

    def spread_copy(row, buffer, d, h):
        held = buffer.at[p, row_halves[h]]
        return ring_copy(row + h, d, held, held, p_device(d))

    def spread_half(row, buffer, h, block):
        buffer[p, row_halves[h]] = block
        for d in (1, 3, 2):
            spread_copy(row, buffer, d, h).start()

    def wait_spread(row, buffer):
        for h in range(len(row_halves)):
            for d in (1, 3, 2):
                spread_copy(row, buffer, d, h).wait()

    column_halves = (pl.ds(0, width // 2), pl.ds(width // 2, width // 2))

    def packed_copies(row, layer, f, h, target):
        return [
            ring_copy(
                row + 2 * f + h,
                d,
                packed_send.at[f, h, d - 1],
                target.at[layer, f, h, d],
                q_device(d),
            )
            for d in (1, 3, 2)
        ]

    def choose_all(layer, f, h):
        return jnp.concatenate(
            [choose_rows(layer, mod(q + d), f, h) for d in range(RING)], axis=0
        )

    def gates_all(layer, f):
        return jnp.concatenate(
            [
                jnp.broadcast_to(weights[layer, 2 * mod(q + d) + f], (part_rows, span))
                for d in range(RING)
            ],
            axis=0,
        )

    def each_chunk(step):
        def body(i, _):
            step(lax.div(i, 2), lax.rem(i, 2))
            return 0

        lax.fori_loop(0, 4, body, 0)

    def pack(row, layer, source, target, gated):
        def step(f, h):
            chosen = choose_all(layer, f, h)
            low = chosen.astype(BF16)
            if gated:
                share = jnp.sum(
                    jnp.where(chosen, gates_all(layer, f), 0.0), axis=1, keepdims=True
                )
            for cut in column_halves:
                block = dot(low, source[:, :, cut].reshape(span, width // 2))
                if gated:
                    block = block * share
                block = block.astype(BF16)
                for d in (1, 3, 2):
                    packed_send[f, h, d - 1, :, cut] = block[
                        d * part_rows : (d + 1) * part_rows
                    ]
                target[layer, f, h, 0, :, cut] = block[:part_rows]
            for copy in packed_copies(row, layer, f, h, target):
                copy.start()

        each_chunk(step)

    def result_copies(row, f, h, send, target):
        return [
            ring_copy(
                row + 2 * f + h,
                d,
                send.at[f, h, d - 1],
                target.at[f, h, d],
                q_device(-d),
            )
            for d in (1, 3, 2)
        ]

    def put_result(row, f, h, send, target, columns):
        for cut in column_halves:
            block = columns(cut).astype(BF16)
            for d in (1, 3, 2):
                send[f, h, d - 1, :, cut] = block[d * part_rows : (d + 1) * part_rows]
            target[f, h, 0, :, cut] = block[:part_rows]
        for copy in result_copies(row, f, h, send, target):
            copy.start()

    def combine(row, layer, send, target, gated):
        parts[...] = jnp.zeros_like(parts)

        def step(f, h):
            chosen = choose_all(layer, f, h)
            if gated:
                share = jnp.where(chosen, gates_all(layer, f), 0.0)
            else:
                share = chosen.astype(F32)
            share = share.astype(BF16)
            wait_all(result_copies(row, f, h, send, target))
            for cut in column_halves:
                parts[:, cut] += dot(
                    share, target[f, h, :, :, cut].reshape(chunk, width // 2), TN
                )

        each_chunk(step)
        for i in range(RING):
            partial_send[i] = parts[i * rows : (i + 1) * rows].astype(BF16)

    def partial_copy(row, target, d, h):
        cut = row_halves[h]
        return ring_copy(
            row + h, d, partial_send.at[mod(p + d), cut], target.at[d - 1, cut], p_device(d)
        )

    def start_partials(row, target):
        for h in range(len(row_halves)):
            for d in (1, 3, 2):
                partial_copy(row, target, d, h).start()

    def total_of_partials(row, target, h):
        cut = row_halves[h]
        for d in (1, 3, 2):
            partial_copy(row, target, d, h).wait()
        total = partial_send[p, cut].astype(F32)
        for d in (1, 2, 3):
            total = total + target[d - 1, cut].astype(F32)
        return total

    def wait_expert_weights(layer):
        @pl.when(core == layer)
        def _():
            for copy in local_weights():
                copy.wait()

        @pl.when(core != layer)
        def _():
            for copy in sent_weights():
                copy.wait_recv()

    def wait_all(copies):
        for copy in copies:
            copy.wait()

    def start_attention(layer, h):
        cut = row_halves[h]
        held = stream[layer, cut]
        attn_all[layer, shard, cut] = (
            held * scale_of(held) * gains[layer, 0:1, :]
        ).astype(BF16)
        start_gather(Y_GATHER, h, attn_all, layer)

    def attention(layer):
        for h in range(len(row_halves)):
            for d in (1, 3, 2):
                y_gather_copy(Y_GATHER, d, h, attn_all, layer).wait()
        whole = attn_all[layer].reshape(span, width)
        raw_qk[layer] = dot(whole, weight_of(layer, 0, 0, 6))
        values[layer] = dot(whole, weight_of(layer, 1, 0, 2)).astype(BF16)
        low_qk[...] = normed_qk(layer)[0]

        key = low_qk[:, head_columns(2)]
        value = values[layer]
        for group_of in ((2, 1, 3, 0),):
            blocks = [mod(shard + d) for d in group_of]
            cuts = [block_rows(block) for block in blocks]
            mask = jnp.concatenate([mask_ref[cut] for cut in cuts], axis=0)
            tiles = []
            for tile in range(2):
                query = jnp.concatenate([low_qk[cut, head_columns(tile)] for cut in cuts], axis=0)
                outs = []
                for half in range(2):
                    expo, share = exp_scores(one_half(query, half), key, mask)
                    outs.append(dot((expo * share).astype(BF16), value))
                tiles.append(jnp.where(low_half, outs[0], outs[1]).astype(BF16))
            whole_mixed = jnp.concatenate(tiles, axis=1)
            out = dot(whole_mixed, weight_of(layer, 1, 2, 6), NT).astype(BF16)
            for i, (d, block, cut) in enumerate(zip(group_of, blocks, cuts)):
                part = slice(i * rows, (i + 1) * rows)
                mixed[layer, cut] = whole_mixed[part]
                y_send[block] = out[part]
        y_scatter(Y_SUM)

    def finish_attention(layer):
        for h, cut in enumerate(row_halves):
            center = stream[layer, cut] + y_total(Y_SUM, h)
            middle[layer, cut] = center
            feed = center * scale_of(center) * gains[layer, 1:2, :]
            spread_half(TOKENS, tokens, h, feed.astype(BF16))

    def feed_block(layer, f):
        return packed[layer, f].reshape(RING * group, width)

    def back_block(layer, f):
        return packed_back[layer, f].reshape(RING * group, width)

    def feed_chunk(layer, f, h):
        return packed[layer, f, h].reshape(chunk, width)

    def back_chunk(layer, f, h):
        return packed_back[layer, f, h].reshape(chunk, width)

    def grad_core(kind):
        return core_copy(C_GRAD + kind, grads.at[other, kind], grads_core.at[kind])

    lower, upper = pl.ds(0, rows), pl.ds(rows, rows)

    def grad_ring(kind, step):
        ahead = step in (0, 2, 4)
        part, cut = (
            (2, lower),
            (2, upper),
            (1, upper),
            (-1, lower),
            (1, lower),
            (-1, upper),
        )[step]
        return pltpu.make_async_remote_copy(
            src_ref=grads.at[core, kind, mod(shard + part), cut],
            dst_ref=grads_y.at[kind, step],
            send_sem=g_send.at[kind, step],
            recv_sem=g_recv.at[kind, step],
            device_id=y_device(1 if ahead else -1),
            device_id_type=MESH,
        )

    def sum_cores(kind):
        grad_core(kind).wait()

        def step(part, _):
            grads[core, kind, part] = (
                grads[core, kind, part].astype(F32) + grads_core[kind, part].astype(F32)
            ).astype(BF16)
            return 0

        lax.fori_loop(0, RING, step, 0)

    def start_ring(kind):
        for i in range(4):
            grad_ring(kind, i).start()

    def pass_grads(kind):
        for i, part, cut in ((0, 1, lower), (1, -1, upper)):
            grad_ring(kind, i).wait()
            at = mod(shard + part)
            grads[core, kind, at, cut] = (
                grads[core, kind, at, cut].astype(F32) + grads_y[kind, i].astype(F32)
            ).astype(BF16)
            grad_ring(kind, i + 4).start()

    def out_expert(layer, kind):
        return core_copy(
            C_OUT_EXPERT + 3 * layer + kind, out_stage.at[kind], expert_out.at[kind, core]
        )

    def out_local(kind):
        return pltpu.make_async_copy(
            out_stage.at[kind], expert_out.at[kind, core], out_sem.at[kind]
        )

    def finish_expert(layer, kind):
        for i in (2, 3, 4, 5):
            grad_ring(kind, i).wait()
        for cut, merged, direct in ((lower, 4, 3), (upper, 5, 2)):
            out_stage[kind, cut] = (
                grads[core, kind, shard, cut].astype(F32)
                + grads_y[kind, merged].astype(F32)
                + grads_y[kind, direct].astype(F32)
            )

        @pl.when(core == layer)
        def _():
            out_local(kind).start()

        @pl.when(core != layer)
        def _():
            out_expert(layer, kind).start()

    def wait_out(layer):
        for kind in range(3):
            @pl.when(core == layer)
            def _():
                out_local(kind).wait()

            @pl.when(core != layer)
            def _():
                out_expert(layer, kind).wait_send()

    def expert_grads(layer):
        for kind in range(3):
            def step(i, _):
                f, j = lax.div(i, 2), lax.rem(i, 2)
                cut = pl.ds(pl.multiple_of(j * 256, 256), 256)
                act = acts[kind, f, :, :, cut].reshape(2 * chunk, 256)
                rhs = back_block(layer, f) if kind == 2 else feed_block(layer, f)
                change = dot(act, rhs, TN).astype(BF16)
                grads[f, kind, 2 * j] = change[:128]
                grads[f, kind, 2 * j + 1] = change[128:]
                return 0

            lax.fori_loop(0, 4, step, 0)
            grad_core(kind).start()

    def proj_core_copy():
        return core_copy(C_PROJ, proj.at[other], proj_core)

    def proj_first(d, i):
        return pltpu.make_async_remote_copy(
            src_ref=proj.at[core, place_of(i, mod(p + d))],
            dst_ref=proj_recv.at[d - 1, i],
            send_sem=j_send.at[d - 1, i],
            recv_sem=j_recv.at[d - 1, i],
            device_id=p_device(d),
            device_id_type=MESH,
        )

    def proj_second(layer, d):
        return ring_copy(
            GRAD_Q + layer,
            d,
            proj_sum.at[mod(q + d)],
            proj_last.at[layer, d - 1],
            q_device(d),
        )

    def out_proj(layer):
        return core_copy(C_OUT_PROJ + layer, proj_stage, proj_out.at[core])

    def proj_one():
        proj_core_copy().wait()

        def step(i, _):
            proj[core, i] = (proj[core, i].astype(F32) + proj_core[i].astype(F32)).astype(BF16)
            return 0

        lax.fori_loop(0, RING * RING, step, 0)
        for i in range(RING):
            for d in (1, 3, 2):
                proj_first(d, i).start()

    def proj_two(layer):
        for i in range(RING):
            for d in (1, 3, 2):
                proj_first(d, i).wait()
            total = proj[core, place_of(i, p)].astype(F32)
            for d in (1, 2, 3):
                total = total + proj_recv[d - 1, i].astype(F32)
            proj_sum[i] = total.astype(BF16)
        for d in (1, 3, 2):
            proj_second(layer, d).start()

    def proj_three(layer):
        total = proj_sum[q].astype(F32)
        for d in (1, 3, 2):
            proj_second(layer, d).wait()
        for d in (1, 2, 3):
            total = total + proj_last[layer, d - 1].astype(F32)

        @pl.when(layer == core)
        def _():
            proj_out[core] = total

        @pl.when(layer != core)
        def _():
            proj_stage[...] = total
            out_proj(layer).start()

    def start_back(layer):
        for h, cut in enumerate(row_halves):
            change = total_of_partials(PARTIAL_BACK, partial_back, h)
            center = middle[layer, cut]
            scale = scale_of(center)
            normed = center * scale
            terms[layer, 1:2] += jnp.sum(change * normed, axis=0, keepdims=True)
            scaled = change * gains[layer, 1:2, :]
            inner = jnp.mean(scaled * normed, axis=-1, keepdims=True)
            back_mid = cotangent[cut] + scale * (scaled - normed * inner)
            cotangent[cut] = back_mid
            attn_back[layer, shard, cut] = back_mid.astype(BF16)
            start_gather(Y_GATHER_BACK, h, attn_back, layer)

    def find_probs(layer):
        low_qk[...] = normed_qk(layer)[0]
        key = low_qk[:, head_columns(2)]
        for i in range(4):
            query = one_half(low_qk[:, head_columns(i // 2)], i % 2)
            expo, share = exp_scores(query, key, mask_ref[...])
            parts[:, i * span : (i + 1) * span] = expo * share

    def change_at(block, columns):
        return slopes.at[0, lax.div(block, 2), lax.rem(block, 2), pl.ds(0, rows), columns]

    def attention_back(layer):
        key = low_qk[:, head_columns(2)]
        value = values[layer]
        back_key = jnp.zeros((span, 2 * HEAD), F32)
        back_value = jnp.zeros((span, 2 * HEAD), F32)
        for group_of in ((0, 1, 3, 2),):
            blocks = [mod(shard - d) for d in group_of]
            cuts = [block_rows(block) for block in blocks]
            for d in group_of:
                for h in range(len(row_halves)):
                    if d:
                        y_gather_copy(Y_GATHER_BACK, d, h, attn_back, layer).wait()
            back = jnp.concatenate([attn_back[layer, block] for block in blocks], axis=0)
            back = dot(back, weight_of(layer, 1, 2, 6)).astype(BF16)
            for tile in range(2):
                pieces = []
                queries = jnp.concatenate(
                    [low_qk[cut, head_columns(tile)] for cut in cuts], axis=0
                )
                for half in range(2):
                    i = 2 * tile + half
                    columns = slice(i * span, (i + 1) * span)
                    probs = jnp.concatenate([parts[cut, columns] for cut in cuts], axis=0)
                    query = one_half(queries, half)
                    piece = one_half(back[:, head_columns(tile)], half)
                    back_probs = dot(piece, value, NT)
                    back_value = back_value + dot(probs.astype(BF16), piece, TN)
                    total = jnp.sum(probs * back_probs, axis=-1, keepdims=True)
                    back_scores = (probs * (back_probs - total)).astype(BF16)
                    pieces.append(dot(back_scores, key))
                    back_key = back_key + dot(back_scores, query, TN)
                joined = jnp.where(low_half, pieces[0], pieces[1])
                for i, block in enumerate(blocks):
                    change_at(block, pl.ds(tile * 2 * HEAD, 2 * HEAD))[...] = joined[
                        i * rows : (i + 1) * rows
                    ]
        _low, normed, scale = normed_qk(layer)
        change = jnp.concatenate(
            [change_at(i, pl.ds(0, 4 * HEAD))[...] for i in range(RING)], axis=0
        )
        change = jnp.concatenate([change, back_key], axis=1) * HEAD ** (-0.5)
        term = jnp.sum(change * normed, axis=0, keepdims=True)
        terms[layer, 2:3, : 6 * HEAD] = term
        scaled = change * qk_gain(layer)
        inner = head_mean(scaled * normed)
        low_qk[...] = (scale * (scaled - normed * inner)).astype(BF16)
        back_v[...] = back_value.astype(BF16)
        for places, cut in zip(half_rows, column_halves):
            out = dot(low_qk[...], weight_of(layer, 0, 0, 6, places), NT)
            out = out + dot(back_v[...], weight_of(layer, 1, 0, 2, places), NT)
            for i in range(RING):
                y_send[i, :, cut] = out[i * rows : (i + 1) * rows].astype(BF16)
        y_scatter(Y_SUM_BACK)

    def proj_grads(layer):
        def step(i, _):
            cut = pl.ds(pl.multiple_of(i * 4 * rows, 4 * rows), 4 * rows)
            at = pl.ds(i * 4, 4)
            feed = attn_all[layer, :, :, cut].reshape(span, 4 * rows)
            back = attn_back[layer, :, :, cut].reshape(span, 4 * rows)
            for half, start, stop, lhs, rhs in (
                (0, 0, 6, feed, low_qk[...]),
                (1, 0, 2, feed, back_v[...]),
                (1, 2, 6, back, mixed[layer]),
            ):
                change = dot(lhs, rhs, TN).astype(BF16)
                proj[half, at, :, start * HEAD : stop * HEAD] = change.reshape(
                    4, rows, (stop - start) * HEAD
                )
            return 0

        lax.fori_loop(0, 4, step, 0)
        proj_core_copy().start()

    def finish_back(layer, take):
        for h, cut in enumerate(row_halves):
            total = y_total(Y_SUM_BACK, h)
            held = stream[layer, cut]
            scale = scale_of(held)
            normed = held * scale
            terms[layer, 0:1] += jnp.sum(total * normed, axis=0, keepdims=True)
            scaled = total * gains[layer, 0:1, :]
            inner = jnp.mean(scaled * normed, axis=-1, keepdims=True)
            take(h, cut, (cotangent[cut] + scale * (scaled - normed * inner)).astype(BF16))

    def slopes_of(gate_part, up_part):
        sigmoid = jax.nn.sigmoid(gate_part)
        silu = gate_part * sigmoid
        return up_part * sigmoid * (1.0 + gate_part * (1.0 - sigmoid)), silu

    def expert_back(layer, f, h, back_hidden, to_gate, to_up):
        back_gate = (back_hidden * to_gate).astype(BF16)
        back_up = (back_hidden * to_up).astype(BF16)
        acts[0, f, h] = back_gate
        acts[1, f, h] = back_up

        def columns(cut):
            return dot(back_gate, w_gate[layer, f, cut], NT) + dot(
                back_up, w_up[layer, f, cut], NT
            )

        put_result(RESULT_BACK, f, h, packed_send, result_back, columns)

    def put_forward(layer, f, h, inner):
        def columns(cut):
            return dot(inner, w_down[layer, f, :, cut])

        put_result(RESULT, f, h, result_send, result, columns)

    def gate_and_up(layer, f, h):
        block = feed_chunk(layer, f, h)
        return dot(block, w_gate[layer, f]), dot(block, w_up[layer, f])

    for h in range(len(row_halves)):
        start_attention(0, h)
    start_second(0)
    make_tables()
    for h, cut in enumerate(row_halves):
        spread_half(TOKENS_BACK, tokens_back, h, cotangent[cut].astype(BF16))
    start_pass(0)
    for copy in sent_weights():
        copy.start()
    wait_pass(0)
    attention(0)
    start_second(1)
    take_tables()
    wait_spread(TOKENS_BACK, tokens_back)
    pack(PACKED_BACK, 1, tokens_back, packed_back, True)
    finish_attention(0)
    start_pass(1)

    def packed_back_sent(f, h):
        for copy in packed_copies(PACKED_BACK, 1, f, h, packed_back):
            copy.wait_send()

    each_chunk(packed_back_sent)
    wait_expert_weights(0)
    wait_spread(TOKENS, tokens)
    pack(PACKED, 0, tokens, packed, False)

    def experts_forward(f, h):
        wait_all(packed_copies(PACKED, 0, f, h, packed))
        gate_part, up_part = gate_and_up(0, f, h)
        inner = (gate_part * jax.nn.sigmoid(gate_part) * up_part).astype(BF16)
        put_forward(0, f, h, inner)

    each_chunk(experts_forward)
    combine(RESULT, 0, result_send, result, True)
    start_partials(PARTIAL, partial)
    for h, cut in enumerate(row_halves):
        final = middle[0, cut] + total_of_partials(PARTIAL, partial, h)
        stream[1, cut] = final.astype(BF16).astype(F32)
        start_attention(1, h)

    wait_pass(1)
    wait_expert_weights(1)

    def hidden_back(f, h):
        for copy in packed_copies(PACKED_BACK, 1, f, h, packed_back):
            copy.wait_recv()
        slopes[0, f, h] = dot(back_chunk(1, f, h), w_down[1, f], NT)

    each_chunk(hidden_back)
    attention(1)
    finish_attention(1)
    wait_spread(TOKENS, tokens)
    pack(PACKED, 1, tokens, packed, False)

    def experts_both(f, h):
        wait_all(packed_copies(PACKED, 1, f, h, packed))
        gate_part, up_part = gate_and_up(1, f, h)
        to_gate, to_up = slopes_of(gate_part, up_part)
        acts[2, f, h] = (to_up * up_part).astype(BF16)
        expert_back(1, f, h, slopes[0, f, h], to_gate, to_up)

    each_chunk(experts_both)
    each_chunk(lambda f, h: put_forward(1, f, h, acts[2, f, h]))
    expert_grads(1)
    combine(RESULT_BACK, 1, packed_send, result_back, False)
    start_partials(PARTIAL_BACK, partial_back)
    sum_cores(0)
    start_ring(0)

    start_back(1)
    combine(RESULT, 1, result_send, result, True)
    start_partials(PARTIAL, partial)
    sum_cores(1)
    find_probs(1)
    pass_grads(0)
    attention_back(1)
    proj_grads(1)
    for h, cut in enumerate(row_halves):
        final = middle[1, cut] + total_of_partials(PARTIAL, partial, h)
        ends_stage[0, cut] = final.astype(BF16)
    sum_cores(2)
    pl.semaphore_signal(credit, inc=1, device_id=core_device, device_id_type=MESH)

    def hand_on(h, cut, block):
        cotangent[cut] = block.astype(F32)
        spread_half(TOKENS_BACK, tokens_back, h, block)

    finish_back(1, hand_on)

    start_ring(1)
    start_ring(2)
    proj_one()

    def find_slopes(f, h):
        gate_part, up_part = gate_and_up(0, f, h)
        to_gate, to_up = slopes_of(gate_part, up_part)
        slopes[0, f, h] = to_gate
        slopes[1, f, h] = to_up
        acts[2, f, h] = (to_up * up_part).astype(BF16)

    each_chunk(find_slopes)
    wait_spread(TOKENS_BACK, tokens_back)
    pack(PACKED_BACK, 0, tokens_back, packed_back, True)
    pass_grads(1)
    pass_grads(2)
    proj_two(1)

    def experts_back(f, h):
        wait_all(packed_copies(PACKED_BACK, 0, f, h, packed_back))
        back_hidden = dot(back_chunk(0, f, h), w_down[0, f], NT)
        expert_back(0, f, h, back_hidden, slopes[0, f, h], slopes[1, f, h])

    each_chunk(experts_back)
    for kind in range(3):
        finish_expert(1, kind)
    for d in (1, -1):
        pl.semaphore_signal(y_credit, inc=1, device_id=y_device(d), device_id_type=MESH)
    pl.semaphore_wait(credit, 1)
    expert_grads(0)
    proj_three(1)
    combine(RESULT_BACK, 0, packed_send, result_back, False)
    start_partials(PARTIAL_BACK, partial_back)
    pl.semaphore_wait(y_credit, 2)
    sum_cores(0)
    start_ring(0)
    start_back(0)
    sum_cores(1)
    find_probs(0)
    pass_grads(0)
    attention_back(0)
    start_ring(1)

    @pl.when(core != 1)
    def _():
        out_proj(1).wait_send()

    proj_grads(0)
    sum_cores(2)
    start_ring(2)

    def keep(h, cut, block):
        ends_stage[1, cut] = block

    finish_back(0, keep)

    ends_out[core] = jnp.where(first, ends_stage[1], ends_stage[0])
    ends_copy_out = core_copy(C_OUT_ENDS, ends_stage.at[core], ends_out.at[core])
    ends_copy_out.start()
    term_copy = core_copy(C_TERM, terms.at[other], terms_core)
    term_copy.start()
    wait_out(1)
    proj_one()
    term_copy.wait()
    terms_recv[0, 0] = terms[core] + terms_core[...]
    for axis, (row, device) in enumerate(
        ((GAIN_P, p_device), (GAIN_Q, q_device), (GAIN_Y, y_device))
    ):
        copies = [
            ring_copy(
                row, d, terms_recv.at[axis, 0], terms_recv.at[axis, d], device(d)
            )
            for d in (1, 3, 2)
        ]
        for copy in copies:
            copy.start()
        if axis == 0:
            pass_grads(1)
            proj_two(0)
        if axis == 1:
            pass_grads(2)
            proj_three(0)
            finish_expert(0, 0)
        if axis == 2:
            finish_expert(0, 1)
        wait_all(copies)
        total = terms_recv[axis, 0]
        for d in (1, 2, 3):
            total = total + terms_recv[axis, d]
        if axis < 2:
            terms_recv[axis + 1, 0] = total
        else:
            gains_out[...] = total

    finish_expert(0, 2)
    wait_out(0)
    for layer in range(2):
        @pl.when(core == layer)
        def _():
            for kind in range(3):
                out_expert(layer, kind).wait_recv()
            out_proj(layer).wait_recv()

    @pl.when(core != 0)
    def _():
        out_proj(0).wait_send()

    ends_copy_out.wait()
    for copy in (piece_copy, ends_copy, gains_copy, routes_copy, gates_copy):
        copy.wait_send()
    for copy in sent_weights():
        copy.wait_send()
    for layer in range(2):
        for d in range(RING):
            for i in range(RING):
                weight_pass(layer, d, i).wait_send()
        for d in (1, 2, 3):
            weight_first(layer, d).wait_send()
            for i in range(RING):
                weight_second(layer, d, i).wait_send()
    for d in (1, 2, 3):
        ring_copy(
            TABLE_P, d, table_send.at[d], table_recv.at[d - 1], p_device(d)
        ).wait_send()


def finish(
    ends_ref,
    gains_ref,
    proj_ref,
    experts_ref,
    ends_out,
    attn_gain_out,
    query_gain_out,
    key_gain_out,
    feed_gain_out,
    query_out,
    key_out,
    value_out,
    out_out,
    gate_out,
    up_out,
    down_out,
    ends,
    gains,
    proj,
    experts,
    turned,
    sems,
):
    pieces = [(kind, f) for kind in range(3) for f in range(2)]
    moves = [
        pltpu.make_async_copy(
            experts_ref.at[kind, f], experts.at[kind, f], sems.at[2 * kind + f]
        )
        for kind, f in pieces
    ]
    moves += [
        pltpu.make_async_copy(ends_ref, ends, sems.at[6]),
        pltpu.make_async_copy(gains_ref, gains, sems.at[7]),
        pltpu.make_async_copy(proj_ref, proj, sems.at[8]),
    ]
    for move in moves:
        move.start()
    results = []
    for i, (kind, f) in enumerate(pieces):
        moves[i].wait()
        if kind < 2:
            turned[kind, f] = experts[kind, f].T
        source = experts.at[kind, f] if kind == 2 else turned.at[kind, f]
        target = (gate_out, up_out, down_out)[kind]
        results.append(pltpu.make_async_copy(source, target.at[0, f], sems.at[9 + i]))
        results[-1].start()
    moves[6].wait()
    results.append(pltpu.make_async_copy(ends, ends_out.at[0], sems.at[15]))
    results[-1].start()
    moves[7].wait()
    attn_gain_out[...] = gains[0:1]
    feed_gain_out[...] = gains[1:2]
    query_gain_out[...] = exact_dot(gains[2:3, : 4 * HEAD], copies_of_head(4), NT)
    key_gain_out[...] = exact_dot(gains[2:3, 4 * HEAD : 6 * HEAD], copies_of_head(2), NT)
    moves[8].wait()
    swap = swap_heads()
    query_out[0] = exact_dot(proj[0, :, : 4 * HEAD], swap)
    key_out[0] = proj[0, :, 4 * HEAD :]
    value_out[0] = proj[1, :, : 2 * HEAD]
    out_out[0] = exact_dot(proj[1, :, 2 * HEAD :], swap)
    for result in results:
        result.wait()


def shards(
    ends_in,
    segments,
    routes,
    gates,
    attn_gain,
    query_gain,
    key_gain,
    feed_gain,
    w_query,
    key_weight,
    value_weight,
    w_out,
    w_gate,
    w_up,
    w_down,
):
    rows = ends_in.shape[2]
    width = ends_in.shape[3]
    top = routes.shape[3]
    hidden = w_gate.shape[3]
    experts_all = w_gate.shape[1] * lax.axis_size("expert")
    capacity = 3 * rows * top // (2 * experts_all)
    group = RING * capacity
    part_rows = group // 2
    chunk = RING * part_rows
    span = RING * rows
    vmem = pl.BlockSpec(memory_space=pltpu.VMEM)
    anywhere = pl.BlockSpec(memory_space=pl.ANY)
    half = 6 * HEAD
    everyone = RING * RING
    scratch = [
        pltpu.VMEM((2, 2, width, hidden), BF16),
        pltpu.VMEM((2, 2, width, hidden), BF16),
        pltpu.VMEM((2, 2, hidden, width), BF16),
        pltpu.VMEM((2, 2, everyone, rows, half), BF16),
        pltpu.VMEM((rows, width), BF16),
        pltpu.VMEM((2, 8, width), F32),
        pltpu.VMEM((2, top, rows), jnp.int32),
        pltpu.VMEM((2, top, rows), F32),
        pltpu.VMEM((span, span), F32),
        pltpu.VMEM((2, rows, half), BF16),
        pltpu.VMEM((8, width), F32),
        pltpu.VMEM((RING, 2, 2, 8, span), F32),
        pltpu.VMEM((RING - 1, 2, 2, 8, span), F32),
        pltpu.VMEM((2, 8, 1, span), F32),
        pltpu.VMEM((2, 8, 1, span), F32),
        pltpu.VMEM((2, rows, width), F32),
        pltpu.VMEM((2, rows, width), F32),
        pltpu.VMEM((rows, width), F32),
        pltpu.VMEM((2, RING, rows, width), BF16),
        pltpu.VMEM((2, span, half), F32),
        pltpu.VMEM((2, span, 2 * HEAD), BF16),
        pltpu.VMEM((2, span, 4 * HEAD), BF16),
        pltpu.VMEM((RING, rows, width), BF16),
        pltpu.VMEM((RING - 1, rows, width), BF16),
        pltpu.VMEM((RING, rows, width), BF16),
        pltpu.VMEM((RING, rows, width), BF16),
        pltpu.VMEM((2, 2, RING - 1, group // 2, width), BF16),
        pltpu.VMEM((2, 2, 2, RING, group // 2, width), BF16),
        pltpu.VMEM((2, 2, 2, RING, group // 2, width), BF16),
        pltpu.VMEM((2, 2, RING - 1, group // 2, width), BF16),
        pltpu.VMEM((2, 2, RING, group // 2, width), BF16),
        pltpu.VMEM((2, 2, RING, group // 2, width), BF16),
        pltpu.VMEM((RING, rows, width), BF16),
        pltpu.VMEM((RING - 1, rows, width), BF16),
        pltpu.VMEM((RING - 1, rows, width), BF16),
        pltpu.VMEM((span, width), F32),
        pltpu.VMEM((2, 2, 2, 2 * group, hidden), F32),
        pltpu.VMEM((2, RING, rows, width), BF16),
        pltpu.VMEM((span, half), BF16),
        pltpu.VMEM((span, 2 * HEAD), BF16),
        pltpu.VMEM((3, 2, 2, 2 * group, hidden), BF16),
        pltpu.VMEM((2, 3, RING, hidden // RING, width), BF16),
        pltpu.VMEM((3, RING, hidden // RING, width), BF16),
        pltpu.VMEM((3, 6, rows, width), BF16),
        pltpu.VMEM((3, hidden // RING, width), F32),
        pltpu.VMEM((2, everyone, rows, half), BF16),
        pltpu.VMEM((everyone, rows, half), BF16),
        pltpu.VMEM((RING - 1, RING, rows, half), BF16),
        pltpu.VMEM((RING, rows, half), BF16),
        pltpu.VMEM((2, RING - 1, rows, half), BF16),
        pltpu.VMEM((rows, half), F32),
        pltpu.VMEM((2, 8, width), F32),
        pltpu.VMEM((8, width), F32),
        pltpu.VMEM((3, RING, 8, width), F32),
        pltpu.VMEM((2, rows, width), BF16),
        pltpu.SemaphoreType.DMA((RING_ROWS, RING - 1)),
        pltpu.SemaphoreType.DMA((RING_ROWS, RING - 1)),
        pltpu.SemaphoreType.DMA((2, RING - 1, RING)),
        pltpu.SemaphoreType.DMA((2, RING - 1, RING)),
        pltpu.SemaphoreType.DMA((2, RING, RING)),
        pltpu.SemaphoreType.DMA((2, RING, RING)),
        pltpu.SemaphoreType.DMA((RING - 1, RING)),
        pltpu.SemaphoreType.DMA((RING - 1, RING)),
        pltpu.SemaphoreType.DMA((3, 6)),
        pltpu.SemaphoreType.DMA((3, 6)),
        pltpu.SemaphoreType.DMA((CORE_ROWS,)),
        pltpu.SemaphoreType.DMA((CORE_ROWS,)),
        pltpu.SemaphoreType.DMA((3,)),
        pltpu.SemaphoreType.DMA((3,)),
        pltpu.SemaphoreType.REGULAR,
        pltpu.SemaphoreType.REGULAR,
    ]
    ends, gain_sums, proj, experts = pl.pallas_call(
        functools.partial(kernel, rows, width, hidden, capacity),
        out_shape=(
            jax.ShapeDtypeStruct((2, rows, width), BF16),
            jax.ShapeDtypeStruct((8, width), F32),
            jax.ShapeDtypeStruct((2, rows, half), F32),
            jax.ShapeDtypeStruct((3, 2, hidden // RING, width), F32),
        ),
        in_specs=[vmem] * 12 + [anywhere] * 3,
        out_specs=(vmem, vmem, vmem, anywhere),
        scratch_shapes=scratch,
        compiler_params=pltpu.CompilerParams(
            collective_id=0, has_side_effects=True, vmem_limit_bytes=63 << 20
        ),
        cost_estimate=pl.CostEstimate(
            flops=60_000_000_000, bytes_accessed=20_000_000, transcendentals=4_000_000
        ),
        name="layers",
    )(
        ends_in[0],
        segments,
        routes[0].transpose(0, 2, 1),
        gates[0].transpose(0, 2, 1),
        attn_gain,
        query_gain,
        key_gain,
        feed_gain,
        w_query[0],
        key_weight[0],
        value_weight[0],
        w_out[0].T,
        w_gate[0],
        w_up[0],
        w_down[0],
    )
    shapes = (
        ((1, 2, rows, width), BF16),
        ((1, width), F32),
        ((1, HEAD), F32),
        ((1, HEAD), F32),
        ((1, width), F32),
        ((1,) + w_query.shape[1:], F32),
        ((1,) + key_weight.shape[1:], F32),
        ((1,) + value_weight.shape[1:], F32),
        ((1, w_out.shape[2], w_out.shape[1]), F32),
        ((1, 2, width, hidden // RING), F32),
        ((1, 2, width, hidden // RING), F32),
        ((1, 2, hidden // RING, width), F32),
    )
    outputs = pl.pallas_call(
        finish,
        out_shape=tuple(jax.ShapeDtypeStruct(shape, dtype) for shape, dtype in shapes),
        in_specs=[anywhere] * 4,
        out_specs=(anywhere,) + (vmem,) * 8 + (anywhere,) * 3,
        scratch_shapes=[
            pltpu.VMEM((2, rows, width), BF16),
            pltpu.VMEM((8, width), F32),
            pltpu.VMEM((2, rows, half), F32),
            pltpu.VMEM((3, 2, hidden // RING, width), F32),
            pltpu.VMEM((2, 2, width, hidden // RING), F32),
            pltpu.SemaphoreType.DMA((16,)),
        ],
        compiler_params=pltpu.CompilerParams(vmem_limit_bytes=60 << 20),
        name="finish",
    )(ends, gain_sums, proj, experts)
    return (*outputs[:8], outputs[8].transpose(0, 2, 1), *outputs[9:])


def solution(mesh):
    return jax.shard_map(
        shards,
        mesh=mesh,
        in_specs=(
            P("section", None, ("expert", "shard"), None),
            P(None, "expert"),
            P("section", None, ("expert", "shard"), None),
            P("section", None, ("expert", "shard"), None),
            P("section", None),
            P("section", None),
            P("section", None),
            P("section", None),
            P("section", "expert", "shard"),
            P("section", "expert", "shard"),
            P("section", "expert", "shard"),
            P("section", "shard", "expert"),
            P("section", "expert", None, None),
            P("section", "expert", None, None),
            P("section", "expert", None, None),
        ),
        out_specs=(
            P("section", None, ("expert", "shard"), None),
            P("section", None),
            P("section", None),
            P("section", None),
            P("section", None),
            P("section", "expert", "shard"),
            P("section", "expert", "shard"),
            P("section", "expert", "shard"),
            P("section", "shard", "expert"),
            P("section", "expert", None, "shard"),
            P("section", "expert", None, "shard"),
            P("section", "expert", "shard", None),
        ),
        check_vma=False,
    )
```

```python
import functools

import jax
import jax.numpy as jnp
from jax import lax
from jax.experimental import pallas as pl
from jax.experimental.pallas import tpu as pltpu
from jax.sharding import PartitionSpec as P

EPS = 1e-06
NEG = -1e30
HEAD = 64
RING = 4
MESH = pl.DeviceIdType.MESH
F32 = jnp.float32
BF16 = jnp.bfloat16

NN = (((1,), (0,)), ((), ()))
NT = (((1,), (1,)), ((), ()))
TN = (((0,), (0,)), ((), ()))

PIECES = 4
Y_GATHER, Y_SUM, Y_GATHER_BACK, Y_SUM_BACK = 0, 4, 8, 12
TOKENS, TOKENS_BACK, PARTIAL, PARTIAL_BACK = 16, 20, 24, 28
GRAD_Q, GAIN_P, GAIN_Q, GAIN_Y, WEIGHT_P, TABLE_P = 32, 34, 35, 36, 37, 39
PACKED, PACKED_BACK, RESULT, RESULT_BACK, RING_ROWS = 40, 44, 48, 52, 56

C_ENDS, C_GAINS, C_ROUTES, C_GATES, C_PIECE = range(5)
C_GATE, C_UP, C_DOWN, C_GRAD, C_PROJ, C_TERM, C_OUT_ENDS = 5, 6, 7, 8, 11, 12, 13
C_OUT_EXPERT, C_OUT_PROJ, CORE_ROWS = 14, 20, 22


def dot(a, b, form=NN):
    return lax.dot_general(a, b, form, preferred_element_type=F32)


def exact_dot(a, b, form=NN):
    return lax.dot_general(
        a, b, form, preferred_element_type=F32, precision=lax.Precision.HIGHEST
    )


def iota(shape, dimension):
    return lax.broadcasted_iota(jnp.int32, shape, dimension)


def swap_heads():
    size = 4 * HEAD
    row, col = iota((size, size), 0), iota((size, size), 1)
    head = lax.div(row, HEAD)
    shift = jnp.where(head == 1, HEAD, jnp.where(head == 2, -HEAD, 0))
    return (col == row + shift).astype(F32)


def copies_of_head(count):
    shape = (HEAD, count * HEAD)
    return (lax.rem(iota(shape, 1), HEAD) == iota(shape, 0)).astype(F32)


def scale_of(rows):
    return lax.rsqrt(jnp.mean(rows * rows, axis=-1, keepdims=True) + EPS)


def kernel(
    rows,
    width,
    hidden,
    capacity,
    ends_ref,
    segments_ref,
    routes_ref,
    gates_ref,
    attn_gain_ref,
    query_gain_ref,
    key_gain_ref,
    feed_gain_ref,
    query_ref,
    key_ref,
    value_ref,
    out_ref,
    gate_ref,
    up_ref,
    down_ref,
    ends_out,
    gains_out,
    proj_out,
    expert_out,
    w_gate,
    w_up,
    w_down,
    w_attn,
    ends_in,
    gains,
    routes,
    gates,
    mask_ref,
    piece_ref,
    gains_ref,
    table_send,
    table_recv,
    slots,
    weights,
    stream,
    middle,
    cotangent,
    attn_all,
    raw_qk,
    values,
    mixed,
    y_send,
    y_recv,
    tokens,
    tokens_back,
    packed_send,
    packed,
    packed_back,
    result_send,
    result,
    result_back,
    partial_send,
    partial,
    partial_back,
    parts,
    slopes,
    attn_back,
    low_qk,
    back_v,
    acts,
    grads,
    grads_core,
    grads_y,
    out_stage,
    proj,
    proj_core,
    proj_recv,
    proj_sum,
    proj_last,
    proj_stage,
    terms,
    terms_core,
    terms_recv,
    ends_stage,
    send_sem,
    recv_sem,
    w_send,
    w_recv,
    h_send,
    h_recv,
    j_send,
    j_recv,
    g_send,
    g_recv,
    c_send,
    c_recv,
    local_sem,
    out_sem,
    credit,
    y_credit,
):
    core = lax.axis_index("section")
    place = lax.axis_index("expert")
    shard = lax.axis_index("shard")
    x = lax.rem(place, RING)
    z = lax.div(place, RING)
    p = x + core * (z - x)
    q = z + core * (x - z)
    span = RING * rows
    group = RING * capacity
    part_rows = group // 2
    chunk = RING * part_rows
    other = 1 - core

    def mod(value):
        return lax.rem(value + 2 * RING, RING)

    def place_of(second, first):
        return (1 - core) * (second * RING + first) + core * (first * RING + second)

    def y_device(d):
        return (core, place, mod(shard + d))

    def p_device(d):
        return (core, place_of(q, mod(p + d)), shard)

    def q_device(d):
        return (core, place_of(mod(q + d), p), shard)

    core_device = (other, place, shard)

    def order(k):
        return k + lax.div(k, 2) * (5 - 2 * k)

    def ring_copy(row, d, src, dst, device):
        return pltpu.make_async_remote_copy(
            src_ref=src,
            dst_ref=dst,
            send_sem=send_sem.at[row, d - 1],
            recv_sem=recv_sem.at[row, d - 1],
            device_id=device,
            device_id_type=MESH,
        )

    def core_copy(row, src, dst):
        return pltpu.make_async_remote_copy(
            src_ref=src,
            dst_ref=dst,
            send_sem=c_send.at[row],
            recv_sem=c_recv.at[row],
            device_id=core_device,
            device_id_type=MESH,
        )

    barrier = pltpu.get_barrier_semaphore()
    for d in (1, 2, 3):
        for device in (y_device(d), p_device(d), q_device(d)):
            pl.semaphore_signal(barrier, inc=1, device_id=device, device_id_type=MESH)
    pl.semaphore_signal(barrier, inc=1, device_id=core_device, device_id_type=MESH)

    def local_weights():
        return (
            pltpu.make_async_copy(gate_ref, w_gate.at[core], local_sem.at[0]),
            pltpu.make_async_copy(up_ref, w_up.at[core], local_sem.at[1]),
            pltpu.make_async_copy(down_ref, w_down.at[core], local_sem.at[2]),
        )

    swap = swap_heads().astype(BF16)
    piece_ref[0, :, : 4 * HEAD] = dot(query_ref[...], swap).astype(BF16)
    piece_ref[0, :, 4 * HEAD :] = key_ref[...]
    piece_ref[1, :, : 2 * HEAD] = value_ref[...]
    piece_ref[1, :, 2 * HEAD :] = dot(out_ref[...], swap).astype(BF16)
    gains_ref[0:1] = attn_gain_ref[...]
    gains_ref[1:2] = feed_gain_ref[...]
    gains_ref[2:3, : 4 * HEAD] = exact_dot(query_gain_ref[...], copies_of_head(4))
    gains_ref[2:3, 4 * HEAD : 6 * HEAD] = exact_dot(key_gain_ref[...], copies_of_head(2))
    w_attn[core, core, place] = piece_ref[core]
    gains[core] = gains_ref[...]
    routes[core] = routes_ref[core]
    gates[core] = gates_ref[core]
    across = jnp.broadcast_to(
        jnp.where(core == 0, segments_ref[0:1], segments_ref[1:2]), (span, span)
    ).astype(F32)
    causal = iota((span, span), 0) >= iota((span, span), 1)
    mask_ref[...] = (causal & (across == across.T)).astype(F32)
    terms[...] = jnp.zeros_like(terms)
    for copy in local_weights():
        copy.start()

    pl.semaphore_wait(barrier, 10)
    piece_copy = core_copy(C_PIECE, piece_ref.at[other], w_attn.at[core, other, place])
    ends_copy = core_copy(C_ENDS, ends_ref.at[other], ends_in)
    gains_copy = core_copy(C_GAINS, gains_ref, gains.at[core])
    routes_copy = core_copy(C_ROUTES, routes_ref.at[other], routes.at[core])
    gates_copy = core_copy(C_GATES, gates_ref.at[other], gates.at[core])
    for copy in (piece_copy, ends_copy, gains_copy, routes_copy, gates_copy):
        copy.start()

    def sent_weights():
        return (
            core_copy(C_GATE, gate_ref, w_gate.at[core]),
            core_copy(C_UP, up_ref, w_up.at[core]),
            core_copy(C_DOWN, down_ref, w_down.at[core]),
        )

    def weight_first(layer, d):
        return pltpu.make_async_remote_copy(
            src_ref=w_attn.at[layer, core, place],
            dst_ref=w_attn.at[layer, core, place],
            send_sem=send_sem.at[WEIGHT_P + layer, d - 1],
            recv_sem=recv_sem.at[WEIGHT_P + layer, d - 1],
            device_id=p_device(d),
            device_id_type=MESH,
        )

    def weight_second(layer, d, i):
        held = place_of(q, mod(p - i))
        return pltpu.make_async_remote_copy(
            src_ref=w_attn.at[layer, core, held],
            dst_ref=w_attn.at[layer, core, held],
            send_sem=w_send.at[layer, d - 1, i],
            recv_sem=w_recv.at[layer, d - 1, i],
            device_id=q_device(d),
            device_id_type=MESH,
        )

    def weight_pass(layer, d, i):
        held = place_of(mod(q - d), mod(p - i))
        return pltpu.make_async_remote_copy(
            src_ref=w_attn.at[layer, core, held],
            dst_ref=w_attn.at[layer, core, held],
            send_sem=h_send.at[layer, d, i],
            recv_sem=h_recv.at[layer, d, i],
            device_id=core_device,
            device_id_type=MESH,
        )

    def start_first(layer):
        for d in (2, 1, 3):
            weight_first(layer, d).start()

    def start_second(layer):
        for i in (0, 1, 3, 2):
            if i:
                weight_first(layer, i).wait_recv()
            for d in (2, 1, 3):
                weight_second(layer, d, i).start()
            weight_pass(layer, 0, i).start()

    def start_pass(layer):
        for i in (0, 1, 3, 2):
            for d in (2, 1, 3):
                weight_second(layer, d, i).wait_recv()
                weight_pass(layer, d, i).start()

    def wait_pass(layer):
        for d in range(RING):
            for i in range(RING):
                weight_pass(layer, d, i).wait_recv()

    piece_copy.wait_recv()
    start_first(0)
    start_first(1)
    ends_copy.wait_recv()
    gains_copy.wait_recv()
    first = core == 0
    stream[0] = jnp.where(first, ends_ref[0], ends_in[...]).astype(F32)
    cotangent[...] = jnp.where(first, ends_in[...], ends_ref[1]).astype(F32)

    def make_tables():
        routes_copy.wait_recv()
        gates_copy.wait_recv()
        tiles = 32
        names = iota((tiles, rows), 0)
        ahead = (iota((rows, rows), 0) < iota((rows, rows), 1)).astype(BF16)
        spread = (iota((rows, span), 1) == iota((rows, span), 0) + rows * p).astype(F32)
        row_at = lax.broadcasted_iota(jnp.int32, (2 * RING, tiles), 0)
        col_at = lax.broadcasted_iota(jnp.int32, (2 * RING, tiles), 1)
        for layer in range(2):
            named = jnp.zeros((tiles, rows), F32)
            gate = jnp.zeros((tiles, rows), F32)
            for j in range(routes.shape[1]):
                hit = (routes[layer, j : j + 1, :] == names).astype(F32)
                named = named + hit
                gate = gate + hit * gates[layer, j : j + 1, :]
            rank = dot(named.astype(BF16), ahead)
            slot = named * (rank + (1 + capacity * p).astype(F32))
            wide_slot = exact_dot(slot, spread)
            wide_gate = exact_dot(gate, spread)
            for d in range(RING):
                first_axis = mod(p + d)
                owner = place_of(lax.div(row_at, 2), first_axis)
                choose = (col_at == 2 * owner + lax.rem(row_at, 2)).astype(F32)
                table_send[d, layer, 0] = exact_dot(choose, wide_slot)
                table_send[d, layer, 1] = exact_dot(choose, wide_gate)
        for d in (2, 1, 3):
            ring_copy(
                TABLE_P, d, table_send.at[d], table_recv.at[d - 1], p_device(d)
            ).start()

    def take_tables():
        for d in (2, 1, 3):
            ring_copy(
                TABLE_P, d, table_send.at[d], table_recv.at[d - 1], p_device(d)
            ).wait_recv()
        for layer in range(2):
            for kind, target in ((0, slots), (1, weights)):
                whole = table_send[0, layer, kind]
                for d in (1, 2, 3):
                    whole = whole + table_recv[d - 1, layer, kind]
                for r in range(2 * RING):
                    target[layer, r] = whole[r : r + 1, :]

    def choose_rows(layer, second, f, h):
        at = iota((part_rows, span), 0) + (1 + part_rows * h)
        return at.astype(F32) == slots[layer, 2 * second + f]

    lanes = lax.broadcasted_iota(jnp.int32, (1, 2 * HEAD), 1)
    low_half = lanes < HEAD
    halves = (low_half, lanes >= HEAD)

    def head_mean(block):
        at_row = lax.broadcasted_iota(jnp.int32, (2 * HEAD, 2 * HEAD), 0) >= HEAD
        at_col = lax.broadcasted_iota(jnp.int32, (2 * HEAD, 2 * HEAD), 1) >= HEAD
        share = jnp.where(at_row == at_col, 1.0 / HEAD, 0.0).astype(F32)
        tiles = [
            exact_dot(block[:, i : i + 2 * HEAD], share)
            for i in range(0, block.shape[1], 2 * HEAD)
        ]
        return jnp.concatenate(tiles, axis=1)

    def qk_gain(layer):
        return gains[layer, 2:3, : 6 * HEAD]

    def normed_qk(layer):
        raw = raw_qk[layer]
        scale = lax.rsqrt(head_mean(raw * raw) + EPS)
        normed = raw * scale
        low = (normed * qk_gain(layer)).astype(BF16)
        return low, normed, scale

    def head_columns(tile):
        return slice(tile * 2 * HEAD, (tile + 1) * 2 * HEAD)

    def block_rows(block):
        return pl.ds(pl.multiple_of(block * rows, rows), rows)

    def one_half(block, half):
        return jnp.where(halves[half], block, jnp.zeros_like(block))

    def exp_scores(query, key, mask):
        scores = dot(query, key, NT) * HEAD ** (-0.5)
        expo = jnp.exp(jnp.where(mask != 0.0, scores, NEG))
        return expo, 1.0 / jnp.sum(expo, axis=-1, keepdims=True)

    half_rows = (slice(0, 8), slice(8, 16))

    def weight_of(layer, half, start, stop, places=slice(0, 16)):
        block = w_attn[layer, half, places, :, start * HEAD : stop * HEAD]
        return block.reshape(block.shape[0] * rows, (stop - start) * HEAD)

    row_halves = tuple(pl.ds(i * rows // PIECES, rows // PIECES) for i in range(PIECES))

    def y_gather_copy(row, d, h, buffer, layer):
        held = buffer.at[layer, shard, row_halves[h]]
        return ring_copy(row + h, d, held, held, y_device(d))

    def start_gather(row, h, buffer, layer):
        for d in (2, 1, 3):
            y_gather_copy(row, d, h, buffer, layer).start()

    def y_scatter_copy(row, d, h):
        cut = row_halves[h]
        return ring_copy(
            row + h, d, y_send.at[mod(shard + d), cut], y_recv.at[d - 1, cut], y_device(d)
        )

    def y_scatter(row):
        for h in range(len(row_halves)):
            for d in (2, 1, 3):
                y_scatter_copy(row, d, h).start()

    def y_total(row, h):
        cut = row_halves[h]
        for d in (2, 1, 3):
            y_scatter_copy(row, d, h).wait()
        total = y_send[shard, cut].astype(F32)
        for d in (1, 2, 3):
            total = total + y_recv[d - 1, cut].astype(F32)
        return total

    def spread_copy(row, buffer, d, h):
        held = buffer.at[p, row_halves[h]]
        return ring_copy(row + h, d, held, held, p_device(d))

    def spread_half(row, buffer, h, block):
        buffer[p, row_halves[h]] = block
        for d in (2, 1, 3):
            spread_copy(row, buffer, d, h).start()

    def wait_spread(row, buffer):
        for h in range(len(row_halves)):
            for d in (2, 1, 3):
                spread_copy(row, buffer, d, h).wait()

    column_halves = (pl.ds(0, width // 2), pl.ds(width // 2, width // 2))

    def packed_copies(row, layer, f, h, target):
        return [
            ring_copy(
                row + 2 * f + h,
                d,
                packed_send.at[f, h, d - 1],
                target.at[layer, f, h, d],
                q_device(d),
            )
            for d in (2, 1, 3)
        ]

    def choose_all(layer, f, h):
        return jnp.concatenate(
            [choose_rows(layer, mod(q + d), f, h) for d in range(RING)], axis=0
        )

    def gates_all(layer, f):
        return jnp.concatenate(
            [
                jnp.broadcast_to(weights[layer, 2 * mod(q + d) + f], (part_rows, span))
                for d in range(RING)
            ],
            axis=0,
        )

    def each_chunk(step):
        def body(i, _):
            step(lax.div(i, 2), lax.rem(i, 2))
            return 0

        lax.fori_loop(0, 4, body, 0)

    def pack(row, layer, source, target, gated):
        def step(f, h):
            chosen = choose_all(layer, f, h)
            low = chosen.astype(BF16)
            if gated:
                share = jnp.sum(
                    jnp.where(chosen, gates_all(layer, f), 0.0), axis=1, keepdims=True
                )
            for cut in column_halves:
                block = dot(low, source[:, :, cut].reshape(span, width // 2))
                if gated:
                    block = block * share
                block = block.astype(BF16)
                for d in (2, 1, 3):
                    packed_send[f, h, d - 1, :, cut] = block[
                        d * part_rows : (d + 1) * part_rows
                    ]
                target[layer, f, h, 0, :, cut] = block[:part_rows]
            for copy in packed_copies(row, layer, f, h, target):
                copy.start()

        each_chunk(step)

    def result_copies(row, f, h, send, target):
        return [
            ring_copy(
                row + 2 * f + h,
                d,
                send.at[f, h, d - 1],
                target.at[f, h, d],
                q_device(-d),
            )
            for d in (2, 1, 3)
        ]

    def put_result(row, f, h, send, target, columns):
        for cut in column_halves:
            block = columns(cut).astype(BF16)
            for d in (2, 1, 3):
                send[f, h, d - 1, :, cut] = block[d * part_rows : (d + 1) * part_rows]
            target[f, h, 0, :, cut] = block[:part_rows]
        for copy in result_copies(row, f, h, send, target):
            copy.start()

    def combine(row, layer, send, target, gated):
        parts[...] = jnp.zeros_like(parts)

        def step(f, h):
            chosen = choose_all(layer, f, h)
            if gated:
                share = jnp.where(chosen, gates_all(layer, f), 0.0)
            else:
                share = chosen.astype(F32)
            share = share.astype(BF16)
            wait_all(result_copies(row, f, h, send, target))
            for cut in column_halves:
                parts[:, cut] += dot(
                    share, target[f, h, :, :, cut].reshape(chunk, width // 2), TN
                )

        each_chunk(step)
        for i in range(RING):
            partial_send[i] = parts[i * rows : (i + 1) * rows].astype(BF16)

    def partial_copy(row, target, d, h):
        cut = row_halves[h]
        return ring_copy(
            row + h, d, partial_send.at[mod(p + d), cut], target.at[d - 1, cut], p_device(d)
        )

    def start_partials(row, target):
        for h in range(len(row_halves)):
            for d in (2, 1, 3):
                partial_copy(row, target, d, h).start()

    def total_of_partials(row, target, h):
        cut = row_halves[h]
        for d in (2, 1, 3):
            partial_copy(row, target, d, h).wait()
        total = partial_send[p, cut].astype(F32)
        for d in (1, 2, 3):
            total = total + target[d - 1, cut].astype(F32)
        return total

    def wait_expert_weights(layer):
        @pl.when(core == layer)
        def _():
            for copy in local_weights():
                copy.wait()

        @pl.when(core != layer)
        def _():
            for copy in sent_weights():
                copy.wait_recv()

    def wait_all(copies):
        for copy in copies:
            copy.wait()

    def start_attention(layer, h):
        cut = row_halves[h]
        held = stream[layer, cut]
        attn_all[layer, shard, cut] = (
            held * scale_of(held) * gains[layer, 0:1, :]
        ).astype(BF16)
        start_gather(Y_GATHER, h, attn_all, layer)

    def attention(layer):
        for h in range(len(row_halves)):
            for d in (2, 1, 3):
                y_gather_copy(Y_GATHER, d, h, attn_all, layer).wait()
        whole = attn_all[layer].reshape(span, width)
        raw_qk[layer] = dot(whole, weight_of(layer, 0, 0, 6))
        values[layer] = dot(whole, weight_of(layer, 1, 0, 2)).astype(BF16)
        low_qk[...] = normed_qk(layer)[0]

        key = low_qk[:, head_columns(2)]
        value = values[layer]
        for group_of in ((2, 1, 3, 0),):
            blocks = [mod(shard + d) for d in group_of]
            cuts = [block_rows(block) for block in blocks]
            mask = jnp.concatenate([mask_ref[cut] for cut in cuts], axis=0)
            tiles = []
            for tile in range(2):
                query = jnp.concatenate([low_qk[cut, head_columns(tile)] for cut in cuts], axis=0)
                outs = []
                for half in range(2):
                    expo, share = exp_scores(one_half(query, half), key, mask)
                    outs.append(dot((expo * share).astype(BF16), value))
                tiles.append(jnp.where(low_half, outs[0], outs[1]).astype(BF16))
            whole_mixed = jnp.concatenate(tiles, axis=1)
            out = dot(whole_mixed, weight_of(layer, 1, 2, 6), NT).astype(BF16)
            for i, (d, block, cut) in enumerate(zip(group_of, blocks, cuts)):
                part = slice(i * rows, (i + 1) * rows)
                mixed[layer, cut] = whole_mixed[part]
                y_send[block] = out[part]
        y_scatter(Y_SUM)

    def finish_attention(layer):
        for h, cut in enumerate(row_halves):
            center = stream[layer, cut] + y_total(Y_SUM, h)
            middle[layer, cut] = center
            feed = center * scale_of(center) * gains[layer, 1:2, :]
            spread_half(TOKENS, tokens, h, feed.astype(BF16))

    def feed_block(layer, f):
        return packed[layer, f].reshape(RING * group, width)

    def back_block(layer, f):
        return packed_back[layer, f].reshape(RING * group, width)

    def feed_chunk(layer, f, h):
        return packed[layer, f, h].reshape(chunk, width)

    def back_chunk(layer, f, h):
        return packed_back[layer, f, h].reshape(chunk, width)

    def grad_core(kind):
        return core_copy(C_GRAD + kind, grads.at[other, kind], grads_core.at[kind])

    lower, upper = pl.ds(0, rows), pl.ds(rows, rows)

    def grad_ring(kind, step):
        ahead = step in (0, 2, 4)
        part, cut = (
            (2, lower),
            (2, upper),
            (1, upper),
            (-1, lower),
            (1, lower),
            (-1, upper),
        )[step]
        return pltpu.make_async_remote_copy(
            src_ref=grads.at[core, kind, mod(shard + part), cut],
            dst_ref=grads_y.at[kind, step],
            send_sem=g_send.at[kind, step],
            recv_sem=g_recv.at[kind, step],
            device_id=y_device(1 if ahead else -1),
            device_id_type=MESH,
        )

    def sum_cores(kind):
        grad_core(kind).wait()

        def step(part, _):
            grads[core, kind, part] = (
                grads[core, kind, part].astype(F32) + grads_core[kind, part].astype(F32)
            ).astype(BF16)
            return 0

        lax.fori_loop(0, RING, step, 0)

    def start_ring(kind):
        for i in range(4):
            grad_ring(kind, i).start()

    def pass_grads(kind):
        for i, part, cut in ((0, 1, lower), (1, -1, upper)):
            grad_ring(kind, i).wait()
            at = mod(shard + part)
            grads[core, kind, at, cut] = (
                grads[core, kind, at, cut].astype(F32) + grads_y[kind, i].astype(F32)
            ).astype(BF16)
            grad_ring(kind, i + 4).start()

    def out_expert(layer, kind):
        return core_copy(
            C_OUT_EXPERT + 3 * layer + kind, out_stage.at[kind], expert_out.at[kind, core]
        )

    def out_local(kind):
        return pltpu.make_async_copy(
            out_stage.at[kind], expert_out.at[kind, core], out_sem.at[kind]
        )

    def finish_expert(layer, kind):
        for i in (2, 3, 4, 5):
            grad_ring(kind, i).wait()
        for cut, merged, direct in ((lower, 4, 3), (upper, 5, 2)):
            out_stage[kind, cut] = (
                grads[core, kind, shard, cut].astype(F32)
                + grads_y[kind, merged].astype(F32)
                + grads_y[kind, direct].astype(F32)
            )

        @pl.when(core == layer)
        def _():
            out_local(kind).start()

        @pl.when(core != layer)
        def _():
            out_expert(layer, kind).start()

    def wait_out(layer):
        for kind in range(3):
            @pl.when(core == layer)
            def _():
                out_local(kind).wait()

            @pl.when(core != layer)
            def _():
                out_expert(layer, kind).wait_send()

    def expert_grads(layer):
        for kind in range(3):
            def step(i, _):
                f, j = lax.div(i, 2), lax.rem(i, 2)
                cut = pl.ds(pl.multiple_of(j * 256, 256), 256)
                act = acts[kind, f, :, :, cut].reshape(2 * chunk, 256)
                rhs = back_block(layer, f) if kind == 2 else feed_block(layer, f)
                change = dot(act, rhs, TN).astype(BF16)
                grads[f, kind, 2 * j] = change[:128]
                grads[f, kind, 2 * j + 1] = change[128:]
                return 0

            lax.fori_loop(0, 4, step, 0)
            grad_core(kind).start()

    def proj_core_copy():
        return core_copy(C_PROJ, proj.at[other], proj_core)

    def proj_first(d, i):
        return pltpu.make_async_remote_copy(
            src_ref=proj.at[core, place_of(i, mod(p + d))],
            dst_ref=proj_recv.at[d - 1, i],
            send_sem=j_send.at[d - 1, i],
            recv_sem=j_recv.at[d - 1, i],
            device_id=p_device(d),
            device_id_type=MESH,
        )

    def proj_second(layer, d):
        return ring_copy(
            GRAD_Q + layer,
            d,
            proj_sum.at[mod(q + d)],
            proj_last.at[layer, d - 1],
            q_device(d),
        )

    def out_proj(layer):
        return core_copy(C_OUT_PROJ + layer, proj_stage, proj_out.at[core])

    def proj_one():
        proj_core_copy().wait()

        def step(i, _):
            proj[core, i] = (proj[core, i].astype(F32) + proj_core[i].astype(F32)).astype(BF16)
            return 0

        lax.fori_loop(0, RING * RING, step, 0)
        for i in range(RING):
            for d in (2, 1, 3):
                proj_first(d, i).start()

    def proj_two(layer):
        for i in range(RING):
            for d in (2, 1, 3):
                proj_first(d, i).wait()
            total = proj[core, place_of(i, p)].astype(F32)
            for d in (1, 2, 3):
                total = total + proj_recv[d - 1, i].astype(F32)
            proj_sum[i] = total.astype(BF16)
        for d in (2, 1, 3):
            proj_second(layer, d).start()

    def proj_three(layer):
        total = proj_sum[q].astype(F32)
        for d in (2, 1, 3):
            proj_second(layer, d).wait()
        for d in (1, 2, 3):
            total = total + proj_last[layer, d - 1].astype(F32)

        @pl.when(layer == core)
        def _():
            proj_out[core] = total

        @pl.when(layer != core)
        def _():
            proj_stage[...] = total
            out_proj(layer).start()

    def start_back(layer):
        for h, cut in enumerate(row_halves):
            change = total_of_partials(PARTIAL_BACK, partial_back, h)
            center = middle[layer, cut]
            scale = scale_of(center)
            normed = center * scale
            terms[layer, 1:2] += jnp.sum(change * normed, axis=0, keepdims=True)
            scaled = change * gains[layer, 1:2, :]
            inner = jnp.mean(scaled * normed, axis=-1, keepdims=True)
            back_mid = cotangent[cut] + scale * (scaled - normed * inner)
            cotangent[cut] = back_mid
            attn_back[layer, shard, cut] = back_mid.astype(BF16)
            start_gather(Y_GATHER_BACK, h, attn_back, layer)

    def find_probs(layer):
        low_qk[...] = normed_qk(layer)[0]
        key = low_qk[:, head_columns(2)]
        for i in range(4):
            query = one_half(low_qk[:, head_columns(i // 2)], i % 2)
            expo, share = exp_scores(query, key, mask_ref[...])
            parts[:, i * span : (i + 1) * span] = expo * share

    def change_at(block, columns):
        return slopes.at[0, lax.div(block, 2), lax.rem(block, 2), pl.ds(0, rows), columns]

    def attention_back(layer):
        key = low_qk[:, head_columns(2)]
        value = values[layer]
        back_key = jnp.zeros((span, 2 * HEAD), F32)
        back_value = jnp.zeros((span, 2 * HEAD), F32)
        for group_of in ((0, 1, 3, 2),):
            blocks = [mod(shard - d) for d in group_of]
            cuts = [block_rows(block) for block in blocks]
            for d in group_of:
                for h in range(len(row_halves)):
                    if d:
                        y_gather_copy(Y_GATHER_BACK, d, h, attn_back, layer).wait()
            back = jnp.concatenate([attn_back[layer, block] for block in blocks], axis=0)
            back = dot(back, weight_of(layer, 1, 2, 6)).astype(BF16)
            for tile in range(2):
                pieces = []
                queries = jnp.concatenate(
                    [low_qk[cut, head_columns(tile)] for cut in cuts], axis=0
                )
                for half in range(2):
                    i = 2 * tile + half
                    columns = slice(i * span, (i + 1) * span)
                    probs = jnp.concatenate([parts[cut, columns] for cut in cuts], axis=0)
                    query = one_half(queries, half)
                    piece = one_half(back[:, head_columns(tile)], half)
                    back_probs = dot(piece, value, NT)
                    back_value = back_value + dot(probs.astype(BF16), piece, TN)
                    total = jnp.sum(probs * back_probs, axis=-1, keepdims=True)
                    back_scores = (probs * (back_probs - total)).astype(BF16)
                    pieces.append(dot(back_scores, key))
                    back_key = back_key + dot(back_scores, query, TN)
                joined = jnp.where(low_half, pieces[0], pieces[1])
                for i, block in enumerate(blocks):
                    change_at(block, pl.ds(tile * 2 * HEAD, 2 * HEAD))[...] = joined[
                        i * rows : (i + 1) * rows
                    ]
        _low, normed, scale = normed_qk(layer)
        change = jnp.concatenate(
            [change_at(i, pl.ds(0, 4 * HEAD))[...] for i in range(RING)], axis=0
        )
        change = jnp.concatenate([change, back_key], axis=1) * HEAD ** (-0.5)
        term = jnp.sum(change * normed, axis=0, keepdims=True)
        terms[layer, 2:3, : 6 * HEAD] = term
        scaled = change * qk_gain(layer)
        inner = head_mean(scaled * normed)
        low_qk[...] = (scale * (scaled - normed * inner)).astype(BF16)
        back_v[...] = back_value.astype(BF16)
        for places, cut in zip(half_rows, column_halves):
            out = dot(low_qk[...], weight_of(layer, 0, 0, 6, places), NT)
            out = out + dot(back_v[...], weight_of(layer, 1, 0, 2, places), NT)
            for i in range(RING):
                y_send[i, :, cut] = out[i * rows : (i + 1) * rows].astype(BF16)
        y_scatter(Y_SUM_BACK)

    def proj_grads(layer):
        def step(i, _):
            cut = pl.ds(pl.multiple_of(i * 4 * rows, 4 * rows), 4 * rows)
            at = pl.ds(i * 4, 4)
            feed = attn_all[layer, :, :, cut].reshape(span, 4 * rows)
            back = attn_back[layer, :, :, cut].reshape(span, 4 * rows)
            for half, start, stop, lhs, rhs in (
                (0, 0, 6, feed, low_qk[...]),
                (1, 0, 2, feed, back_v[...]),
                (1, 2, 6, back, mixed[layer]),
            ):
                change = dot(lhs, rhs, TN).astype(BF16)
                proj[half, at, :, start * HEAD : stop * HEAD] = change.reshape(
                    4, rows, (stop - start) * HEAD
                )
            return 0

        lax.fori_loop(0, 4, step, 0)
        proj_core_copy().start()

    def finish_back(layer, take):
        for h, cut in enumerate(row_halves):
            total = y_total(Y_SUM_BACK, h)
            held = stream[layer, cut]
            scale = scale_of(held)
            normed = held * scale
            terms[layer, 0:1] += jnp.sum(total * normed, axis=0, keepdims=True)
            scaled = total * gains[layer, 0:1, :]
            inner = jnp.mean(scaled * normed, axis=-1, keepdims=True)
            take(h, cut, (cotangent[cut] + scale * (scaled - normed * inner)).astype(BF16))

    def slopes_of(gate_part, up_part):
        sigmoid = jax.nn.sigmoid(gate_part)
        silu = gate_part * sigmoid
        return up_part * sigmoid * (1.0 + gate_part * (1.0 - sigmoid)), silu

    def expert_back(layer, f, h, back_hidden, to_gate, to_up):
        back_gate = (back_hidden * to_gate).astype(BF16)
        back_up = (back_hidden * to_up).astype(BF16)
        acts[0, f, h] = back_gate
        acts[1, f, h] = back_up

        def columns(cut):
            return dot(back_gate, w_gate[layer, f, cut], NT) + dot(
                back_up, w_up[layer, f, cut], NT
            )

        put_result(RESULT_BACK, f, h, packed_send, result_back, columns)

    def put_forward(layer, f, h, inner):
        def columns(cut):
            return dot(inner, w_down[layer, f, :, cut])

        put_result(RESULT, f, h, result_send, result, columns)

    def gate_and_up(layer, f, h):
        block = feed_chunk(layer, f, h)
        return dot(block, w_gate[layer, f]), dot(block, w_up[layer, f])

    for h in range(len(row_halves)):
        start_attention(0, h)
    start_second(0)
    make_tables()
    for h, cut in enumerate(row_halves):
        spread_half(TOKENS_BACK, tokens_back, h, cotangent[cut].astype(BF16))
    start_pass(0)
    for copy in sent_weights():
        copy.start()
    wait_pass(0)
    attention(0)
    start_second(1)
    take_tables()
    wait_spread(TOKENS_BACK, tokens_back)
    pack(PACKED_BACK, 1, tokens_back, packed_back, True)
    finish_attention(0)
    start_pass(1)

    def packed_back_sent(f, h):
        for copy in packed_copies(PACKED_BACK, 1, f, h, packed_back):
            copy.wait_send()

    each_chunk(packed_back_sent)
    wait_expert_weights(0)
    wait_spread(TOKENS, tokens)
    pack(PACKED, 0, tokens, packed, False)

    def experts_forward(f, h):
        wait_all(packed_copies(PACKED, 0, f, h, packed))
        gate_part, up_part = gate_and_up(0, f, h)
        inner = (gate_part * jax.nn.sigmoid(gate_part) * up_part).astype(BF16)
        put_forward(0, f, h, inner)

    each_chunk(experts_forward)
    combine(RESULT, 0, result_send, result, True)
    start_partials(PARTIAL, partial)
    for h, cut in enumerate(row_halves):
        final = middle[0, cut] + total_of_partials(PARTIAL, partial, h)
        stream[1, cut] = final.astype(BF16).astype(F32)
        start_attention(1, h)

    wait_pass(1)
    wait_expert_weights(1)

    def hidden_back(f, h):
        for copy in packed_copies(PACKED_BACK, 1, f, h, packed_back):
            copy.wait_recv()
        slopes[0, f, h] = dot(back_chunk(1, f, h), w_down[1, f], NT)

    each_chunk(hidden_back)
    attention(1)
    finish_attention(1)
    wait_spread(TOKENS, tokens)
    pack(PACKED, 1, tokens, packed, False)

    def experts_both(f, h):
        wait_all(packed_copies(PACKED, 1, f, h, packed))
        gate_part, up_part = gate_and_up(1, f, h)
        to_gate, to_up = slopes_of(gate_part, up_part)
        acts[2, f, h] = (to_up * up_part).astype(BF16)
        expert_back(1, f, h, slopes[0, f, h], to_gate, to_up)

    each_chunk(experts_both)
    each_chunk(lambda f, h: put_forward(1, f, h, acts[2, f, h]))
    expert_grads(1)
    combine(RESULT_BACK, 1, packed_send, result_back, False)
    start_partials(PARTIAL_BACK, partial_back)
    sum_cores(0)
    start_ring(0)

    start_back(1)
    combine(RESULT, 1, result_send, result, True)
    start_partials(PARTIAL, partial)
    sum_cores(1)
    find_probs(1)
    pass_grads(0)
    attention_back(1)
    proj_grads(1)
    for h, cut in enumerate(row_halves):
        final = middle[1, cut] + total_of_partials(PARTIAL, partial, h)
        ends_stage[0, cut] = final.astype(BF16)
    sum_cores(2)
    pl.semaphore_signal(credit, inc=1, device_id=core_device, device_id_type=MESH)

    def hand_on(h, cut, block):
        cotangent[cut] = block.astype(F32)
        spread_half(TOKENS_BACK, tokens_back, h, block)

    finish_back(1, hand_on)

    start_ring(1)
    start_ring(2)
    proj_one()

    def find_slopes(f, h):
        gate_part, up_part = gate_and_up(0, f, h)
        to_gate, to_up = slopes_of(gate_part, up_part)
        slopes[0, f, h] = to_gate
        slopes[1, f, h] = to_up
        acts[2, f, h] = (to_up * up_part).astype(BF16)

    each_chunk(find_slopes)
    wait_spread(TOKENS_BACK, tokens_back)
    pack(PACKED_BACK, 0, tokens_back, packed_back, True)
    pass_grads(1)
    pass_grads(2)
    proj_two(1)

    def experts_back(f, h):
        wait_all(packed_copies(PACKED_BACK, 0, f, h, packed_back))
        back_hidden = dot(back_chunk(0, f, h), w_down[0, f], NT)
        expert_back(0, f, h, back_hidden, slopes[0, f, h], slopes[1, f, h])

    each_chunk(experts_back)
    for kind in range(3):
        finish_expert(1, kind)
    for d in (1, -1):
        pl.semaphore_signal(y_credit, inc=1, device_id=y_device(d), device_id_type=MESH)
    pl.semaphore_wait(credit, 1)
    expert_grads(0)
    proj_three(1)
    combine(RESULT_BACK, 0, packed_send, result_back, False)
    start_partials(PARTIAL_BACK, partial_back)
    pl.semaphore_wait(y_credit, 2)
    sum_cores(0)
    start_ring(0)
    start_back(0)
    sum_cores(1)
    find_probs(0)
    pass_grads(0)
    attention_back(0)
    start_ring(1)

    @pl.when(core != 1)
    def _():
        out_proj(1).wait_send()

    proj_grads(0)
    sum_cores(2)
    start_ring(2)

    def keep(h, cut, block):
        ends_stage[1, cut] = block

    finish_back(0, keep)

    ends_out[core] = jnp.where(first, ends_stage[1], ends_stage[0])
    ends_copy_out = core_copy(C_OUT_ENDS, ends_stage.at[core], ends_out.at[core])
    ends_copy_out.start()
    term_copy = core_copy(C_TERM, terms.at[other], terms_core)
    term_copy.start()
    wait_out(1)
    proj_one()
    term_copy.wait()
    terms_recv[0, 0] = terms[core] + terms_core[...]
    for axis, (row, device) in enumerate(
        ((GAIN_P, p_device), (GAIN_Q, q_device), (GAIN_Y, y_device))
    ):
        copies = [
            ring_copy(
                row, d, terms_recv.at[axis, 0], terms_recv.at[axis, d], device(d)
            )
            for d in (2, 1, 3)
        ]
        for copy in copies:
            copy.start()
        if axis == 0:
            pass_grads(1)
            proj_two(0)
        if axis == 1:
            pass_grads(2)
            proj_three(0)
            finish_expert(0, 0)
        if axis == 2:
            finish_expert(0, 1)
        wait_all(copies)
        total = terms_recv[axis, 0]
        for d in (1, 2, 3):
            total = total + terms_recv[axis, d]
        if axis < 2:
            terms_recv[axis + 1, 0] = total
        else:
            gains_out[...] = total

    finish_expert(0, 2)
    wait_out(0)
    for layer in range(2):
        @pl.when(core == layer)
        def _():
            for kind in range(3):
                out_expert(layer, kind).wait_recv()
            out_proj(layer).wait_recv()

    @pl.when(core != 0)
    def _():
        out_proj(0).wait_send()

    ends_copy_out.wait()
    for copy in (piece_copy, ends_copy, gains_copy, routes_copy, gates_copy):
        copy.wait_send()
    for copy in sent_weights():
        copy.wait_send()
    for layer in range(2):
        for d in range(RING):
            for i in range(RING):
                weight_pass(layer, d, i).wait_send()
        for d in (1, 2, 3):
            weight_first(layer, d).wait_send()
            for i in range(RING):
                weight_second(layer, d, i).wait_send()
    for d in (1, 2, 3):
        ring_copy(
            TABLE_P, d, table_send.at[d], table_recv.at[d - 1], p_device(d)
        ).wait_send()


def finish(
    ends_ref,
    gains_ref,
    proj_ref,
    experts_ref,
    ends_out,
    attn_gain_out,
    query_gain_out,
    key_gain_out,
    feed_gain_out,
    query_out,
    key_out,
    value_out,
    out_out,
    gate_out,
    up_out,
    down_out,
    ends,
    gains,
    proj,
    experts,
    turned,
    sems,
):
    pieces = [(kind, f) for kind in range(3) for f in range(2)]
    moves = [
        pltpu.make_async_copy(
            experts_ref.at[kind, f], experts.at[kind, f], sems.at[2 * kind + f]
        )
        for kind, f in pieces
    ]
    moves += [
        pltpu.make_async_copy(ends_ref, ends, sems.at[6]),
        pltpu.make_async_copy(gains_ref, gains, sems.at[7]),
        pltpu.make_async_copy(proj_ref, proj, sems.at[8]),
    ]
    for move in moves:
        move.start()
    results = []
    for i, (kind, f) in enumerate(pieces):
        moves[i].wait()
        if kind < 2:
            turned[kind, f] = experts[kind, f].T
        source = experts.at[kind, f] if kind == 2 else turned.at[kind, f]
        target = (gate_out, up_out, down_out)[kind]
        results.append(pltpu.make_async_copy(source, target.at[0, f], sems.at[9 + i]))
        results[-1].start()
    moves[6].wait()
    results.append(pltpu.make_async_copy(ends, ends_out.at[0], sems.at[15]))
    results[-1].start()
    moves[7].wait()
    attn_gain_out[...] = gains[0:1]
    feed_gain_out[...] = gains[1:2]
    query_gain_out[...] = exact_dot(gains[2:3, : 4 * HEAD], copies_of_head(4), NT)
    key_gain_out[...] = exact_dot(gains[2:3, 4 * HEAD : 6 * HEAD], copies_of_head(2), NT)
    moves[8].wait()
    swap = swap_heads()
    query_out[0] = exact_dot(proj[0, :, : 4 * HEAD], swap)
    key_out[0] = proj[0, :, 4 * HEAD :]
    value_out[0] = proj[1, :, : 2 * HEAD]
    out_out[0] = exact_dot(proj[1, :, 2 * HEAD :], swap)
    for result in results:
        result.wait()


def shards(
    ends_in,
    segments,
    routes,
    gates,
    attn_gain,
    query_gain,
    key_gain,
    feed_gain,
    w_query,
    key_weight,
    value_weight,
    w_out,
    w_gate,
    w_up,
    w_down,
):
    rows = ends_in.shape[2]
    width = ends_in.shape[3]
    top = routes.shape[3]
    hidden = w_gate.shape[3]
    experts_all = w_gate.shape[1] * lax.axis_size("expert")
    capacity = 3 * rows * top // (2 * experts_all)
    group = RING * capacity
    part_rows = group // 2
    chunk = RING * part_rows
    span = RING * rows
    vmem = pl.BlockSpec(memory_space=pltpu.VMEM)
    anywhere = pl.BlockSpec(memory_space=pl.ANY)
    half = 6 * HEAD
    everyone = RING * RING
    scratch = [
        pltpu.VMEM((2, 2, width, hidden), BF16),
        pltpu.VMEM((2, 2, width, hidden), BF16),
        pltpu.VMEM((2, 2, hidden, width), BF16),
        pltpu.VMEM((2, 2, everyone, rows, half), BF16),
        pltpu.VMEM((rows, width), BF16),
        pltpu.VMEM((2, 8, width), F32),
        pltpu.VMEM((2, top, rows), jnp.int32),
        pltpu.VMEM((2, top, rows), F32),
        pltpu.VMEM((span, span), F32),
        pltpu.VMEM((2, rows, half), BF16),
        pltpu.VMEM((8, width), F32),
        pltpu.VMEM((RING, 2, 2, 8, span), F32),
        pltpu.VMEM((RING - 1, 2, 2, 8, span), F32),
        pltpu.VMEM((2, 8, 1, span), F32),
        pltpu.VMEM((2, 8, 1, span), F32),
        pltpu.VMEM((2, rows, width), F32),
        pltpu.VMEM((2, rows, width), F32),
        pltpu.VMEM((rows, width), F32),
        pltpu.VMEM((2, RING, rows, width), BF16),
        pltpu.VMEM((2, span, half), F32),
        pltpu.VMEM((2, span, 2 * HEAD), BF16),
        pltpu.VMEM((2, span, 4 * HEAD), BF16),
        pltpu.VMEM((RING, rows, width), BF16),
        pltpu.VMEM((RING - 1, rows, width), BF16),
        pltpu.VMEM((RING, rows, width), BF16),
        pltpu.VMEM((RING, rows, width), BF16),
        pltpu.VMEM((2, 2, RING - 1, group // 2, width), BF16),
        pltpu.VMEM((2, 2, 2, RING, group // 2, width), BF16),
        pltpu.VMEM((2, 2, 2, RING, group // 2, width), BF16),
        pltpu.VMEM((2, 2, RING - 1, group // 2, width), BF16),
        pltpu.VMEM((2, 2, RING, group // 2, width), BF16),
        pltpu.VMEM((2, 2, RING, group // 2, width), BF16),
        pltpu.VMEM((RING, rows, width), BF16),
        pltpu.VMEM((RING - 1, rows, width), BF16),
        pltpu.VMEM((RING - 1, rows, width), BF16),
        pltpu.VMEM((span, width), F32),
        pltpu.VMEM((2, 2, 2, 2 * group, hidden), F32),
        pltpu.VMEM((2, RING, rows, width), BF16),
        pltpu.VMEM((span, half), BF16),
        pltpu.VMEM((span, 2 * HEAD), BF16),
        pltpu.VMEM((3, 2, 2, 2 * group, hidden), BF16),
        pltpu.VMEM((2, 3, RING, hidden // RING, width), BF16),
        pltpu.VMEM((3, RING, hidden // RING, width), BF16),
        pltpu.VMEM((3, 6, rows, width), BF16),
        pltpu.VMEM((3, hidden // RING, width), F32),
        pltpu.VMEM((2, everyone, rows, half), BF16),
        pltpu.VMEM((everyone, rows, half), BF16),
        pltpu.VMEM((RING - 1, RING, rows, half), BF16),
        pltpu.VMEM((RING, rows, half), BF16),
        pltpu.VMEM((2, RING - 1, rows, half), BF16),
        pltpu.VMEM((rows, half), F32),
        pltpu.VMEM((2, 8, width), F32),
        pltpu.VMEM((8, width), F32),
        pltpu.VMEM((3, RING, 8, width), F32),
        pltpu.VMEM((2, rows, width), BF16),
        pltpu.SemaphoreType.DMA((RING_ROWS, RING - 1)),
        pltpu.SemaphoreType.DMA((RING_ROWS, RING - 1)),
        pltpu.SemaphoreType.DMA((2, RING - 1, RING)),
        pltpu.SemaphoreType.DMA((2, RING - 1, RING)),
        pltpu.SemaphoreType.DMA((2, RING, RING)),
        pltpu.SemaphoreType.DMA((2, RING, RING)),
        pltpu.SemaphoreType.DMA((RING - 1, RING)),
        pltpu.SemaphoreType.DMA((RING - 1, RING)),
        pltpu.SemaphoreType.DMA((3, 6)),
        pltpu.SemaphoreType.DMA((3, 6)),
        pltpu.SemaphoreType.DMA((CORE_ROWS,)),
        pltpu.SemaphoreType.DMA((CORE_ROWS,)),
        pltpu.SemaphoreType.DMA((3,)),
        pltpu.SemaphoreType.DMA((3,)),
        pltpu.SemaphoreType.REGULAR,
        pltpu.SemaphoreType.REGULAR,
    ]
    ends, gain_sums, proj, experts = pl.pallas_call(
        functools.partial(kernel, rows, width, hidden, capacity),
        out_shape=(
            jax.ShapeDtypeStruct((2, rows, width), BF16),
            jax.ShapeDtypeStruct((8, width), F32),
            jax.ShapeDtypeStruct((2, rows, half), F32),
            jax.ShapeDtypeStruct((3, 2, hidden // RING, width), F32),
        ),
        in_specs=[vmem] * 12 + [anywhere] * 3,
        out_specs=(vmem, vmem, vmem, anywhere),
        scratch_shapes=scratch,
        compiler_params=pltpu.CompilerParams(
            collective_id=0, has_side_effects=True, vmem_limit_bytes=63 << 20
        ),
        cost_estimate=pl.CostEstimate(
            flops=60_000_000_000, bytes_accessed=20_000_000, transcendentals=4_000_000
        ),
        name="layers",
    )(
        ends_in[0],
        segments,
        routes[0].transpose(0, 2, 1),
        gates[0].transpose(0, 2, 1),
        attn_gain,
        query_gain,
        key_gain,
        feed_gain,
        w_query[0],
        key_weight[0],
        value_weight[0],
        w_out[0].T,
        w_gate[0],
        w_up[0],
        w_down[0],
    )
    shapes = (
        ((1, 2, rows, width), BF16),
        ((1, width), F32),
        ((1, HEAD), F32),
        ((1, HEAD), F32),
        ((1, width), F32),
        ((1,) + w_query.shape[1:], F32),
        ((1,) + key_weight.shape[1:], F32),
        ((1,) + value_weight.shape[1:], F32),
        ((1, w_out.shape[2], w_out.shape[1]), F32),
        ((1, 2, width, hidden // RING), F32),
        ((1, 2, width, hidden // RING), F32),
        ((1, 2, hidden // RING, width), F32),
    )
    outputs = pl.pallas_call(
        finish,
        out_shape=tuple(jax.ShapeDtypeStruct(shape, dtype) for shape, dtype in shapes),
        in_specs=[anywhere] * 4,
        out_specs=(anywhere,) + (vmem,) * 8 + (anywhere,) * 3,
        scratch_shapes=[
            pltpu.VMEM((2, rows, width), BF16),
            pltpu.VMEM((8, width), F32),
            pltpu.VMEM((2, rows, half), F32),
            pltpu.VMEM((3, 2, hidden // RING, width), F32),
            pltpu.VMEM((2, 2, width, hidden // RING), F32),
            pltpu.SemaphoreType.DMA((16,)),
        ],
        compiler_params=pltpu.CompilerParams(vmem_limit_bytes=60 << 20),
        name="finish",
    )(ends, gain_sums, proj, experts)
    return (*outputs[:8], outputs[8].transpose(0, 2, 1), *outputs[9:])


def solution(mesh):
    return jax.shard_map(
        shards,
        mesh=mesh,
        in_specs=(
            P("section", None, ("expert", "shard"), None),
            P(None, "expert"),
            P("section", None, ("expert", "shard"), None),
            P("section", None, ("expert", "shard"), None),
            P("section", None),
            P("section", None),
            P("section", None),
            P("section", None),
            P("section", "expert", "shard"),
            P("section", "expert", "shard"),
            P("section", "expert", "shard"),
            P("section", "shard", "expert"),
            P("section", "expert", None, None),
            P("section", "expert", None, None),
            P("section", "expert", None, None),
        ),
        out_specs=(
            P("section", None, ("expert", "shard"), None),
            P("section", None),
            P("section", None),
            P("section", None),
            P("section", None),
            P("section", "expert", "shard"),
            P("section", "expert", "shard"),
            P("section", "expert", "shard"),
            P("section", "shard", "expert"),
            P("section", "expert", None, "shard"),
            P("section", "expert", None, "shard"),
            P("section", "expert", "shard", None),
        ),
        check_vma=False,
    )
```

```python
import functools

import jax
import jax.numpy as jnp
from jax import lax
from jax.experimental import pallas as pl
from jax.experimental.pallas import tpu as pltpu
from jax.sharding import PartitionSpec as P

EPS = 1e-06
NEG = -1e30
HEAD = 64
RING = 4
MESH = pl.DeviceIdType.MESH
F32 = jnp.float32
BF16 = jnp.bfloat16

NN = (((1,), (0,)), ((), ()))
NT = (((1,), (1,)), ((), ()))
TN = (((0,), (0,)), ((), ()))

PIECES = 4
Y_GATHER, Y_SUM, Y_GATHER_BACK, Y_SUM_BACK = 0, 4, 8, 12
TOKENS, TOKENS_BACK, PARTIAL, PARTIAL_BACK = 16, 20, 24, 28
GRAD_Q, GAIN_P, GAIN_Q, GAIN_Y, WEIGHT_P, TABLE_P = 32, 34, 35, 36, 37, 39
PACKED, PACKED_BACK, RESULT, RESULT_BACK, RING_ROWS = 40, 44, 48, 52, 56

C_ENDS, C_GAINS, C_ROUTES, C_GATES, C_PIECE = range(5)
C_GATE, C_UP, C_DOWN, C_GRAD, C_TERM, C_OUT_ENDS = 5, 6, 7, 8, 12, 13
C_OUT_EXPERT, C_OUT_PROJ, C_PROJ, CORE_ROWS = 14, 20, 22, 26


def dot(a, b, form=NN):
    return lax.dot_general(a, b, form, preferred_element_type=F32)


def exact_dot(a, b, form=NN):
    return lax.dot_general(
        a, b, form, preferred_element_type=F32, precision=lax.Precision.HIGHEST
    )


def iota(shape, dimension):
    return lax.broadcasted_iota(jnp.int32, shape, dimension)


def swap_heads():
    size = 4 * HEAD
    row, col = iota((size, size), 0), iota((size, size), 1)
    head = lax.div(row, HEAD)
    shift = jnp.where(head == 1, HEAD, jnp.where(head == 2, -HEAD, 0))
    return (col == row + shift).astype(F32)


def copies_of_head(count):
    shape = (HEAD, count * HEAD)
    return (lax.rem(iota(shape, 1), HEAD) == iota(shape, 0)).astype(F32)


def scale_of(rows):
    return lax.rsqrt(jnp.mean(rows * rows, axis=-1, keepdims=True) + EPS)


def kernel(
    rows,
    width,
    hidden,
    capacity,
    ends_ref,
    segments_ref,
    routes_ref,
    gates_ref,
    attn_gain_ref,
    query_gain_ref,
    key_gain_ref,
    feed_gain_ref,
    query_ref,
    key_ref,
    value_ref,
    out_ref,
    gate_ref,
    up_ref,
    down_ref,
    ends_out,
    gains_out,
    proj_out,
    expert_out,
    w_gate,
    w_up,
    w_down,
    w_attn,
    ends_in,
    gains,
    routes,
    gates,
    mask_ref,
    piece_ref,
    gains_ref,
    table_send,
    table_recv,
    slots,
    weights,
    stream,
    middle,
    cotangent,
    attn_all,
    raw_qk,
    values,
    mixed,
    y_send,
    y_recv,
    tokens,
    tokens_back,
    packed_send,
    packed,
    packed_back,
    result_send,
    result,
    result_back,
    partial_send,
    partial,
    partial_back,
    parts,
    slopes,
    attn_back,
    low_qk,
    back_v,
    acts,
    grads,
    grads_core,
    grads_y,
    out_stage,
    proj,
    proj_core,
    proj_recv,
    proj_sum,
    proj_last,
    proj_stage,
    terms,
    terms_core,
    terms_recv,
    ends_stage,
    send_sem,
    recv_sem,
    w_send,
    w_recv,
    h_send,
    h_recv,
    j_send,
    j_recv,
    g_send,
    g_recv,
    c_send,
    c_recv,
    local_sem,
    out_sem,
    credit,
    y_credit,
):
    core = lax.axis_index("section")
    place = lax.axis_index("expert")
    shard = lax.axis_index("shard")
    x = lax.rem(place, RING)
    z = lax.div(place, RING)
    p = x + core * (z - x)
    q = z + core * (x - z)
    span = RING * rows
    group = RING * capacity
    part_rows = group // 2
    chunk = RING * part_rows
    other = 1 - core

    def mod(value):
        return lax.rem(value + 2 * RING, RING)

    def place_of(second, first):
        return (1 - core) * (second * RING + first) + core * (first * RING + second)

    def y_device(d):
        return (core, place, mod(shard + d))

    def p_device(d):
        return (core, place_of(q, mod(p + d)), shard)

    def q_device(d):
        return (core, place_of(mod(q + d), p), shard)

    core_device = (other, place, shard)

    def order(k):
        return k + lax.div(k, 2) * (5 - 2 * k)

    def ring_copy(row, d, src, dst, device):
        return pltpu.make_async_remote_copy(
            src_ref=src,
            dst_ref=dst,
            send_sem=send_sem.at[row, d - 1],
            recv_sem=recv_sem.at[row, d - 1],
            device_id=device,
            device_id_type=MESH,
        )

    def core_copy(row, src, dst):
        return pltpu.make_async_remote_copy(
            src_ref=src,
            dst_ref=dst,
            send_sem=c_send.at[row],
            recv_sem=c_recv.at[row],
            device_id=core_device,
            device_id_type=MESH,
        )

    barrier = pltpu.get_barrier_semaphore()
    for d in (1, 2, 3):
        for device in (y_device(d), p_device(d), q_device(d)):
            pl.semaphore_signal(barrier, inc=1, device_id=device, device_id_type=MESH)
    pl.semaphore_signal(barrier, inc=1, device_id=core_device, device_id_type=MESH)

    def local_weights():
        return (
            pltpu.make_async_copy(gate_ref, w_gate.at[core], local_sem.at[0]),
            pltpu.make_async_copy(up_ref, w_up.at[core], local_sem.at[1]),
            pltpu.make_async_copy(down_ref, w_down.at[core], local_sem.at[2]),
        )

    swap = swap_heads().astype(BF16)
    piece_ref[0, :, : 4 * HEAD] = dot(query_ref[...], swap).astype(BF16)
    piece_ref[0, :, 4 * HEAD :] = key_ref[...]
    piece_ref[1, :, : 2 * HEAD] = value_ref[...]
    piece_ref[1, :, 2 * HEAD :] = dot(out_ref[...], swap).astype(BF16)
    gains_ref[0:1] = attn_gain_ref[...]
    gains_ref[1:2] = feed_gain_ref[...]
    gains_ref[2:3, : 4 * HEAD] = exact_dot(query_gain_ref[...], copies_of_head(4))
    gains_ref[2:3, 4 * HEAD : 6 * HEAD] = exact_dot(key_gain_ref[...], copies_of_head(2))
    w_attn[core, core, place] = piece_ref[core]
    gains[core] = gains_ref[...]
    routes[core] = routes_ref[core]
    gates[core] = gates_ref[core]
    across = jnp.broadcast_to(
        jnp.where(core == 0, segments_ref[0:1], segments_ref[1:2]), (span, span)
    ).astype(F32)
    causal = iota((span, span), 0) >= iota((span, span), 1)
    mask_ref[...] = (causal & (across == across.T)).astype(F32)
    terms[...] = jnp.zeros_like(terms)
    for copy in local_weights():
        copy.start()

    pl.semaphore_wait(barrier, 10)
    piece_copy = core_copy(C_PIECE, piece_ref.at[other], w_attn.at[core, other, place])
    ends_copy = core_copy(C_ENDS, ends_ref.at[other], ends_in)
    gains_copy = core_copy(C_GAINS, gains_ref, gains.at[core])
    routes_copy = core_copy(C_ROUTES, routes_ref.at[other], routes.at[core])
    gates_copy = core_copy(C_GATES, gates_ref.at[other], gates.at[core])
    for copy in (piece_copy, ends_copy, gains_copy, routes_copy, gates_copy):
        copy.start()

    def sent_weights():
        return (
            core_copy(C_GATE, gate_ref, w_gate.at[core]),
            core_copy(C_UP, up_ref, w_up.at[core]),
            core_copy(C_DOWN, down_ref, w_down.at[core]),
        )

    def weight_first(layer, d):
        return pltpu.make_async_remote_copy(
            src_ref=w_attn.at[layer, core, place],
            dst_ref=w_attn.at[layer, core, place],
            send_sem=send_sem.at[WEIGHT_P + layer, d - 1],
            recv_sem=recv_sem.at[WEIGHT_P + layer, d - 1],
            device_id=p_device(d),
            device_id_type=MESH,
        )

    def weight_second(layer, d, i):
        held = place_of(q, mod(p - i))
        return pltpu.make_async_remote_copy(
            src_ref=w_attn.at[layer, core, held],
            dst_ref=w_attn.at[layer, core, held],
            send_sem=w_send.at[layer, d - 1, i],
            recv_sem=w_recv.at[layer, d - 1, i],
            device_id=q_device(d),
            device_id_type=MESH,
        )

    def weight_pass(layer, d, i):
        held = place_of(mod(q - d), mod(p - i))
        return pltpu.make_async_remote_copy(
            src_ref=w_attn.at[layer, core, held],
            dst_ref=w_attn.at[layer, core, held],
            send_sem=h_send.at[layer, d, i],
            recv_sem=h_recv.at[layer, d, i],
            device_id=core_device,
            device_id_type=MESH,
        )

    def start_first(layer):
        for d in (2, 1, 3):
            weight_first(layer, d).start()

    def start_second(layer):
        for i in (0, 1, 3, 2):
            if i:
                weight_first(layer, i).wait_recv()
            for d in (2, 1, 3):
                weight_second(layer, d, i).start()
            weight_pass(layer, 0, i).start()

    def start_pass(layer):
        for i in (0, 1, 3, 2):
            for d in (2, 1, 3):
                weight_second(layer, d, i).wait_recv()
                weight_pass(layer, d, i).start()

    def wait_pass(layer):
        for d in range(RING):
            for i in range(RING):
                weight_pass(layer, d, i).wait_recv()

    piece_copy.wait_recv()
    start_first(0)
    start_first(1)
    ends_copy.wait_recv()
    gains_copy.wait_recv()
    first = core == 0
    stream[0] = jnp.where(first, ends_ref[0], ends_in[...]).astype(F32)
    cotangent[...] = jnp.where(first, ends_in[...], ends_ref[1]).astype(F32)

    def make_tables():
        routes_copy.wait_recv()
        gates_copy.wait_recv()
        tiles = 32
        names = iota((tiles, rows), 0)
        ahead = (iota((rows, rows), 0) < iota((rows, rows), 1)).astype(BF16)
        spread = (iota((rows, span), 1) == iota((rows, span), 0) + rows * p).astype(F32)
        row_at = lax.broadcasted_iota(jnp.int32, (2 * RING, tiles), 0)
        col_at = lax.broadcasted_iota(jnp.int32, (2 * RING, tiles), 1)
        for layer in range(2):
            named = jnp.zeros((tiles, rows), F32)
            gate = jnp.zeros((tiles, rows), F32)
            for j in range(routes.shape[1]):
                hit = (routes[layer, j : j + 1, :] == names).astype(F32)
                named = named + hit
                gate = gate + hit * gates[layer, j : j + 1, :]
            rank = dot(named.astype(BF16), ahead)
            slot = named * (rank + (1 + capacity * p).astype(F32))
            wide_slot = exact_dot(slot, spread)
            wide_gate = exact_dot(gate, spread)
            for d in range(RING):
                first_axis = mod(p + d)
                owner = place_of(lax.div(row_at, 2), first_axis)
                choose = (col_at == 2 * owner + lax.rem(row_at, 2)).astype(F32)
                table_send[d, layer, 0] = exact_dot(choose, wide_slot)
                table_send[d, layer, 1] = exact_dot(choose, wide_gate)
        for d in (2, 1, 3):
            ring_copy(
                TABLE_P, d, table_send.at[d], table_recv.at[d - 1], p_device(d)
            ).start()

    def take_tables():
        for d in (2, 1, 3):
            ring_copy(
                TABLE_P, d, table_send.at[d], table_recv.at[d - 1], p_device(d)
            ).wait_recv()
        for layer in range(2):
            for kind, target in ((0, slots), (1, weights)):
                whole = table_send[0, layer, kind]
                for d in (1, 2, 3):
                    whole = whole + table_recv[d - 1, layer, kind]
                for r in range(2 * RING):
                    target[layer, r] = whole[r : r + 1, :]

    def choose_rows(layer, second, f, h):
        at = iota((part_rows, span), 0) + (1 + part_rows * h)
        return at.astype(F32) == slots[layer, 2 * second + f]

    lanes = lax.broadcasted_iota(jnp.int32, (1, 2 * HEAD), 1)
    low_half = lanes < HEAD
    halves = (low_half, lanes >= HEAD)

    def head_mean(block):
        at_row = lax.broadcasted_iota(jnp.int32, (2 * HEAD, 2 * HEAD), 0) >= HEAD
        at_col = lax.broadcasted_iota(jnp.int32, (2 * HEAD, 2 * HEAD), 1) >= HEAD
        share = jnp.where(at_row == at_col, 1.0 / HEAD, 0.0).astype(F32)
        tiles = [
            exact_dot(block[:, i : i + 2 * HEAD], share)
            for i in range(0, block.shape[1], 2 * HEAD)
        ]
        return jnp.concatenate(tiles, axis=1)

    def qk_gain(layer):
        return gains[layer, 2:3, : 6 * HEAD]

    def normed_qk(layer):
        raw = raw_qk[layer]
        scale = lax.rsqrt(head_mean(raw * raw) + EPS)
        normed = raw * scale
        low = (normed * qk_gain(layer)).astype(BF16)
        return low, normed, scale

    def head_columns(tile):
        return slice(tile * 2 * HEAD, (tile + 1) * 2 * HEAD)

    def block_rows(block):
        return pl.ds(pl.multiple_of(block * rows, rows), rows)

    def one_half(block, half):
        return jnp.where(halves[half], block, jnp.zeros_like(block))

    def exp_scores(query, key, mask):
        scores = dot(query, key, NT) * HEAD ** (-0.5)
        expo = jnp.exp(jnp.where(mask != 0.0, scores, NEG))
        return expo, 1.0 / jnp.sum(expo, axis=-1, keepdims=True)

    half_rows = (slice(0, 8), slice(8, 16))

    def weight_of(layer, half, start, stop, places=slice(0, 16)):
        block = w_attn[layer, half, places, :, start * HEAD : stop * HEAD]
        return block.reshape(block.shape[0] * rows, (stop - start) * HEAD)

    row_halves = tuple(pl.ds(i * rows // PIECES, rows // PIECES) for i in range(PIECES))

    def y_gather_copy(row, d, h, buffer, layer):
        held = buffer.at[layer, shard, row_halves[h]]
        return ring_copy(row + h, d, held, held, y_device(d))

    def start_gather(row, h, buffer, layer):
        for d in (2, 1, 3):
            y_gather_copy(row, d, h, buffer, layer).start()

    def y_scatter_copy(row, d, h):
        cut = row_halves[h]
        return ring_copy(
            row + h, d, y_send.at[mod(shard + d), cut], y_recv.at[d - 1, cut], y_device(d)
        )

    def y_scatter(row):
        for h in range(len(row_halves)):
            for d in (2, 1, 3):
                y_scatter_copy(row, d, h).start()

    def y_total(row, h):
        cut = row_halves[h]
        for d in (2, 1, 3):
            y_scatter_copy(row, d, h).wait()
        total = y_send[shard, cut].astype(F32)
        for d in (1, 2, 3):
            total = total + y_recv[d - 1, cut].astype(F32)
        return total

    def spread_copy(row, buffer, d, h):
        held = buffer.at[p, row_halves[h]]
        return ring_copy(row + h, d, held, held, p_device(d))

    def spread_half(row, buffer, h, block):
        buffer[p, row_halves[h]] = block
        for d in (2, 1, 3):
            spread_copy(row, buffer, d, h).start()

    def wait_spread(row, buffer):
        for h in range(len(row_halves)):
            for d in (2, 1, 3):
                spread_copy(row, buffer, d, h).wait()

    column_halves = (pl.ds(0, width // 2), pl.ds(width // 2, width // 2))

    def packed_copies(row, layer, f, h, target):
        return [
            ring_copy(
                row + 2 * f + h,
                d,
                packed_send.at[f, h, d - 1],
                target.at[layer, f, h, d],
                q_device(d),
            )
            for d in (2, 1, 3)
        ]

    def choose_all(layer, f, h):
        return jnp.concatenate(
            [choose_rows(layer, mod(q + d), f, h) for d in range(RING)], axis=0
        )

    def gates_all(layer, f):
        return jnp.concatenate(
            [
                jnp.broadcast_to(weights[layer, 2 * mod(q + d) + f], (part_rows, span))
                for d in range(RING)
            ],
            axis=0,
        )

    def each_chunk(step):
        def body(i, _):
            step(lax.div(i, 2), lax.rem(i, 2))
            return 0

        lax.fori_loop(0, 4, body, 0)

    def pack(row, layer, source, target, gated):
        def step(f, h):
            chosen = choose_all(layer, f, h)
            low = chosen.astype(BF16)
            if gated:
                share = jnp.sum(
                    jnp.where(chosen, gates_all(layer, f), 0.0), axis=1, keepdims=True
                )
            for cut in column_halves:
                block = dot(low, source[:, :, cut].reshape(span, width // 2))
                if gated:
                    block = block * share
                block = block.astype(BF16)
                for d in (2, 1, 3):
                    packed_send[f, h, d - 1, :, cut] = block[
                        d * part_rows : (d + 1) * part_rows
                    ]
                target[layer, f, h, 0, :, cut] = block[:part_rows]
            for copy in packed_copies(row, layer, f, h, target):
                copy.start()

        each_chunk(step)

    def result_copies(row, f, h, send, target):
        return [
            ring_copy(
                row + 2 * f + h,
                d,
                send.at[f, h, d - 1],
                target.at[f, h, d],
                q_device(-d),
            )
            for d in (2, 1, 3)
        ]

    def put_result(row, f, h, send, target, columns):
        for cut in column_halves:
            block = columns(cut).astype(BF16)
            for d in (2, 1, 3):
                send[f, h, d - 1, :, cut] = block[d * part_rows : (d + 1) * part_rows]
            target[f, h, 0, :, cut] = block[:part_rows]
        for copy in result_copies(row, f, h, send, target):
            copy.start()

    def combine(row, layer, send, target, gated):
        parts[...] = jnp.zeros_like(parts)

        def step(f, h):
            chosen = choose_all(layer, f, h)
            if gated:
                share = jnp.where(chosen, gates_all(layer, f), 0.0)
            else:
                share = chosen.astype(F32)
            share = share.astype(BF16)
            wait_all(result_copies(row, f, h, send, target))
            for cut in column_halves:
                parts[:, cut] += dot(
                    share, target[f, h, :, :, cut].reshape(chunk, width // 2), TN
                )

        each_chunk(step)
        for i in range(RING):
            partial_send[i] = parts[i * rows : (i + 1) * rows].astype(BF16)

    def partial_copy(row, target, d, h):
        cut = row_halves[h]
        return ring_copy(
            row + h, d, partial_send.at[mod(p + d), cut], target.at[d - 1, cut], p_device(d)
        )

    def start_partials(row, target):
        for h in range(len(row_halves)):
            for d in (2, 1, 3):
                partial_copy(row, target, d, h).start()

    def total_of_partials(row, target, h):
        cut = row_halves[h]
        for d in (2, 1, 3):
            partial_copy(row, target, d, h).wait()
        total = partial_send[p, cut].astype(F32)
        for d in (1, 2, 3):
            total = total + target[d - 1, cut].astype(F32)
        return total

    def wait_expert_weights(layer):
        @pl.when(core == layer)
        def _():
            for copy in local_weights():
                copy.wait()

        @pl.when(core != layer)
        def _():
            for copy in sent_weights():
                copy.wait_recv()

    def wait_all(copies):
        for copy in copies:
            copy.wait()

    def start_attention(layer, h):
        cut = row_halves[h]
        held = stream[layer, cut]
        attn_all[layer, shard, cut] = (
            held * scale_of(held) * gains[layer, 0:1, :]
        ).astype(BF16)
        start_gather(Y_GATHER, h, attn_all, layer)

    def attention(layer):
        for h in range(len(row_halves)):
            for d in (2, 1, 3):
                y_gather_copy(Y_GATHER, d, h, attn_all, layer).wait()
        whole = attn_all[layer].reshape(span, width)
        raw_qk[layer] = dot(whole, weight_of(layer, 0, 0, 6))
        values[layer] = dot(whole, weight_of(layer, 1, 0, 2)).astype(BF16)
        low_qk[...] = normed_qk(layer)[0]

        key = low_qk[:, head_columns(2)]
        value = values[layer]
        for group_of in ((2, 1, 3, 0),):
            blocks = [mod(shard + d) for d in group_of]
            cuts = [block_rows(block) for block in blocks]
            mask = jnp.concatenate([mask_ref[cut] for cut in cuts], axis=0)
            tiles = []
            for tile in range(2):
                query = jnp.concatenate([low_qk[cut, head_columns(tile)] for cut in cuts], axis=0)
                outs = []
                for half in range(2):
                    expo, share = exp_scores(one_half(query, half), key, mask)
                    outs.append(dot((expo * share).astype(BF16), value))
                tiles.append(jnp.where(low_half, outs[0], outs[1]).astype(BF16))
            whole_mixed = jnp.concatenate(tiles, axis=1)
            out = dot(whole_mixed, weight_of(layer, 1, 2, 6), NT).astype(BF16)
            for i, (d, block, cut) in enumerate(zip(group_of, blocks, cuts)):
                part = slice(i * rows, (i + 1) * rows)
                mixed[layer, cut] = whole_mixed[part]
                y_send[block] = out[part]
        y_scatter(Y_SUM)

    def finish_attention(layer):
        for h, cut in enumerate(row_halves):
            center = stream[layer, cut] + y_total(Y_SUM, h)
            middle[layer, cut] = center
            feed = center * scale_of(center) * gains[layer, 1:2, :]
            spread_half(TOKENS, tokens, h, feed.astype(BF16))

    def feed_block(layer, f):
        return packed[layer, f].reshape(RING * group, width)

    def back_block(layer, f):
        return packed_back[layer, f].reshape(RING * group, width)

    def feed_chunk(layer, f, h):
        return packed[layer, f, h].reshape(chunk, width)

    def back_chunk(layer, f, h):
        return packed_back[layer, f, h].reshape(chunk, width)

    def grad_core(kind):
        return core_copy(C_GRAD + kind, grads.at[other, kind], grads_core.at[kind])

    lower, upper = pl.ds(0, rows), pl.ds(rows, rows)

    def grad_ring(kind, step):
        ahead = step in (0, 2, 4)
        part, cut = (
            (2, lower),
            (2, upper),
            (1, upper),
            (-1, lower),
            (1, lower),
            (-1, upper),
        )[step]
        return pltpu.make_async_remote_copy(
            src_ref=grads.at[core, kind, mod(shard + part), cut],
            dst_ref=grads_y.at[kind, step],
            send_sem=g_send.at[kind, step],
            recv_sem=g_recv.at[kind, step],
            device_id=y_device(1 if ahead else -1),
            device_id_type=MESH,
        )

    def sum_cores(kind):
        grad_core(kind).wait()

        def step(part, _):
            grads[core, kind, part] = (
                grads[core, kind, part].astype(F32) + grads_core[kind, part].astype(F32)
            ).astype(BF16)
            return 0

        lax.fori_loop(0, RING, step, 0)

    def start_ring(kind):
        for i in range(4):
            grad_ring(kind, i).start()

    def pass_grads(kind):
        for i, part, cut in ((0, 1, lower), (1, -1, upper)):
            grad_ring(kind, i).wait()
            at = mod(shard + part)
            grads[core, kind, at, cut] = (
                grads[core, kind, at, cut].astype(F32) + grads_y[kind, i].astype(F32)
            ).astype(BF16)
            grad_ring(kind, i + 4).start()

    def out_expert(layer, kind):
        return core_copy(
            C_OUT_EXPERT + 3 * layer + kind, out_stage.at[kind], expert_out.at[kind, core]
        )

    def out_local(kind):
        return pltpu.make_async_copy(
            out_stage.at[kind], expert_out.at[kind, core], out_sem.at[kind]
        )

    def finish_expert(layer, kind):
        for i in (2, 3, 4, 5):
            grad_ring(kind, i).wait()
        for cut, merged, direct in ((lower, 4, 3), (upper, 5, 2)):
            out_stage[kind, cut] = (
                grads[core, kind, shard, cut].astype(F32)
                + grads_y[kind, merged].astype(F32)
                + grads_y[kind, direct].astype(F32)
            )

        @pl.when(core == layer)
        def _():
            out_local(kind).start()

        @pl.when(core != layer)
        def _():
            out_expert(layer, kind).start()

    def wait_out(layer):
        for kind in range(3):
            @pl.when(core == layer)
            def _():
                out_local(kind).wait()

            @pl.when(core != layer)
            def _():
                out_expert(layer, kind).wait_send()

    def expert_grads(layer):
        for kind in range(3):
            def step(i, _):
                f, j = lax.div(i, 2), lax.rem(i, 2)
                cut = pl.ds(pl.multiple_of(j * 256, 256), 256)
                act = acts[kind, f, :, :, cut].reshape(2 * chunk, 256)
                rhs = back_block(layer, f) if kind == 2 else feed_block(layer, f)
                change = dot(act, rhs, TN).astype(BF16)
                grads[f, kind, 2 * j] = change[:128]
                grads[f, kind, 2 * j + 1] = change[128:]
                return 0

            lax.fori_loop(0, 4, step, 0)
            grad_core(kind).start()

    def proj_core_copy(i):
        at = pl.ds(RING * i, RING)
        return core_copy(C_PROJ + i, proj.at[other, at], proj_core.at[at])

    def proj_first(d, i):
        return pltpu.make_async_remote_copy(
            src_ref=proj.at[core, place_of(i, mod(p + d))],
            dst_ref=proj_recv.at[d - 1, i],
            send_sem=j_send.at[d - 1, i],
            recv_sem=j_recv.at[d - 1, i],
            device_id=p_device(d),
            device_id_type=MESH,
        )

    def proj_second(layer, d):
        return ring_copy(
            GRAD_Q + layer,
            d,
            proj_sum.at[mod(q + d)],
            proj_last.at[layer, d - 1],
            q_device(d),
        )

    def out_proj(layer):
        return core_copy(C_OUT_PROJ + layer, proj_stage, proj_out.at[core])

    def proj_one():
        def step(i, _):
            proj_core_copy(i).wait()
            at = pl.ds(RING * i, RING)
            proj[core, at] = (proj[core, at].astype(F32) + proj_core[at].astype(F32)).astype(BF16)
            return 0

        lax.fori_loop(0, RING, step, 0)
        for i in range(RING):
            for d in (2, 1, 3):
                proj_first(d, i).start()

    def proj_two(layer):
        for i in range(RING):
            for d in (2, 1, 3):
                proj_first(d, i).wait()
            total = proj[core, place_of(i, p)].astype(F32)
            for d in (1, 2, 3):
                total = total + proj_recv[d - 1, i].astype(F32)
            proj_sum[i] = total.astype(BF16)
        for d in (2, 1, 3):
            proj_second(layer, d).start()

    def proj_three(layer):
        total = proj_sum[q].astype(F32)
        for d in (2, 1, 3):
            proj_second(layer, d).wait()
        for d in (1, 2, 3):
            total = total + proj_last[layer, d - 1].astype(F32)

        @pl.when(layer == core)
        def _():
            proj_out[core] = total

        @pl.when(layer != core)
        def _():
            proj_stage[...] = total
            out_proj(layer).start()

    def start_back(layer):
        for h, cut in enumerate(row_halves):
            change = total_of_partials(PARTIAL_BACK, partial_back, h)
            center = middle[layer, cut]
            scale = scale_of(center)
            normed = center * scale
            terms[layer, 1:2] += jnp.sum(change * normed, axis=0, keepdims=True)
            scaled = change * gains[layer, 1:2, :]
            inner = jnp.mean(scaled * normed, axis=-1, keepdims=True)
            back_mid = cotangent[cut] + scale * (scaled - normed * inner)
            cotangent[cut] = back_mid
            attn_back[layer, shard, cut] = back_mid.astype(BF16)
            start_gather(Y_GATHER_BACK, h, attn_back, layer)

    def find_probs(layer):
        low_qk[...] = normed_qk(layer)[0]
        key = low_qk[:, head_columns(2)]
        for i in range(4):
            query = one_half(low_qk[:, head_columns(i // 2)], i % 2)
            expo, share = exp_scores(query, key, mask_ref[...])
            parts[:, i * span : (i + 1) * span] = expo * share

    def change_at(block, columns):
        return slopes.at[0, lax.div(block, 2), lax.rem(block, 2), pl.ds(0, rows), columns]

    def attention_back(layer):
        key = low_qk[:, head_columns(2)]
        value = values[layer]
        back_key = jnp.zeros((span, 2 * HEAD), F32)
        back_value = jnp.zeros((span, 2 * HEAD), F32)
        for group_of in ((0, 1, 3, 2),):
            blocks = [mod(shard - d) for d in group_of]
            cuts = [block_rows(block) for block in blocks]
            for d in group_of:
                for h in range(len(row_halves)):
                    if d:
                        y_gather_copy(Y_GATHER_BACK, d, h, attn_back, layer).wait()
            back = jnp.concatenate([attn_back[layer, block] for block in blocks], axis=0)
            back = dot(back, weight_of(layer, 1, 2, 6)).astype(BF16)
            for tile in range(2):
                pieces = []
                queries = jnp.concatenate(
                    [low_qk[cut, head_columns(tile)] for cut in cuts], axis=0
                )
                for half in range(2):
                    i = 2 * tile + half
                    columns = slice(i * span, (i + 1) * span)
                    probs = jnp.concatenate([parts[cut, columns] for cut in cuts], axis=0)
                    query = one_half(queries, half)
                    piece = one_half(back[:, head_columns(tile)], half)
                    back_probs = dot(piece, value, NT)
                    back_value = back_value + dot(probs.astype(BF16), piece, TN)
                    total = jnp.sum(probs * back_probs, axis=-1, keepdims=True)
                    back_scores = (probs * (back_probs - total)).astype(BF16)
                    pieces.append(dot(back_scores, key))
                    back_key = back_key + dot(back_scores, query, TN)
                joined = jnp.where(low_half, pieces[0], pieces[1])
                for i, block in enumerate(blocks):
                    change_at(block, pl.ds(tile * 2 * HEAD, 2 * HEAD))[...] = joined[
                        i * rows : (i + 1) * rows
                    ]
        _low, normed, scale = normed_qk(layer)
        change = jnp.concatenate(
            [change_at(i, pl.ds(0, 4 * HEAD))[...] for i in range(RING)], axis=0
        )
        change = jnp.concatenate([change, back_key], axis=1) * HEAD ** (-0.5)
        term = jnp.sum(change * normed, axis=0, keepdims=True)
        terms[layer, 2:3, : 6 * HEAD] = term
        scaled = change * qk_gain(layer)
        inner = head_mean(scaled * normed)
        low_qk[...] = (scale * (scaled - normed * inner)).astype(BF16)
        back_v[...] = back_value.astype(BF16)
        for places, cut in zip(half_rows, column_halves):
            out = dot(low_qk[...], weight_of(layer, 0, 0, 6, places), NT)
            out = out + dot(back_v[...], weight_of(layer, 1, 0, 2, places), NT)
            for i in range(RING):
                y_send[i, :, cut] = out[i * rows : (i + 1) * rows].astype(BF16)
        y_scatter(Y_SUM_BACK)

    def proj_grads(layer):
        def step(i, _):
            cut = pl.ds(pl.multiple_of(i * 4 * rows, 4 * rows), 4 * rows)
            at = pl.ds(i * 4, 4)
            feed = attn_all[layer, :, :, cut].reshape(span, 4 * rows)
            back = attn_back[layer, :, :, cut].reshape(span, 4 * rows)
            for half, start, stop, lhs, rhs in (
                (0, 0, 6, feed, low_qk[...]),
                (1, 0, 2, feed, back_v[...]),
                (1, 2, 6, back, mixed[layer]),
            ):
                change = dot(lhs, rhs, TN).astype(BF16)
                proj[half, at, :, start * HEAD : stop * HEAD] = change.reshape(
                    4, rows, (stop - start) * HEAD
                )
            proj_core_copy(i).start()
            return 0

        lax.fori_loop(0, 4, step, 0)

    def finish_back(layer, take):
        for h, cut in enumerate(row_halves):
            total = y_total(Y_SUM_BACK, h)
            held = stream[layer, cut]
            scale = scale_of(held)
            normed = held * scale
            terms[layer, 0:1] += jnp.sum(total * normed, axis=0, keepdims=True)
            scaled = total * gains[layer, 0:1, :]
            inner = jnp.mean(scaled * normed, axis=-1, keepdims=True)
            take(h, cut, (cotangent[cut] + scale * (scaled - normed * inner)).astype(BF16))

    def slopes_of(gate_part, up_part):
        sigmoid = jax.nn.sigmoid(gate_part)
        silu = gate_part * sigmoid
        return up_part * sigmoid * (1.0 + gate_part * (1.0 - sigmoid)), silu

    def expert_back(layer, f, h, back_hidden, to_gate, to_up):
        back_gate = (back_hidden * to_gate).astype(BF16)
        back_up = (back_hidden * to_up).astype(BF16)
        acts[0, f, h] = back_gate
        acts[1, f, h] = back_up

        def columns(cut):
            return dot(back_gate, w_gate[layer, f, cut], NT) + dot(
                back_up, w_up[layer, f, cut], NT
            )

        put_result(RESULT_BACK, f, h, packed_send, result_back, columns)

    def put_forward(layer, f, h, inner):
        def columns(cut):
            return dot(inner, w_down[layer, f, :, cut])

        put_result(RESULT, f, h, result_send, result, columns)

    def gate_and_up(layer, f, h):
        block = feed_chunk(layer, f, h)
        return dot(block, w_gate[layer, f]), dot(block, w_up[layer, f])

    for h in range(len(row_halves)):
        start_attention(0, h)
    start_second(0)
    make_tables()
    for h, cut in enumerate(row_halves):
        spread_half(TOKENS_BACK, tokens_back, h, cotangent[cut].astype(BF16))
    start_pass(0)
    for copy in sent_weights():
        copy.start()
    wait_pass(0)
    attention(0)
    start_second(1)
    take_tables()
    wait_spread(TOKENS_BACK, tokens_back)
    pack(PACKED_BACK, 1, tokens_back, packed_back, True)
    finish_attention(0)
    start_pass(1)

    def packed_back_sent(f, h):
        for copy in packed_copies(PACKED_BACK, 1, f, h, packed_back):
            copy.wait_send()

    each_chunk(packed_back_sent)
    wait_expert_weights(0)
    wait_spread(TOKENS, tokens)
    pack(PACKED, 0, tokens, packed, False)

    def experts_forward(f, h):
        wait_all(packed_copies(PACKED, 0, f, h, packed))
        gate_part, up_part = gate_and_up(0, f, h)
        inner = (gate_part * jax.nn.sigmoid(gate_part) * up_part).astype(BF16)
        put_forward(0, f, h, inner)

    each_chunk(experts_forward)
    combine(RESULT, 0, result_send, result, True)
    start_partials(PARTIAL, partial)
    for h, cut in enumerate(row_halves):
        final = middle[0, cut] + total_of_partials(PARTIAL, partial, h)
        stream[1, cut] = final.astype(BF16).astype(F32)
        start_attention(1, h)

    wait_pass(1)
    wait_expert_weights(1)

    def hidden_back(f, h):
        for copy in packed_copies(PACKED_BACK, 1, f, h, packed_back):
            copy.wait_recv()
        slopes[0, f, h] = dot(back_chunk(1, f, h), w_down[1, f], NT)

    each_chunk(hidden_back)
    attention(1)
    finish_attention(1)
    wait_spread(TOKENS, tokens)
    pack(PACKED, 1, tokens, packed, False)

    def experts_both(f, h):
        wait_all(packed_copies(PACKED, 1, f, h, packed))
        gate_part, up_part = gate_and_up(1, f, h)
        to_gate, to_up = slopes_of(gate_part, up_part)
        acts[2, f, h] = (to_up * up_part).astype(BF16)
        expert_back(1, f, h, slopes[0, f, h], to_gate, to_up)

    each_chunk(experts_both)
    each_chunk(lambda f, h: put_forward(1, f, h, acts[2, f, h]))
    expert_grads(1)
    combine(RESULT_BACK, 1, packed_send, result_back, False)
    start_partials(PARTIAL_BACK, partial_back)
    sum_cores(0)
    start_ring(0)

    start_back(1)
    combine(RESULT, 1, result_send, result, True)
    start_partials(PARTIAL, partial)
    sum_cores(1)
    find_probs(1)
    pass_grads(0)
    attention_back(1)
    proj_grads(1)
    for h, cut in enumerate(row_halves):
        final = middle[1, cut] + total_of_partials(PARTIAL, partial, h)
        ends_stage[0, cut] = final.astype(BF16)
    sum_cores(2)
    pl.semaphore_signal(credit, inc=1, device_id=core_device, device_id_type=MESH)

    def hand_on(h, cut, block):
        cotangent[cut] = block.astype(F32)
        spread_half(TOKENS_BACK, tokens_back, h, block)

    finish_back(1, hand_on)

    start_ring(1)
    start_ring(2)
    proj_one()

    def find_slopes(f, h):
        gate_part, up_part = gate_and_up(0, f, h)
        to_gate, to_up = slopes_of(gate_part, up_part)
        slopes[0, f, h] = to_gate
        slopes[1, f, h] = to_up
        acts[2, f, h] = (to_up * up_part).astype(BF16)

    each_chunk(find_slopes)
    wait_spread(TOKENS_BACK, tokens_back)
    pack(PACKED_BACK, 0, tokens_back, packed_back, True)
    pass_grads(1)
    pass_grads(2)
    proj_two(1)

    def experts_back(f, h):
        wait_all(packed_copies(PACKED_BACK, 0, f, h, packed_back))
        back_hidden = dot(back_chunk(0, f, h), w_down[0, f], NT)
        expert_back(0, f, h, back_hidden, slopes[0, f, h], slopes[1, f, h])

    each_chunk(experts_back)
    for kind in range(3):
        finish_expert(1, kind)
    for d in (1, -1):
        pl.semaphore_signal(y_credit, inc=1, device_id=y_device(d), device_id_type=MESH)
    pl.semaphore_wait(credit, 1)
    expert_grads(0)
    proj_three(1)
    combine(RESULT_BACK, 0, packed_send, result_back, False)
    start_partials(PARTIAL_BACK, partial_back)
    pl.semaphore_wait(y_credit, 2)
    sum_cores(0)
    start_ring(0)
    start_back(0)
    sum_cores(1)
    find_probs(0)
    pass_grads(0)
    attention_back(0)
    start_ring(1)

    @pl.when(core != 1)
    def _():
        out_proj(1).wait_send()

    proj_grads(0)
    sum_cores(2)
    start_ring(2)

    def keep(h, cut, block):
        ends_stage[1, cut] = block

    finish_back(0, keep)

    ends_out[core] = jnp.where(first, ends_stage[1], ends_stage[0])
    ends_copy_out = core_copy(C_OUT_ENDS, ends_stage.at[core], ends_out.at[core])
    ends_copy_out.start()
    term_copy = core_copy(C_TERM, terms.at[other], terms_core)
    term_copy.start()
    wait_out(1)
    proj_one()
    term_copy.wait()
    terms_recv[0, 0] = terms[core] + terms_core[...]
    for axis, (row, device) in enumerate(
        ((GAIN_P, p_device), (GAIN_Q, q_device), (GAIN_Y, y_device))
    ):
        copies = [
            ring_copy(
                row, d, terms_recv.at[axis, 0], terms_recv.at[axis, d], device(d)
            )
            for d in (2, 1, 3)
        ]
        for copy in copies:
            copy.start()
        if axis == 0:
            pass_grads(1)
            proj_two(0)
        if axis == 1:
            pass_grads(2)
            proj_three(0)
            finish_expert(0, 0)
        if axis == 2:
            finish_expert(0, 1)
        wait_all(copies)
        total = terms_recv[axis, 0]
        for d in (1, 2, 3):
            total = total + terms_recv[axis, d]
        if axis < 2:
            terms_recv[axis + 1, 0] = total
        else:
            gains_out[...] = total

    finish_expert(0, 2)
    wait_out(0)
    for layer in range(2):
        @pl.when(core == layer)
        def _():
            for kind in range(3):
                out_expert(layer, kind).wait_recv()
            out_proj(layer).wait_recv()

    @pl.when(core != 0)
    def _():
        out_proj(0).wait_send()

    ends_copy_out.wait()
    for copy in (piece_copy, ends_copy, gains_copy, routes_copy, gates_copy):
        copy.wait_send()
    for copy in sent_weights():
        copy.wait_send()
    for layer in range(2):
        for d in range(RING):
            for i in range(RING):
                weight_pass(layer, d, i).wait_send()
        for d in (1, 2, 3):
            weight_first(layer, d).wait_send()
            for i in range(RING):
                weight_second(layer, d, i).wait_send()
    for d in (1, 2, 3):
        ring_copy(
            TABLE_P, d, table_send.at[d], table_recv.at[d - 1], p_device(d)
        ).wait_send()


def finish(
    ends_ref,
    gains_ref,
    proj_ref,
    experts_ref,
    ends_out,
    attn_gain_out,
    query_gain_out,
    key_gain_out,
    feed_gain_out,
    query_out,
    key_out,
    value_out,
    out_out,
    gate_out,
    up_out,
    down_out,
    ends,
    gains,
    proj,
    experts,
    turned,
    sems,
):
    pieces = [(kind, f) for kind in range(3) for f in range(2)]
    moves = [
        pltpu.make_async_copy(
            experts_ref.at[kind, f], experts.at[kind, f], sems.at[2 * kind + f]
        )
        for kind, f in pieces
    ]
    moves += [
        pltpu.make_async_copy(ends_ref, ends, sems.at[6]),
        pltpu.make_async_copy(gains_ref, gains, sems.at[7]),
        pltpu.make_async_copy(proj_ref, proj, sems.at[8]),
    ]
    for move in moves:
        move.start()
    results = []
    for i, (kind, f) in enumerate(pieces):
        moves[i].wait()
        if kind < 2:
            turned[kind, f] = experts[kind, f].T
        source = experts.at[kind, f] if kind == 2 else turned.at[kind, f]
        target = (gate_out, up_out, down_out)[kind]
        results.append(pltpu.make_async_copy(source, target.at[0, f], sems.at[9 + i]))
        results[-1].start()
    moves[6].wait()
    results.append(pltpu.make_async_copy(ends, ends_out.at[0], sems.at[15]))
    results[-1].start()
    moves[7].wait()
    attn_gain_out[...] = gains[0:1]
    feed_gain_out[...] = gains[1:2]
    query_gain_out[...] = exact_dot(gains[2:3, : 4 * HEAD], copies_of_head(4), NT)
    key_gain_out[...] = exact_dot(gains[2:3, 4 * HEAD : 6 * HEAD], copies_of_head(2), NT)
    moves[8].wait()
    swap = swap_heads()
    query_out[0] = exact_dot(proj[0, :, : 4 * HEAD], swap)
    key_out[0] = proj[0, :, 4 * HEAD :]
    value_out[0] = proj[1, :, : 2 * HEAD]
    out_out[0] = exact_dot(proj[1, :, 2 * HEAD :], swap)
    for result in results:
        result.wait()


def shards(
    ends_in,
    segments,
    routes,
    gates,
    attn_gain,
    query_gain,
    key_gain,
    feed_gain,
    w_query,
    key_weight,
    value_weight,
    w_out,
    w_gate,
    w_up,
    w_down,
):
    rows = ends_in.shape[2]
    width = ends_in.shape[3]
    top = routes.shape[3]
    hidden = w_gate.shape[3]
    experts_all = w_gate.shape[1] * lax.axis_size("expert")
    capacity = 3 * rows * top // (2 * experts_all)
    group = RING * capacity
    part_rows = group // 2
    chunk = RING * part_rows
    span = RING * rows
    vmem = pl.BlockSpec(memory_space=pltpu.VMEM)
    anywhere = pl.BlockSpec(memory_space=pl.ANY)
    half = 6 * HEAD
    everyone = RING * RING
    scratch = [
        pltpu.VMEM((2, 2, width, hidden), BF16),
        pltpu.VMEM((2, 2, width, hidden), BF16),
        pltpu.VMEM((2, 2, hidden, width), BF16),
        pltpu.VMEM((2, 2, everyone, rows, half), BF16),
        pltpu.VMEM((rows, width), BF16),
        pltpu.VMEM((2, 8, width), F32),
        pltpu.VMEM((2, top, rows), jnp.int32),
        pltpu.VMEM((2, top, rows), F32),
        pltpu.VMEM((span, span), F32),
        pltpu.VMEM((2, rows, half), BF16),
        pltpu.VMEM((8, width), F32),
        pltpu.VMEM((RING, 2, 2, 8, span), F32),
        pltpu.VMEM((RING - 1, 2, 2, 8, span), F32),
        pltpu.VMEM((2, 8, 1, span), F32),
        pltpu.VMEM((2, 8, 1, span), F32),
        pltpu.VMEM((2, rows, width), F32),
        pltpu.VMEM((2, rows, width), F32),
        pltpu.VMEM((rows, width), F32),
        pltpu.VMEM((2, RING, rows, width), BF16),
        pltpu.VMEM((2, span, half), F32),
        pltpu.VMEM((2, span, 2 * HEAD), BF16),
        pltpu.VMEM((2, span, 4 * HEAD), BF16),
        pltpu.VMEM((RING, rows, width), BF16),
        pltpu.VMEM((RING - 1, rows, width), BF16),
        pltpu.VMEM((RING, rows, width), BF16),
        pltpu.VMEM((RING, rows, width), BF16),
        pltpu.VMEM((2, 2, RING - 1, group // 2, width), BF16),
        pltpu.VMEM((2, 2, 2, RING, group // 2, width), BF16),
        pltpu.VMEM((2, 2, 2, RING, group // 2, width), BF16),
        pltpu.VMEM((2, 2, RING - 1, group // 2, width), BF16),
        pltpu.VMEM((2, 2, RING, group // 2, width), BF16),
        pltpu.VMEM((2, 2, RING, group // 2, width), BF16),
        pltpu.VMEM((RING, rows, width), BF16),
        pltpu.VMEM((RING - 1, rows, width), BF16),
        pltpu.VMEM((RING - 1, rows, width), BF16),
        pltpu.VMEM((span, width), F32),
        pltpu.VMEM((2, 2, 2, 2 * group, hidden), F32),
        pltpu.VMEM((2, RING, rows, width), BF16),
        pltpu.VMEM((span, half), BF16),
        pltpu.VMEM((span, 2 * HEAD), BF16),
        pltpu.VMEM((3, 2, 2, 2 * group, hidden), BF16),
        pltpu.VMEM((2, 3, RING, hidden // RING, width), BF16),
        pltpu.VMEM((3, RING, hidden // RING, width), BF16),
        pltpu.VMEM((3, 6, rows, width), BF16),
        pltpu.VMEM((3, hidden // RING, width), F32),
        pltpu.VMEM((2, everyone, rows, half), BF16),
        pltpu.VMEM((everyone, rows, half), BF16),
        pltpu.VMEM((RING - 1, RING, rows, half), BF16),
        pltpu.VMEM((RING, rows, half), BF16),
        pltpu.VMEM((2, RING - 1, rows, half), BF16),
        pltpu.VMEM((rows, half), F32),
        pltpu.VMEM((2, 8, width), F32),
        pltpu.VMEM((8, width), F32),
        pltpu.VMEM((3, RING, 8, width), F32),
        pltpu.VMEM((2, rows, width), BF16),
        pltpu.SemaphoreType.DMA((RING_ROWS, RING - 1)),
        pltpu.SemaphoreType.DMA((RING_ROWS, RING - 1)),
        pltpu.SemaphoreType.DMA((2, RING - 1, RING)),
        pltpu.SemaphoreType.DMA((2, RING - 1, RING)),
        pltpu.SemaphoreType.DMA((2, RING, RING)),
        pltpu.SemaphoreType.DMA((2, RING, RING)),
        pltpu.SemaphoreType.DMA((RING - 1, RING)),
        pltpu.SemaphoreType.DMA((RING - 1, RING)),
        pltpu.SemaphoreType.DMA((3, 6)),
        pltpu.SemaphoreType.DMA((3, 6)),
        pltpu.SemaphoreType.DMA((CORE_ROWS,)),
        pltpu.SemaphoreType.DMA((CORE_ROWS,)),
        pltpu.SemaphoreType.DMA((3,)),
        pltpu.SemaphoreType.DMA((3,)),
        pltpu.SemaphoreType.REGULAR,
        pltpu.SemaphoreType.REGULAR,
    ]
    ends, gain_sums, proj, experts = pl.pallas_call(
        functools.partial(kernel, rows, width, hidden, capacity),
        out_shape=(
            jax.ShapeDtypeStruct((2, rows, width), BF16),
            jax.ShapeDtypeStruct((8, width), F32),
            jax.ShapeDtypeStruct((2, rows, half), F32),
            jax.ShapeDtypeStruct((3, 2, hidden // RING, width), F32),
        ),
        in_specs=[vmem] * 12 + [anywhere] * 3,
        out_specs=(vmem, vmem, vmem, anywhere),
        scratch_shapes=scratch,
        compiler_params=pltpu.CompilerParams(
            collective_id=0, has_side_effects=True, vmem_limit_bytes=63 << 20
        ),
        cost_estimate=pl.CostEstimate(
            flops=60_000_000_000, bytes_accessed=20_000_000, transcendentals=4_000_000
        ),
        name="layers",
    )(
        ends_in[0],
        segments,
        routes[0].transpose(0, 2, 1),
        gates[0].transpose(0, 2, 1),
        attn_gain,
        query_gain,
        key_gain,
        feed_gain,
        w_query[0],
        key_weight[0],
        value_weight[0],
        w_out[0].T,
        w_gate[0],
        w_up[0],
        w_down[0],
    )
    shapes = (
        ((1, 2, rows, width), BF16),
        ((1, width), F32),
        ((1, HEAD), F32),
        ((1, HEAD), F32),
        ((1, width), F32),
        ((1,) + w_query.shape[1:], F32),
        ((1,) + key_weight.shape[1:], F32),
        ((1,) + value_weight.shape[1:], F32),
        ((1, w_out.shape[2], w_out.shape[1]), F32),
        ((1, 2, width, hidden // RING), F32),
        ((1, 2, width, hidden // RING), F32),
        ((1, 2, hidden // RING, width), F32),
    )
    outputs = pl.pallas_call(
        finish,
        out_shape=tuple(jax.ShapeDtypeStruct(shape, dtype) for shape, dtype in shapes),
        in_specs=[anywhere] * 4,
        out_specs=(anywhere,) + (vmem,) * 8 + (anywhere,) * 3,
        scratch_shapes=[
            pltpu.VMEM((2, rows, width), BF16),
            pltpu.VMEM((8, width), F32),
            pltpu.VMEM((2, rows, half), F32),
            pltpu.VMEM((3, 2, hidden // RING, width), F32),
            pltpu.VMEM((2, 2, width, hidden // RING), F32),
            pltpu.SemaphoreType.DMA((16,)),
        ],
        compiler_params=pltpu.CompilerParams(vmem_limit_bytes=60 << 20),
        name="finish",
    )(ends, gain_sums, proj, experts)
    return (*outputs[:8], outputs[8].transpose(0, 2, 1), *outputs[9:])


def solution(mesh):
    return jax.shard_map(
        shards,
        mesh=mesh,
        in_specs=(
            P("section", None, ("expert", "shard"), None),
            P(None, "expert"),
            P("section", None, ("expert", "shard"), None),
            P("section", None, ("expert", "shard"), None),
            P("section", None),
            P("section", None),
            P("section", None),
            P("section", None),
            P("section", "expert", "shard"),
            P("section", "expert", "shard"),
            P("section", "expert", "shard"),
            P("section", "shard", "expert"),
            P("section", "expert", None, None),
            P("section", "expert", None, None),
            P("section", "expert", None, None),
        ),
        out_specs=(
            P("section", None, ("expert", "shard"), None),
            P("section", None),
            P("section", None),
            P("section", None),
            P("section", None),
            P("section", "expert", "shard"),
            P("section", "expert", "shard"),
            P("section", "expert", "shard"),
            P("section", "shard", "expert"),
            P("section", "expert", None, "shard"),
            P("section", "expert", None, "shard"),
            P("section", "expert", "shard", None),
        ),
        check_vma=False,
    )
```
